32 devices in a mesh: dp: 8 (over z, y), tensor: 4 (over x, core).
Axes of the slice: x: 2, y: 2, z: 4, core: 2. Of those that a mesh axis runs over, the one named last changes fastest.
Arguments:
- tokens: bfloat16 [32, 1024, 768], P(('dp', 'tensor')), may hold values from -6 to 6
- thoughts: bfloat16 [32, 32, 768], P(('dp', 'tensor')), may hold values from -6 to 6
- thought_slots: int32 [32, 32], P(('dp', 'tensor')), may hold values from 0 to 1023, as said below
- segment_ids: int32 [32, 1024], P(('dp', 'tensor')), may hold values from 0 to 7, never falling along the last dimension, each value on 1 to 256 neighbouring positions
- attn_gain: bfloat16 [768], replicated, may hold values from 0.5 to 1.5
- attn_shift: bfloat16 [768], replicated, may hold values from -1.5 to 1.5
- qkv_weight: bfloat16 [768, 3, 768], P(None, None, 'tensor'), may hold values from -0.21875 to 0.21875
- qkv_bias: bfloat16 [2, 768], P(None, 'tensor'), may hold values from -2.5 to 2.5
- out_weight: bfloat16 [768, 768], P('tensor'), may hold values from -0.875 to 0.875
- out_bias: bfloat16 [768], replicated, may hold values from -1.5 to 1.5
- mlp_gain: bfloat16 [768], replicated, may hold values from 0.5 to 1.5
- mlp_shift: bfloat16 [768], replicated, may hold values from -1.5 to 1.5
- up_weight: bfloat16 [768, 3072], P(None, 'tensor'), may hold values from -0.21875 to 0.21875
- up_bias: bfloat16 [3072], P('tensor'), may hold values from -1.5 to 1.5
- down_weight: bfloat16 [3072, 768], P('tensor'), may hold values from -0.15625 to 0.15625
- down_bias: bfloat16 [768], replicated, may hold values from -1.5 to 1.5
- cotangent: bfloat16 [32, 1024, 768], P(('dp', 'tensor')), may hold values from -6 to 6
Outputs:
- block_output: bfloat16 [32, 1024, 768], P(('dp', 'tensor'))
- grad_tokens: bfloat16 [32, 1024, 768], P(('dp', 'tensor'))
- grad_thoughts: bfloat16 [32, 32, 768], P(('dp', 'tensor'))
- grad_attn_gain: float32 [768], replicated
- grad_attn_shift: float32 [768], replicated
- grad_qkv_weight: float32 [768, 3, 768], P('dp', None, 'tensor')
- grad_qkv_bias: float32 [2, 768], P(None, 'tensor')
- grad_out_weight: float32 [768, 768], P('tensor', 'dp')
- grad_out_bias: float32 [768], replicated
- grad_mlp_gain: float32 [768], replicated
- grad_mlp_shift: float32 [768], replicated
- grad_up_weight: float32 [768, 3072], P('dp', 'tensor')
- grad_up_bias: float32 [3072], P('tensor')
- grad_down_weight: float32 [3072, 768], P('tensor', 'dp')
- grad_down_bias: float32 [768], replicated
The draws below stay inside these ranges and needn't reach their ends.
Inputs may be any that keep to these rules, and one draw needn't show every extreme that they name: `thought_slots`: the 32 slots of one row are distinct. `segment_ids`: within a row segment numbers never fall, and each segment holds 1 to 256 slots.
All inputs are finite; a program needn't handle non-finite values.
Results may differ from the reference program's by a relative error of at most 0.012.
The reference program's roundings to bfloat16 on the way count: a program that leaves them out, or rounds other values in their place, can miss the bound.
Values may be sent and summed in bfloat16 or wider, within the bound.
No kernel may reach another device: no remote copies, remote signals or barrier semaphores. Data moves between devices by JAX's collectives and lax.ppermute only.
A program may use at most 192 MiB of HBM per device.

```python
import math
import jax
import jax.numpy as jnp
import numpy as np
from jax import lax

D = 768
HEADS = 12
HD = 64
FF = 3072
L = 1024
NT = 32
SEGS = 8
ROWS = 32


def draw_thought_slots(key, part):
    row_keys = jax.random.split(key, ROWS)

    def one_row(row_key):
        return jax.random.permutation(row_key, L)[:NT]
    return jax.vmap(one_row)(row_keys).astype(jnp.int32)


def steps_of(stream_key, extent, shards, low, high):
    factor_of, own = 1.0, jax.random.fold_in(stream_key, 6)
    for position, parts in shards:
        heights = jnp.exp(jax.random.uniform(jax.random.fold_in(own, position), (parts,), jnp.float32, low / len(shards), high / len(shards)))
        factor_of = factor_of * jnp.repeat(heights, extent[position] // parts).reshape([-1 if axis == position else 1 for axis in range(len(extent))])
    return factor_of


def split_up(number_of, total, limit, slope):
    loads = [(1 << 20) // math.isqrt(grade ** slope) + 1 for grade in range(2, number_of + 1)]
    spare, counts = total - limit - (number_of - 1), [1] * (number_of - 1)
    while spare > 0:
        candidates = [i for i in range(number_of - 1) if counts[i] < limit]
        whole, remaining = sum([loads[i] for i in candidates]), spare
        for i in candidates:
            addition = min(limit - counts[i], max(1, remaining * loads[i] // whole), spare)
            counts[i] = counts[i] + addition
            spare = spare - addition
    return np.array([limit] + counts)


def uneven_parts(key, amount, total, limit, skew):
    if amount == 2:
        one = jax.random.randint(key, (), max(1, total - limit), min(limit, total - 1) + 1)
        return jnp.stack([one, total - one])
    lengths = jnp.asarray(split_up(amount, total, limit, skew), jnp.int32)
    couples = (amount - 1) // 2
    giver, taker = lengths[1:1 + 2 * couples:2], lengths[2:2 + 2 * couples:2]
    slack = jnp.minimum(giver - 1, limit - taker)
    moved = jax.random.randint(jax.random.fold_in(key, 1), (couples,), 0, 1 << 20) % (slack + 1)
    lengths = lengths.at[1:1 + 2 * couples:2].set(giver - moved).at[2:2 + 2 * couples:2].set(taker + moved)
    return lengths[jax.random.permutation(jax.random.fold_in(key, 2), amount)]


def normal_values(own_key, shape, spread, reach, pieces=(), kind=jnp.bfloat16):
    level = steps_of(own_key, shape, pieces, -0.22, 0.18) if pieces else 1.0
    entries = jax.random.normal(own_key, shape, jnp.float32) * spread * level
    return jnp.minimum(jnp.maximum(entries, -reach), reach).astype(kind)


def setup_inputs(seed: int = 0) -> dict:
    keys = jax.random.split(jax.random.key(seed), 18)
    return {
        "tokens": normal_values(keys[0], (ROWS, L, D), 1.0, 6.0, ((0, 32),)),
        "thoughts": normal_values(keys[1], (ROWS, NT, D), 1.0, 6.0, ((0, 32),)),
        "thought_slots": draw_thought_slots(jax.random.fold_in(keys[17], 71), 0),
        "segment_ids": jax.vmap(lambda own: jnp.searchsorted(jnp.cumsum(uneven_parts(own, SEGS, L, L // 4, 1)), jnp.arange(L), side="right"))(jax.random.split(keys[3], ROWS)).reshape((ROWS, L)).astype(jnp.int32),
        "attn_gain": jnp.clip(1.0 + 0.1 * jax.random.normal(keys[4], (D,), jnp.float32), 0.5, 1.5).astype(jnp.bfloat16),
        "attn_shift": normal_values(keys[5], (D,), 0.3, 1.5),
        "qkv_weight": normal_values(keys[6], (D, 3, D), D ** -0.5, 0.21875, ((2, 4),)),
        "qkv_bias": normal_values(keys[7], (2, D), 0.5, 2.5, ((1, 4),)),
        "out_weight": normal_values(keys[8], (D, D), (D // 16) ** -0.5, 0.875, ((0, 4),)),
        "out_bias": normal_values(keys[9], (D,), 0.3, 1.5),
        "mlp_gain": jnp.clip(1.0 + 0.1 * jax.random.normal(keys[10], (D,), jnp.float32), 0.5, 1.5).astype(jnp.bfloat16),
        "mlp_shift": normal_values(keys[11], (D,), 0.3, 1.5),
        "up_weight": normal_values(keys[12], (D, FF), D ** -0.5, 0.21875, ((1, 4),)),
        "up_bias": normal_values(keys[13], (FF,), 0.3, 1.5, ((0, 4),)),
        "down_weight": normal_values(keys[14], (FF, D), (FF // 2) ** -0.5, 0.15625, ((0, 4),)),
        "down_bias": normal_values(keys[15], (D,), 0.3, 1.5),
        "cotangent": normal_values(keys[16], (ROWS, L, D), 1.0, 6.0, ((0, 32),)),
    }


epsilon = 1e-05

@jax.custom_vjp
def low(v):
    return lax.optimization_barrier(v.astype(jnp.bfloat16)).astype(jnp.float32)

@jax.custom_vjp
def low_back(v):
    return v

def low_keep(v):
    return (low(v), None)

def low_pass(kept, grad):
    return (grad,)

def back_keep(v):
    return (v, None)

def back_low(kept, grad):
    return (low(grad),)
low.defvjp(low_keep, low_pass)
low_back.defvjp(back_keep, back_low)

def product(form, left, right):
    return jnp.einsum(form, left, right, precision=lax.Precision.HIGHEST)

def layer_norm(stream, gain, shift):
    average = lax.optimization_barrier(jnp.mean(stream, axis=-1, keepdims=True))
    centered = stream - average
    variance = lax.optimization_barrier(jnp.mean(centered * centered, axis=-1, keepdims=True))
    return centered * lax.rsqrt(variance + epsilon) * gain + shift

def row_forward(row_tokens, row_thoughts, weights, segments, slots):
    attn_gain, attn_shift, qkv_weight, qkv_bias, out_weight, out_bias, mlp_gain, mlp_shift, up_weight, up_bias, down_weight, down_bias = weights
    positions = jnp.arange(L, dtype=jnp.int32)
    slot_grid = (slots[:, None] == positions[None, :]).astype(jnp.float32)
    covered = lax.optimization_barrier(jnp.sum(slot_grid, axis=0))[:, None]
    stream = row_tokens * (1.0 - covered) + product('nl,nd->ld', slot_grid, row_thoughts)
    normed = low(layer_norm(stream, attn_gain, attn_shift))
    zero_row = jnp.zeros_like(qkv_bias[0])
    full_bias = jnp.stack([qkv_bias[0], zero_row, qkv_bias[1]])
    joined = low_back(low(product('ld,dcf->lcf', normed, qkv_weight) + full_bias))
    split_heads = joined.reshape(L, 3, HEADS, HD)
    queries = split_heads[:, 0]
    key_rows = split_heads[:, 1]
    values = split_heads[:, 2]
    allowed = (segments[:, None] == segments[None, :]) & (positions[None, :] <= positions[:, None])
    score_scale = HD ** (-0.5)
    scores = low_back(product('qhe,khe->hqk', queries, key_rows) * score_scale)
    scores = jnp.where(allowed[None], scores, -1e+30)
    row_max = lax.optimization_barrier(jnp.max(scores, axis=-1, keepdims=True))
    exponent = jnp.exp(scores - row_max)
    probs = low(exponent / lax.optimization_barrier(jnp.sum(exponent, axis=-1, keepdims=True)))
    context = low_back(low(product('hqk,khe->qhe', probs, values).reshape(L, D)))
    attended = low_back(product('lf,fd->ld', context, out_weight) + out_bias)
    middle = stream + attended
    normed_mlp = low(layer_norm(middle, mlp_gain, mlp_shift))
    pre_gelu = low_back(product('ld,df->lf', normed_mlp, up_weight) + up_bias)
    hidden = low(jax.nn.gelu(pre_gelu, approximate=True))
    return middle + product('lf,fd->ld', hidden, down_weight) + down_bias

def reference(tokens, thoughts, thought_slots, segment_ids, attn_gain, attn_shift, qkv_weight, qkv_bias, out_weight, out_bias, mlp_gain, mlp_shift, up_weight, up_bias, down_weight, down_bias, cotangent):
    weights = (attn_gain.astype(jnp.float32), attn_shift.astype(jnp.float32), qkv_weight.astype(jnp.float32), qkv_bias.astype(jnp.float32), out_weight.astype(jnp.float32), out_bias.astype(jnp.float32), mlp_gain.astype(jnp.float32), mlp_shift.astype(jnp.float32), up_weight.astype(jnp.float32), up_bias.astype(jnp.float32), down_weight.astype(jnp.float32), down_bias.astype(jnp.float32))

    def row_step(totals, inputs_row):
        row_tokens, row_thoughts, slots, segments, row_cot = inputs_row

        def forward(tok_float, thought_float, weight_set):
            return row_forward(tok_float, thought_float, weight_set, segments, slots)
        output, pullback = jax.vjp(forward, row_tokens.astype(jnp.float32), row_thoughts.astype(jnp.float32), weights)
        token_grad, thought_grad, weight_grads = pullback(row_cot.astype(jnp.float32))
        totals = jax.tree.map(lambda left, right: left + right, totals, weight_grads)
        return (totals, (output.astype(jnp.bfloat16), token_grad.astype(jnp.bfloat16), thought_grad.astype(jnp.bfloat16)))
    zeros = jax.tree.map(jnp.zeros_like, weights)
    grads, (outputs, token_grads, thought_grads) = lax.scan(row_step, zeros, (tokens, thoughts, thought_slots, segment_ids, cotangent))
    return (outputs, token_grads, thought_grads, grads[0], grads[1], grads[2], grads[3], grads[4], grads[5], grads[6], grads[7], grads[8], grads[9], grads[10], grads[11])
```

```python
import functools

import jax
import jax.numpy as jnp
from jax import lax
from jax.experimental import pallas as pl
from jax.experimental.pallas import tpu as pltpu
from jax.sharding import PartitionSpec as P

F32 = jnp.float32
BF = jnp.bfloat16
HD = 64
QB = 256
EPS = 1e-05
NEG = -1e30
NN = ((1,), (0,))
NT = ((1,), (1,))
GA, GB = 0.7978845608028654, 0.044715
EXTRA = 16


def dot(a, b, dims=NN):
    return lax.dot_general(a, b, (dims, ((), ())), preferred_element_type=F32)


def full(shape):
    zeros = (0,) * len(shape)
    return pl.BlockSpec(tuple(shape), lambda *_: zeros)


def sds(shape, dtype):
    return jax.ShapeDtypeStruct(tuple(shape), dtype)


def params(mib):
    return pltpu.CompilerParams(vmem_limit_bytes=mib << 20)


def cost(micros):
    return pl.CostEstimate(flops=int(micros * 1e9), bytes_accessed=int(micros * 1e6), transcendentals=0)


def normalize(x):
    mean = jnp.mean(x, axis=-1, keepdims=True)
    xc = x - mean
    var = jnp.mean(xc * xc, axis=-1, keepdims=True)
    rstd = lax.rsqrt(var + EPS)
    return xc * rstd, rstd


def norm_back(u, xhat, rstd):
    mu = jnp.mean(u, axis=-1, keepdims=True)
    mux = jnp.mean(u * xhat, axis=-1, keepdims=True)
    return rstd * (u - mu - xhat * mux)


def one_hot(slots, row0, rows):
    pos = lax.broadcasted_iota(jnp.int32, (rows, slots.shape[1]), 0) + row0
    return pos == slots


def first_kernel(tok, cot, slots, thoughts, gain, shift, seg, stream, normed, normed_t, cot_t, cot_sum, mask):
    i = pl.program_id(0)
    hot = one_hot(slots[...], i * QB, QB)
    inserted = dot(hot.astype(BF), thoughts[...])
    covered = jnp.sum(hot.astype(F32), axis=1, keepdims=True) > 0.5
    x = jnp.where(covered, inserted, tok[...].astype(F32))
    stream[...] = x.astype(BF)
    xhat, _ = normalize(x)
    n = (xhat * gain[...] + shift[...]).astype(BF)
    normed[...] = n
    normed_t[...] = n.T
    g = cot[...]
    cot_t[...] = g.T

    @pl.when(i == 0)
    def _():
        cot_sum[...] = jnp.zeros_like(cot_sum)

    cot_sum[...] += jnp.sum(g.astype(F32), axis=0, keepdims=True)
    k0 = pl.multiple_of(jnp.maximum(i - 1, 0) * QB, QB)
    seg_q = seg[:, pl.ds(pl.multiple_of(i * QB, QB), QB)]
    seg_k = jnp.broadcast_to(seg[:, pl.ds(k0, 2 * QB)], (QB, 2 * QB)).T
    kpos = lax.broadcasted_iota(jnp.int32, (2 * QB, QB), 0) + k0
    qpos = lax.broadcasted_iota(jnp.int32, (2 * QB, QB), 1) + i * QB
    mask[0] = jnp.where((seg_k == seg_q) & (kpos <= qpos), 0.0, NEG)


def first_norm(tok, cot, slots, thoughts, gain, shift, seg):
    L, D = tok.shape
    nq = L // QB
    rows = pl.BlockSpec((QB, D), lambda i: (i, 0))
    cols = pl.BlockSpec((D, QB), lambda i: (0, i))
    return pl.pallas_call(
        first_kernel,
        grid=(nq,),
        in_specs=[rows, rows] + [full(a.shape) for a in (slots, thoughts, gain, shift, seg)],
        out_specs=[rows, rows, cols, cols, full((1, D)), pl.BlockSpec((1, 2 * QB, QB), lambda i: (i, 0, 0))],
        out_shape=[sds((L, D), BF), sds((L, D), BF), sds((D, L), BF), sds((D, L), BF), sds((1, D), F32), sds((nq, 2 * QB, QB), F32)],
        compiler_params=params(60),
        cost_estimate=cost(4),
        name="first_norm",
    )(tok, cot, slots, thoughts, gain, shift, seg)


def window(i):
    return (0, QB) if i == 0 else ((i - 1) * QB, 2 * QB)


def head_mask(h, width):
    lane = lax.broadcasted_iota(jnp.int32, (1, width), 1)
    return ((lane >= h * HD) & (lane < (h + 1) * HD)).astype(BF)


def attend_kernel(n, *refs):
    normed, mask = refs[:2]
    ws = refs[2:2 + n]
    joined, ctx, lse, w, vt = refs[2 + n:]
    t = pl.program_id(0)
    L = normed.shape[0]
    C = ctx.shape[2]
    for j in range(n):
        @pl.when(t == j)
        def _(j=j):
            w[...] = ws[j][...]
    bias = w[4 * C:, :].astype(F32)
    for i in range(L // QB):
        r = pl.ds(i * QB, QB)
        for c in range(3):
            v = dot(normed[r, :], w[c * C:(c + 1) * C, :], NT)
            if c != 1:
                b = 1 + c // 2
                v = v + bias[b:b + 1, :C]
            v = v.astype(BF)
            joined[0, c, r, :] = v
            if c == 2:
                vt[:, r] = v.T
    masks = [head_mask(h, C) for h in range(C // HD)]
    for i in range(L // QB):
        k0, kn = window(i)
        r = pl.ds(i * QB, QB)
        q = joined[0, 0, r, :] * BF(HD ** -0.5)
        k = joined[0, 1, pl.ds(k0, kn), :]
        m = mask[i, :kn, :]
        outs, stats = [], []
        for h in range(C // HD):
            s = dot(k, q * masks[h], NT) + m
            top = jnp.max(s, axis=0, keepdims=True)
            e = jnp.exp(s - top)
            total = jnp.sum(e, axis=0, keepdims=True)
            p = (e * (1.0 / total)).astype(BF)
            outs.append(dot(vt[h * HD:(h + 1) * HD, pl.ds(k0, kn)], p))
            stats.append(top + jnp.log(total))
        ctx[0, r, :] = jnp.concatenate(outs, axis=0).T.astype(BF)
        for h in range(C // HD):
            lse[0, h:h + 1, r] = stats[h]


def attend(normed, mask, ws, C, name):
    n = len(ws)
    L, D = normed.shape
    sh = lambda *s: pl.BlockSpec((1,) + s, lambda t: (t,) + (0,) * len(s))
    return pl.pallas_call(
        functools.partial(attend_kernel, n),
        grid=(n,),
        in_specs=[full(a.shape) for a in (normed, mask, *ws)],
        out_specs=[sh(3, L, C), sh(L, C), sh(8, L)],
        out_shape=[sds((n, 3, L, C), BF), sds((n, L, C), BF), sds((n, 8, L), F32)],
        scratch_shapes=[pltpu.VMEM(ws[0].shape, BF), pltpu.VMEM((C, L), BF)],
        compiler_params=params(60),
        cost_estimate=cost(7 * n),
        name=name,
    )(normed, mask, *ws)


def second_norm(stream, out_bias, gain, shift, ctxs, ws):
    L, D = stream.shape
    n = len(ws)
    C = ctxs[0].shape[2]
    groups = len(ctxs)

    def kernel(*refs):
        stream, out_bias, gain, shift = refs[:4]
        cs = refs[4:4 + groups]
        wr = refs[4 + groups:4 + groups + n]
        middle, nm, nm_t = refs[4 + groups + n:]
        acc = stream[...].astype(F32) + out_bias[...]
        j = 0
        for c in cs:
            for s in range(c.shape[0]):
                acc = acc + dot(c[s], wr[j][...])
                j += 1
        middle[...] = acc
        xhat, _ = normalize(acc)
        v = (xhat * gain[...] + shift[...]).astype(BF)
        nm[...] = v
        nm_t[...] = v.T

    rows = pl.BlockSpec((QB, D), lambda i: (i, 0))
    cols = pl.BlockSpec((D, QB), lambda i: (0, i))
    return pl.pallas_call(
        kernel,
        grid=(L // QB,),
        in_specs=[rows] + [full(a.shape) for a in (out_bias, gain, shift)]
        + [pl.BlockSpec((c.shape[0], QB, C), lambda i: (0, i, 0)) for c in ctxs]
        + [pl.BlockSpec((C, D), lambda i: (3, 0)) for w in ws],
        out_specs=[rows, rows, cols],
        out_shape=[sds((L, D), F32), sds((L, D), BF), sds((D, L), BF)],
        compiler_params=params(60),
        cost_estimate=cost(4),
        name="second_norm",
    )(stream, out_bias, gain, shift, *ctxs, *ws)


def mlp_kernel(n, first, *refs):
    nm, nm_t, g, g_t = refs[:4]
    bs, ups, dns = refs[4:4 + n], refs[4 + n:4 + 2 * n], refs[4 + 2 * n:4 + 3 * n]
    rest = refs[4 + 3 * n:]
    if not first:
        o_in, m_in = rest[:2]
        rest = rest[2:]
    o_acc, m_acc = rest[:2]
    g_ups, g_dns, g_ubs = rest[2:2 + n], rest[2 + n:2 + 2 * n], rest[2 + 2 * n:2 + 3 * n]
    w_up, w_dn, up_b, hs, ps = rest[2 + 3 * n:]
    t = pl.program_id(0)
    for j in range(n):
        @pl.when(t == j)
        def _(j=j):
            w_up[...] = ups[j][...]
            w_dn[...] = dns[j][...]
            up_b[...] = bs[j][...].astype(F32)

    @pl.when(t == 0)
    def _():
        if first:
            o_acc[...] = jnp.zeros_like(o_acc)
            m_acc[...] = jnp.zeros_like(m_acc)
        else:
            o_acc[...] = o_in[...]
            m_acc[...] = m_in[...]

    L = nm.shape[0]
    total = jnp.zeros((1, w_up.shape[1]), F32)
    for i in range(L // QB):
        r = pl.ds(i * QB, QB)
        x = dot(nm[r, :], w_up[...]) + up_b[0:1, :]
        gd = dot(g[r, :], w_dn[...], NT)
        x2 = x * x
        th = jnp.tanh(x * (GA + (GA * GB) * x2))
        ht = 0.5 * th + 0.5
        h = (x * ht).astype(BF)
        dg = ht + x * (0.5 - 0.5 * (th * th)) * (GA + (3 * GA * GB) * x2)
        pg = (gd * dg).astype(BF)
        hs[r, :] = h
        ps[r, :] = pg
        total = total + jnp.sum(pg.astype(F32), axis=0, keepdims=True)
        o_acc[r, :] += dot(h, w_dn[...])
        m_acc[r, :] += dot(pg, w_up[...], NT)
    g_up = dot(nm_t[...], ps[...]).astype(BF)
    g_dn = dot(g_t[...], hs[...]).astype(BF)
    for j in range(n):
        @pl.when(t == j)
        def _(j=j):
            g_ubs[j][...] = total
            g_ups[j][...] = g_up
            g_dns[j][...] = g_dn


def mlp(nm, nm_t, g, g_t, bs, ups, dns, accs, name):
    n = len(ups)
    L, D = nm.shape
    F = ups[0].shape[1]
    last = bs[0].shape[0] // EXTRA - 1
    ins = [nm, nm_t, g, g_t]
    outs = pl.pallas_call(
        functools.partial(mlp_kernel, n, not accs),
        grid=(n,),
        in_specs=[full(a.shape) for a in ins]
        + [pl.BlockSpec((EXTRA, F), lambda t: (last, 0))] * n
        + [full(a.shape) for a in (*ups, *dns, *accs)],
        out_specs=[full((L, D))] * 2 + [full((D, F))] * (2 * n) + [full((1, F))] * n,
        out_shape=[sds((L, D), F32)] * 2 + [sds((D, F), BF)] * (2 * n) + [sds((1, F), F32)] * n,
        scratch_shapes=[pltpu.VMEM((D, F), BF), pltpu.VMEM((F, D), BF), pltpu.VMEM((EXTRA, F), F32), pltpu.VMEM((L, F), BF), pltpu.VMEM((L, F), BF)],
        compiler_params=params(60),
        cost_estimate=cost(11 * n),
        name=name,
    )(*ins, *bs, *ups, *dns, *accs)
    return outs[0], outs[1], outs[2:2 + n], outs[2 + n:2 + 2 * n], outs[2 + 2 * n:]


def second_back_kernel(middle, o_acc, m_acc, g, gain, down_bias, out, ag, ag_t, mg, sums):
    i = pl.program_id(0)
    mid = middle[...]
    out[...] = (mid + o_acc[...] + down_bias[...]).astype(BF)
    xhat, rstd = normalize(mid)
    d = m_acc[...]
    m = g[...].astype(F32) + norm_back(d * gain[...], xhat, rstd)
    mg[...] = m
    a = m.astype(BF)
    ag[...] = a
    ag_t[...] = a.T

    @pl.when(i == 0)
    def _():
        sums[...] = jnp.zeros_like(sums)

    sums[0:1, :] += jnp.sum(d * xhat, axis=0, keepdims=True)
    sums[1:2, :] += jnp.sum(d, axis=0, keepdims=True)
    sums[2:3, :] += jnp.sum(a.astype(F32), axis=0, keepdims=True)


def second_back(middle, o_acc, m_acc, g, gain, down_bias):
    L, D = middle.shape
    rows = pl.BlockSpec((QB, D), lambda i: (i, 0))
    cols = pl.BlockSpec((D, QB), lambda i: (0, i))
    return pl.pallas_call(
        second_back_kernel,
        grid=(L // QB,),
        in_specs=[rows] * 4 + [full(gain.shape), full(down_bias.shape)],
        out_specs=[rows, rows, cols, rows, full((8, D))],
        out_shape=[sds((L, D), BF), sds((L, D), BF), sds((D, L), BF), sds((L, D), F32), sds((8, D), F32)],
        compiler_params=params(60),
        cost_estimate=cost(5),
        name="second_back",
    )(middle, o_acc, m_acc, g, gain, down_bias)


def attend_back_kernel(first, *refs):
    ag, ag_t, normed_t, mask, ctx, joined, lse, w = refs[:8]
    rest = refs[8:]
    if not first:
        n_in = rest[0]
        rest = rest[1:]
    n_out, g_w, g_b, dctx, kt, dk, dv, jg = rest
    L, D = ag.shape
    C = ctx.shape[2]
    H = C // HD
    for i in range(L // QB):
        r = pl.ds(i * QB, QB)
        dctx[r, :] = dot(ag[r, :], w[3 * C:4 * C, :], NT).astype(BF)
        kt[:, r] = joined[0, 1, r, :].T
    masks = [head_mask(h, C) for h in range(H)]
    dk[...] = jnp.zeros_like(dk)
    dv[...] = jnp.zeros_like(dv)
    for i in range(L // QB):
        k0, kn = window(i)
        r = pl.ds(i * QB, QB)
        kr = pl.ds(k0, kn)
        q = joined[0, 0, r, :] * BF(HD ** -0.5)
        k = joined[0, 1, kr, :]
        v = joined[0, 2, kr, :]
        do = dctx[r, :]
        m = mask[i, :kn, :]
        lows, scores, dq = [], [], []
        qms = [q * masks[h] for h in range(H)]
        dos = [do * masks[h] for h in range(H)]
        for h in range(H):
            s = dot(k, qms[h], NT) + m
            p = jnp.exp(s - lse[0, h:h + 1, r])
            dp = dot(v, dos[h], NT)
            inner = jnp.sum(p * dp, axis=0, keepdims=True)
            ds = (p * (dp - inner)).astype(BF)
            lows.append(p.astype(BF))
            scores.append(ds)
            dq.append(dot(kt[h * HD:(h + 1) * HD, kr], ds))
        dv[kr, :] += dot(jnp.concatenate(lows, axis=1), jnp.concatenate(dos, axis=0))
        dk[kr, :] += dot(jnp.concatenate(scores, axis=1), jnp.concatenate(qms, axis=0))
        jg[r, :C] = (jnp.concatenate(dq, axis=0).T * HD ** -0.5).astype(BF)
    jg[:, C:2 * C] = dk[...].astype(BF)
    jg[:, 2 * C:] = dv[...].astype(BF)
    g_w[:, :3 * C] = dot(normed_t[...], jg[...]).astype(BF)
    g_w[:, 3 * C:] = dot(ag_t[...], ctx[0]).astype(BF)
    g_b[...] = jnp.sum(jg[...].astype(F32), axis=0, keepdims=True)
    for i in range(L // QB):
        r = pl.ds(i * QB, QB)
        a = dot(jg[r, :], w[:3 * C, :])
        n_out[r, :] = a if first else n_in[r, :] + a


def attend_back(ag, ag_t, normed_t, mask, saved, w, accs, name):
    joined, ctx, lse, s = saved
    L, D = ag.shape
    C = ctx.shape[2]
    at = lambda *shape: pl.BlockSpec((1,) + shape, lambda _: (s,) + (0,) * len(shape))
    return pl.pallas_call(
        functools.partial(attend_back_kernel, not accs),
        grid=(1,),
        in_specs=[full(a.shape) for a in (ag, ag_t, normed_t, mask)]
        + [at(L, C), at(3, L, C), at(8, L)]
        + [full(a.shape) for a in (w, *accs)],
        out_specs=[full((L, D)), full((D, 4 * C)), full((1, 3 * C))],
        out_shape=[sds((L, D), F32), sds((D, 4 * C), BF), sds((1, 3 * C), F32)],
        scratch_shapes=[pltpu.VMEM((L, C), BF), pltpu.VMEM((C, L), BF), pltpu.VMEM((L, C), F32), pltpu.VMEM((L, C), F32), pltpu.VMEM((L, 3 * C), BF)],
        compiler_params=params(60),
        cost_estimate=cost(15),
        name=name,
    )(ag, ag_t, normed_t, mask, ctx, joined, lse, w, *accs)


def first_back_kernel(stream, mg, n_acc, gain, slots, gtok, gth, sums):
    i = pl.program_id(0)
    xhat, rstd = normalize(stream[...].astype(F32))
    d = n_acc[...]
    sg = (mg[...] + norm_back(d * gain[...], xhat, rstd)).astype(BF)
    hot = one_hot(slots[...], i * QB, QB)
    covered = jnp.sum(hot.astype(F32), axis=1, keepdims=True) > 0.5
    gtok[...] = jnp.where(covered, 0.0, sg.astype(F32)).astype(BF)

    @pl.when(i == 0)
    def _():
        sums[...] = jnp.zeros_like(sums)
        gth[...] = jnp.zeros_like(gth)

    gth[...] += dot(hot.astype(BF), sg, ((0,), (0,)))
    sums[0:1, :] += jnp.sum(d * xhat, axis=0, keepdims=True)
    sums[1:2, :] += jnp.sum(d, axis=0, keepdims=True)


def first_back(stream, mg, n_acc, gain, slots):
    L, D = stream.shape
    rows = pl.BlockSpec((QB, D), lambda i: (i, 0))
    return pl.pallas_call(
        first_back_kernel,
        grid=(L // QB,),
        in_specs=[rows] * 3 + [full(gain.shape), full(slots.shape)],
        out_specs=[rows, full((slots.shape[1], D)), full((8, D))],
        out_shape=[sds((L, D), BF), sds((slots.shape[1], D), F32), sds((8, D), F32)],
        compiler_params=params(60),
        cost_estimate=cost(4),
        name="first_back",
    )(stream, mg, n_acc, gain, slots)


def swap(x, axis, size, bit):
    return lax.ppermute(x, axis, [(i, i ^ bit) for i in range(size)])


def local(
    n_dp,
    tokens,
    thoughts,
    thought_slots,
    segment_ids,
    attn_gain,
    attn_shift,
    qkv_weight,
    qkv_bias,
    out_weight,
    out_bias,
    mlp_gain,
    mlp_shift,
    up_weight,
    up_bias,
    down_weight,
    down_bias,
    cotangent,
):
    D = tokens.shape[2]
    C = qkv_weight.shape[2]
    F = up_weight.shape[1]
    core = lambda x: swap(x, "tensor", 4, 1)
    cross = lambda x: swap(x, "tensor", 4, 2)
    vec = lambda a: a.astype(F32).reshape(1, -1)

    biases = jnp.concatenate(
        [up_bias.reshape(1, F), jnp.pad(qkv_bias, ((0, 0), (0, F - C))), jnp.zeros((EXTRA - 3, F), BF)], 0
    )
    own = jnp.concatenate([jnp.transpose(qkv_weight, (1, 2, 0)).reshape(3 * C, D), out_weight, biases], 0)

    def gather(w):
        far = cross(w)
        return [w, core(w), far, core(far)]

    attn_w = gather(own)
    up_w = gather(up_weight)
    down_w = gather(down_weight)

    seg = segment_ids
    stream, normed, normed_t, cot_t, cot_sum, mask = first_norm(
        tokens[0], cotangent[0], thought_slots, thoughts[0], vec(attn_gain), vec(attn_shift), seg
    )
    j1, c1, l1 = attend(normed, mask, attn_w[:2], C, "attend_near")
    j2, c2, l2 = attend(normed, mask, attn_w[2:], C, "attend_far")
    middle, nm, nm_t = second_norm(stream, vec(out_bias), vec(mlp_gain), vec(mlp_shift), (c1, c2), attn_w)
    g = cotangent[0]
    o, m, gu1, gd1, gb1 = mlp(nm, nm_t, g, cot_t, attn_w[:2], up_w[:2], down_w[:2], (), "mlp_near")
    o, m, gu2, gd2, gb2 = mlp(nm, nm_t, g, cot_t, attn_w[2:], up_w[2:], down_w[2:], (o, m), "mlp_far")
    out, ag, ag_t, mg, sums2 = second_back(middle, o, m, g, vec(mlp_gain), vec(down_bias))
    saved = [(j1, c1, l1, 0), (j1, c1, l1, 1), (j2, c2, l2, 0), (j2, c2, l2, 1)]
    g_attn, g_qb, accs = [None] * 4, [None] * 4, ()
    for s in (3, 2, 1, 0):
        acc, g_attn[s], g_qb[s] = attend_back(ag, ag_t, normed_t, mask, saved[s], attn_w[s], accs, "attend_back%d" % s)
        accs = (acc,)
    gtok, gth, sums1 = first_back(stream, mg, accs[0], vec(attn_gain), thought_slots)

    wide = lambda a: a.astype(F32)

    def scatter(parts):
        near = core(parts[1])
        far = (wide(parts[2]) + wide(core(parts[3]))).astype(BF)
        total = (wide(parts[0]) + wide(near) + wide(cross(far))).astype(BF)
        pieces = lax.all_to_all(total, "dp", 0, 0, tiled=True)
        return jnp.sum(wide(pieces).reshape(n_dp, D // n_dp, -1), axis=0)

    r_up = scatter((*gu1, *gu2))
    r_dn = scatter((*gd1, *gd2))
    r_at = scatter(g_attn)

    me = lax.axis_index("tensor")
    rel = jnp.stack(
        [jnp.concatenate([b, jnp.pad(q, ((0, 0), (0, F - 3 * C)))], 0) for b, q in zip((*gb1, *gb2), g_qb)]
    )
    ordered = jnp.concatenate([rel[me ^ t] for t in range(4)], 0)
    small = jnp.concatenate([ordered, sums1[:2], sums2[:3], cot_sum], 0)
    for axis, size in (("tensor", 4), ("dp", n_dp)):
        bit = 1
        while bit < size:
            small = small + swap(small, axis, size, bit)
            bit *= 2
    mine = lax.dynamic_slice(small, (2 * me, 0), (2, F))
    return (
        out[None],
        gtok[None],
        gth.astype(BF)[None],
        small[8],
        small[9],
        r_at[:, :3 * C].reshape(-1, 3, C),
        jnp.stack([mine[1, :C], mine[1, 2 * C:3 * C]]),
        r_at[:, 3 * C:].T,
        small[12],
        small[10],
        small[11],
        r_up,
        mine[0],
        r_dn.T,
        small[13],
    )


def solution(mesh):
    rows = P(("dp", "tensor"), None, None)
    placed = (
        rows,
        rows,
        P(("dp", "tensor"), None),
        P(("dp", "tensor"), None),
        P(),
        P(),
        P(None, None, "tensor"),
        P(None, "tensor"),
        P("tensor", None),
        P(),
        P(),
        P(),
        P(None, "tensor"),
        P("tensor"),
        P("tensor", None),
        P(),
        rows,
    )
    return jax.shard_map(
        functools.partial(local, mesh.shape["dp"]),
        mesh=mesh,
        in_specs=placed,
        out_specs=(
            rows,
            rows,
            rows,
            P(),
            P(),
            P("dp", None, "tensor"),
            P(None, "tensor"),
            P("tensor", "dp"),
            P(),
            P(),
            P(),
            P("dp", "tensor"),
            P("tensor"),
            P("tensor", "dp"),
            P(),
        ),
        check_vma=False,
    )
```

```python
import functools

import jax
import jax.numpy as jnp
from jax import lax
from jax.experimental import pallas as pl
from jax.experimental.pallas import tpu as pltpu
from jax.sharding import PartitionSpec as P

F32 = jnp.float32
BF = jnp.bfloat16
HD = 64
QB = 256
EPS = 1e-05
NEG = -1e30
NN = ((1,), (0,))
NT = ((1,), (1,))
GA, GB = 0.7978845608028654, 0.044715
EXTRA = 32
SMALL = pl.BlockSpec(memory_space=pltpu.SMEM)


def dot(a, b, dims=NN):
    return lax.dot_general(a, b, (dims, ((), ())), preferred_element_type=F32)


def full(shape):
    zeros = (0,) * len(shape)
    return pl.BlockSpec(tuple(shape), lambda *_: zeros)


def sds(shape, dtype):
    return jax.ShapeDtypeStruct(tuple(shape), dtype)


def vmem(shape, dtype):
    return pltpu.VMEM(tuple(shape), dtype)


def keep(x):
    return pltpu.with_memory_space_constraint(x, pltpu.VMEM)


RES = pl.BlockSpec(memory_space=pltpu.VMEM)


def params(mib):
    return pltpu.CompilerParams(vmem_limit_bytes=mib << 20)


def cost(micros):
    return pl.CostEstimate(flops=int(micros * 1e8), bytes_accessed=int(micros * 1e5), transcendentals=0)


def normalize(x):
    mean = jnp.mean(x, axis=-1, keepdims=True)
    xc = x - mean
    var = jnp.mean(xc * xc, axis=-1, keepdims=True)
    rstd = lax.rsqrt(var + EPS)
    return xc * rstd, rstd


def norm_back(u, xhat, rstd):
    mu = jnp.mean(u, axis=-1, keepdims=True)
    mux = jnp.mean(u * xhat, axis=-1, keepdims=True)
    return rstd * (u - mu - xhat * mux)


def one_hot(slots, row0, rows):
    pos = lax.broadcasted_iota(jnp.int32, (rows, slots.shape[1]), 0) + row0
    return pos == slots


def run(kernel, ins, specs, deps, outs, out_specs, scratch=(), mib=16, micros=4, name=None, grid=(1,), aliases=None):
    n, k = len(ins), len(deps)
    return pl.pallas_call(
        lambda *refs: kernel(*refs[:n], *refs[n + k:]),
        grid=grid,
        in_specs=list(specs) + [pl.BlockSpec(memory_space=pl.ANY)] * k,
        out_specs=out_specs,
        out_shape=outs,
        scratch_shapes=list(scratch),
        input_output_aliases=aliases or {},
        compiler_params=params(mib),
        cost_estimate=cost(micros),
        name=name,
    )(*[keep(a) if sp is RES else a for a, sp in zip(ins, specs)], *deps)


def piece_order(bits):
    k = len(bits)
    return [sum(bits[j] for j in range(k) if p >> (k - 1 - j) & 1) for p in range(1 << k)]


def ordered(x, order):
    rows = x.shape[0] // len(order)
    if rows % 16:
        x = x.astype(F32)
    return jnp.concatenate([x[d * rows:(d + 1) * rows] for d in order], 0).astype(BF)


def halves(h, refs):
    n = refs[0].shape[0]
    first = h[0] * n
    for ref, at in zip(refs, (first, n - first)):
        yield ref, pl.ds(pl.multiple_of(at, 16), n)


def whole(h, refs, scratch):
    if len(refs) == 1:
        return refs[0]
    for ref, rows in halves(h, refs):
        scratch[rows, :] = ref[...]
    return scratch


def front(h, refs):
    return refs[0][...] if len(refs) == 1 else jnp.where(h[0] == 0, refs[0][...], refs[1][...])


def first_kernel(attn_order, down_order, tok, cot, slots, thoughts, gain, shift, seg, stream, normed, normed_t, cot_v, cot_t, cot_sum, mask):
    i = pl.program_id(0)
    r = pl.ds(pl.multiple_of(i * QB, QB), QB)
    hot = one_hot(slots[...], i * QB, QB)
    inserted = dot(hot.astype(BF), thoughts[...])
    covered = jnp.sum(hot.astype(F32), axis=1, keepdims=True) > 0.5
    x = jnp.where(covered, inserted, tok[...].astype(F32))
    stream[r, :] = x.astype(BF)
    xhat, _ = normalize(x)
    n = (xhat * gain[...] + shift[...]).astype(BF)
    normed[r, :] = n
    normed_t[:, r] = ordered(n.T, attn_order)
    g = cot[...]
    cot_v[r, :] = g
    cot_t[:, r] = ordered(g.T, down_order)

    @pl.when(i == 0)
    def _():
        cot_sum[...] = jnp.zeros_like(cot_sum)

    cot_sum[...] += jnp.sum(g.astype(F32), axis=0, keepdims=True)
    k0 = pl.multiple_of(jnp.maximum(i - 1, 0) * QB, QB)
    seg_q = seg[:, r]
    seg_k = jnp.broadcast_to(seg[:, pl.ds(k0, 2 * QB)], (QB, 2 * QB)).T
    kpos = lax.broadcasted_iota(jnp.int32, (2 * QB, QB), 0) + k0
    qpos = lax.broadcasted_iota(jnp.int32, (2 * QB, QB), 1) + i * QB
    mask[i] = jnp.where((seg_k == seg_q) & (kpos <= qpos), 0.0, NEG)


def first_norm(orders, tok, cot, slots, thoughts, gain, shift, seg):
    L, D = tok.shape
    nq = L // QB
    rows = pl.BlockSpec((QB, D), lambda i: (i, 0))
    ins = (tok, cot, slots, thoughts, gain, shift, seg)
    return run(
        functools.partial(first_kernel, *orders),
        ins,
        [rows, rows] + [full(a.shape) for a in ins[2:]],
        (),
        [vmem((L, D), BF), vmem((L, D), BF), vmem((D, L), BF), vmem((L, D), BF), vmem((D, L), BF), sds((1, D), F32), vmem((nq, 2 * QB, QB), F32)],
        [RES] * 5 + [full((1, D)), RES],
        grid=(nq,),
        name="first_norm",
    )


def window(i):
    return (0, QB) if i == 0 else ((i - 1) * QB, 2 * QB)


def head_mask(h, width):
    lane = lax.broadcasted_iota(jnp.int32, (1, width), 1)
    return ((lane >= h * HD) & (lane < (h + 1) * HD)).astype(BF)


def attend_kernel(h0, normed, mask, *refs):
    *ws, joined, ctx, lse, vt, buf = refs
    L = normed.shape[0]
    C = ctx.shape[1]
    w = whole(h0, ws, buf)
    bias = w[:EXTRA, :].astype(F32)
    base = EXTRA
    for i in range(L // QB):
        r = pl.ds(i * QB, QB)
        for c in range(3):
            v = dot(normed[r, :], w[base + c * C:base + (c + 1) * C, :], NT)
            if c != 1:
                b = 1 + c // 2
                v = v + bias[b:b + 1, :C]
            v = v.astype(BF)
            joined[c, r, :] = v
            if c == 2:
                vt[:, r] = v.T
    masks = [head_mask(h, C) for h in range(C // HD)]
    for i in range(L // QB):
        k0, kn = window(i)
        r = pl.ds(i * QB, QB)
        q = joined[0, r, :] * BF(HD ** -0.5)
        k = joined[1, pl.ds(k0, kn), :]
        m = mask[i, :kn, :]
        outs, stats = [], []
        for h in range(C // HD):
            s = dot(k, q * masks[h], NT) + m
            top = jnp.max(s, axis=0, keepdims=True)
            e = jnp.exp(s - top)
            total = jnp.sum(e, axis=0, keepdims=True)
            p = (e * (1.0 / total)).astype(BF)
            outs.append(dot(vt[h * HD:(h + 1) * HD, pl.ds(k0, kn)], p))
            stats.append(top + jnp.log(total))
        ctx[r, :] = jnp.concatenate(outs, axis=0).T.astype(BF)
        for h in range(C // HD):
            lse[h:h + 1, r] = stats[h]


def attend(h, normed, mask, ws, C, name, deps=()):
    L, D = normed.shape
    return run(
        attend_kernel,
        (h, normed, mask, *ws),
        [SMALL, RES, RES] + [full(w.shape) for w in ws],
        deps,
        [vmem((3, L, C), BF), vmem((L, C), BF), sds((8, L), F32)],
        [RES, RES, full((8, L))],
        [pltpu.VMEM((C, L), BF), pltpu.VMEM((3 * C + EXTRA, D), BF)],
        name=name,
    )


def second_norm(h, order, stream, out_bias, gain, shift, ctxs, ws):
    L, D = stream.shape
    n = len(ws)
    C = ctxs[0].shape[1]
    flat = [w for pair in ws for w in pair]

    def kernel(h, stream, out_bias, gain, shift, *refs):
        *refs, middle, nm, nm_t, buf = refs
        i = pl.program_id(0)
        r = pl.ds(pl.multiple_of(i * QB, QB), QB)

        @pl.when(i == 0)
        def _():
            at = n
            for j, pair in enumerate(ws):
                for ref, rows in halves(h, refs[at:at + len(pair)]) if len(pair) > 1 else [(refs[at], slice(None))]:
                    buf[j, rows, :] = ref[...]
                at += len(pair)

        acc = stream[r, :].astype(F32) + out_bias[...]
        for j in range(n):
            acc = acc + dot(refs[j][r, :], buf[j])
        middle[r, :] = acc
        xhat, _ = normalize(acc)
        v = (xhat * gain[...] + shift[...]).astype(BF)
        nm[r, :] = v
        nm_t[:, r] = ordered(v.T, order)

    return run(
        kernel,
        (h, stream, out_bias, gain, shift, *ctxs, *flat),
        [SMALL, RES] + [full(a.shape) for a in (out_bias, gain, shift)] + [RES] * n + [full(w.shape) for w in flat],
        (),
        [vmem((L, D), F32), vmem((L, D), BF), vmem((D, L), BF)],
        [RES] * 3,
        [pltpu.VMEM((n, C, D), BF)],
        grid=(L // QB,),
        name="second_norm",
    )


def mlp_kernel(n, first, h0, nm, g, *refs):
    bias, ups, dns, rest = refs[:n], refs[n:2 * n], refs[2 * n:3 * n], refs[3 * n:]
    if not first:
        o_in, m_in = rest[:2]
        rest = rest[2:]
    o_acc, m_acc, hs, ps, g_ub, u_buf, d_buf = rest
    L = nm.shape[0]
    w_up, w_dn = whole(h0, ups, u_buf), whole(h0, dns, d_buf)
    up_b = front(h0, bias)[0:1, :].astype(F32)
    total = jnp.zeros((1, w_up.shape[1]), F32)
    for i in range(L // QB):
        r = pl.ds(i * QB, QB)
        x = dot(nm[r, :], w_up[...]) + up_b
        gd = dot(g[r, :], w_dn[...], NT)
        x2 = x * x
        th = jnp.tanh(x * (GA + (GA * GB) * x2))
        ht = 0.5 * th + 0.5
        h = (x * ht).astype(BF)
        dg = ht + x * (0.5 - 0.5 * (th * th)) * (GA + (3 * GA * GB) * x2)
        pg = (gd * dg).astype(BF)
        hs[r, :] = h
        ps[r, :] = pg
        total = total + jnp.sum(pg.astype(F32), axis=0, keepdims=True)
        o, m = dot(h, w_dn[...]), dot(pg, w_up[...], NT)
        o_acc[r, :] = o if first else o_in[r, :] + o
        m_acc[r, :] = m if first else m_in[r, :] + m
    g_ub[...] = total


def mlp(h, nm, g, biases, ups, dns, accs, name, deps=()):
    L, D = nm.shape
    n = len(ups)
    F = ups[0].shape[1] if n == 1 else D
    return run(
        functools.partial(mlp_kernel, n, not accs),
        (h, nm, g, *biases, *ups, *dns, *accs),
        [SMALL, RES, RES] + [pl.BlockSpec((EXTRA, F), lambda _: (0, 0))] * n + [full(w.shape) for w in (*ups, *dns)] + [RES] * len(accs),
        deps,
        [vmem((L, D), F32)] * 2 + [vmem((L, F), BF)] * 2 + [sds((1, F), F32)],
        [RES] * 4 + [full((1, F))],
        [pltpu.VMEM((D, F), BF), pltpu.VMEM((F, D), BF)],
        aliases={3 + 3 * n: 0, 4 + 3 * n: 1} if accs else None,
        mib=20,
        name=name,
    )


def split_kernel(products, h0, refs, outs, adds):
    for j, (left, right, bit) in enumerate(products):
        n = left.shape[0] // 2
        for half, out in ((h0[bit], outs[2 * j]), (1 - h0[bit], outs[2 * j + 1])):
            rows = pl.ds(pl.multiple_of(half * n, n), n)
            v = dot(left[rows, :], right[...])
            out[...] = (v + adds[j][rows, :].astype(F32)).astype(BF)


def mlp_grads(h, nm_t, g_t, hs, ps, adds, bits, name, deps=()):
    D, L = nm_t.shape
    F = hs.shape[1]

    def kernel(h0, nm_t, g_t, hs, ps, *refs):
        if not adds:
            refs[0][...] = dot(nm_t[...], ps[...]).astype(BF)
            refs[1][...] = dot(g_t[...], hs[...]).astype(BF)
        else:
            split_kernel([(nm_t, ps, bits[0]), (g_t, hs, bits[1])], h0, refs, refs[2:], refs[:2])

    shape = (D // 2, F) if adds else (D, F)
    count = 4 if adds else 2
    return run(
        kernel,
        (h, nm_t, g_t, hs, ps, *adds),
        [SMALL] + [RES] * 4 + [full(a.shape) for a in adds],
        deps,
        [sds(shape, BF)] * count,
        [full(shape)] * count,
        mib=16,
        name=name,
    )


def second_back_kernel(order, middle, o_acc, m_acc, g, gain, down_bias, out, ag, ag_t, mg, sums):
    i = pl.program_id(0)
    r = pl.ds(pl.multiple_of(i * QB, QB), QB)
    mid = middle[r, :]
    out[...] = (mid + o_acc[r, :] + down_bias[...]).astype(BF)
    xhat, rstd = normalize(mid)
    d = m_acc[r, :]
    m = g[r, :].astype(F32) + norm_back(d * gain[...], xhat, rstd)
    mg[r, :] = m
    a = m.astype(BF)
    ag[r, :] = a
    ag_t[:, r] = ordered(a.T, order)

    @pl.when(i == 0)
    def _():
        sums[...] = jnp.zeros_like(sums)

    sums[0:1, :] += jnp.sum(d * xhat, axis=0, keepdims=True)
    sums[1:2, :] += jnp.sum(d, axis=0, keepdims=True)
    sums[2:3, :] += jnp.sum(a.astype(F32), axis=0, keepdims=True)


def second_back(order, middle, o_acc, m_acc, g, gain, down_bias):
    L, D = middle.shape
    rows = pl.BlockSpec((QB, D), lambda i: (i, 0))
    return run(
        functools.partial(second_back_kernel, order),
        (middle, o_acc, m_acc, g, gain, down_bias),
        [RES] * 4 + [full(gain.shape), full(down_bias.shape)],
        (),
        [sds((L, D), BF), vmem((L, D), BF), vmem((D, L), BF), vmem((L, D), F32), sds((8, D), F32)],
        [rows, RES, RES, RES, full((8, D))],
        grid=(L // QB,),
        name="second_back",
    )


def attend_back_kernel(n, first, split, bit, h0, ag, ag_t, normed_t, mask, joined, ctx, lse, *refs):
    ws, outs_w, rest = refs[:n], refs[n:2 * n], refs[2 * n:]
    if not first:
        n_in, rest = rest[0], rest[1:]
    if split:
        add, rest = rest[0], rest[1:]
    n_out, *g_w, g_b, dctx, kt, dk, dv, jg, buf, o_buf = rest
    L, D = ag.shape
    C = ctx.shape[1]
    H = C // HD
    w = whole(h0, ws, buf)
    w_out = whole(h0, outs_w, o_buf)
    for i in range(L // QB):
        r = pl.ds(i * QB, QB)
        dctx[r, :] = dot(ag[r, :], w_out[...], NT).astype(BF)
        kt[:, r] = joined[1, r, :].T
    masks = [head_mask(h, C) for h in range(H)]
    dk[...] = jnp.zeros_like(dk)
    dv[...] = jnp.zeros_like(dv)
    for i in range(L // QB):
        k0, kn = window(i)
        r = pl.ds(i * QB, QB)
        kr = pl.ds(k0, kn)
        q = joined[0, r, :] * BF(HD ** -0.5)
        k = joined[1, kr, :]
        v = joined[2, kr, :]
        do = dctx[r, :]
        m = mask[i, :kn, :]
        lows, scores, dq = [], [], []
        qms = [q * masks[h] for h in range(H)]
        dos = [do * masks[h] for h in range(H)]
        for h in range(H):
            s = dot(k, qms[h], NT) + m
            p = jnp.exp(s - lse[h:h + 1, r])
            dp = dot(v, dos[h], NT)
            inner = jnp.sum(p * dp, axis=0, keepdims=True)
            ds = (p * (dp - inner)).astype(BF)
            lows.append(p.astype(BF))
            scores.append(ds)
            dq.append(dot(kt[h * HD:(h + 1) * HD, kr], ds))
        dv[kr, :] += dot(jnp.concatenate(lows, axis=1), jnp.concatenate(dos, axis=0))
        dk[kr, :] += dot(jnp.concatenate(scores, axis=1), jnp.concatenate(qms, axis=0))
        jg[r, :C] = (jnp.concatenate(dq, axis=0).T * HD ** -0.5).astype(BF)
    jg[:, C:2 * C] = dk[...].astype(BF)
    jg[:, 2 * C:] = dv[...].astype(BF)
    if split:
        rows_n = D // 2
        for half, out in ((h0[bit], g_w[0]), (1 - h0[bit], g_w[1])):
            rows = pl.ds(pl.multiple_of(half * rows_n, rows_n), rows_n)
            v = dot(normed_t[rows, :], jg[...]) + add[rows, :3 * C].astype(F32)
            out[:, :3 * C] = v.astype(BF)
            v = dot(ag_t[rows, :], ctx[...]) + add[rows, 3 * C:].astype(F32)
            out[:, 3 * C:] = v.astype(BF)
    else:
        g_w[0][:, :3 * C] = dot(normed_t[...], jg[...]).astype(BF)
        g_w[0][:, 3 * C:] = dot(ag_t[...], ctx[...]).astype(BF)
    g_b[...] = jnp.sum(jg[...].astype(F32), axis=0, keepdims=True)
    for i in range(L // QB):
        r = pl.ds(i * QB, QB)
        a = dot(jg[r, :], w[EXTRA:, :])
        n_out[r, :] = a if first else n_in[r, :] + a


def attend_back(h, ag, ag_t, normed_t, mask, saved, ws, outs_w, accs, adds, bit, name, deps=()):
    joined, ctx, lse = saved
    L, D = ag.shape
    C = ctx.shape[1]
    n = len(ws)
    shape = (D // 2, 4 * C) if adds else (D, 4 * C)
    count = 2 if adds else 1
    return run(
        functools.partial(attend_back_kernel, n, not accs, bool(adds), bit),
        (h, ag, ag_t, normed_t, mask, joined, ctx, lse, *ws, *outs_w, *accs, *adds),
        [SMALL] + [RES] * 6 + [full(a.shape) for a in (lse, *ws, *outs_w)] + [RES] * len(accs) + [full(a.shape) for a in adds],
        deps,
        [vmem((L, D), F32)] + [sds(shape, BF)] * count + [sds((1, 3 * C), F32)],
        [RES] + [full(shape)] * count + [full((1, 3 * C))],
        [pltpu.VMEM((L, C), BF), pltpu.VMEM((C, L), BF), pltpu.VMEM((L, C), F32), pltpu.VMEM((L, C), F32), pltpu.VMEM((L, 3 * C), BF), pltpu.VMEM((3 * C + EXTRA, D), BF), pltpu.VMEM((C, D), BF)],
        aliases={8 + 2 * n: 0} if accs else None,
        mib=20,
        name=name,
    )


def first_back_kernel(stream, mg, n_acc, gain, slots, gtok, gth, sums):
    i = pl.program_id(0)
    r = pl.ds(pl.multiple_of(i * QB, QB), QB)
    xhat, rstd = normalize(stream[r, :].astype(F32))
    d = n_acc[r, :]
    sg = (mg[r, :] + norm_back(d * gain[...], xhat, rstd)).astype(BF)
    hot = one_hot(slots[...], i * QB, QB)
    covered = jnp.sum(hot.astype(F32), axis=1, keepdims=True) > 0.5
    gtok[...] = jnp.where(covered, 0.0, sg.astype(F32)).astype(BF)

    @pl.when(i == 0)
    def _():
        sums[...] = jnp.zeros_like(sums)
        gth[...] = jnp.zeros_like(gth)

    gth[...] += dot(hot.astype(BF), sg, ((0,), (0,)))
    sums[0:1, :] += jnp.sum(d * xhat, axis=0, keepdims=True)
    sums[1:2, :] += jnp.sum(d, axis=0, keepdims=True)


def first_back(stream, mg, n_acc, gain, slots):
    L, D = stream.shape
    rows = pl.BlockSpec((QB, D), lambda i: (i, 0))
    return run(
        first_back_kernel,
        (stream, mg, n_acc, gain, slots),
        [RES] * 3 + [full(gain.shape), full(slots.shape)],
        (),
        [sds((L, D), BF), sds((slots.shape[1], D), F32), sds((8, D), F32)],
        [rows, full((slots.shape[1], D)), full((8, D))],
        grid=(L // QB,),
        name="first_back",
    )


def swap(x, axis, size, bit):
    return lax.ppermute(x, axis, [(i, i ^ bit) for i in range(size)])


def after(x, dep):
    return lax.optimization_barrier((x, dep))


def local(
    n_dp,
    tokens,
    thoughts,
    thought_slots,
    segment_ids,
    attn_gain,
    attn_shift,
    qkv_weight,
    qkv_bias,
    out_weight,
    out_bias,
    mlp_gain,
    mlp_shift,
    up_weight,
    up_bias,
    down_weight,
    down_bias,
    cotangent,
):
    D = tokens.shape[2]
    C = qkv_weight.shape[2]
    F = up_weight.shape[1]
    core = lambda x: swap(x, "tensor", 4, 1)
    cross = lambda x: swap(x, "tensor", 4, 2)
    vec = lambda a: a.astype(F32).reshape(1, -1)

    tie = lax.optimization_barrier
    dp = lax.axis_index("dp")
    h = jnp.stack([dp & 1, dp >> 1 & 1]).astype(jnp.int32)
    beside = lambda x: swap(x, "dp", n_dp, 1)
    my_half = lambda w: lax.dynamic_slice_in_dim(w, (dp & 1) * (w.shape[0] // 2), w.shape[0] // 2, 0)

    bits = [1 << i for i in range(n_dp.bit_length() - 1)]
    attn_bits, up_bits, down_bits = bits, bits, bits[1:2] + bits[:1] + bits[2:]
    attn_order, up_order, down_order = map(piece_order, (attn_bits, up_bits, down_bits))

    biases = jnp.concatenate(
        [up_bias.reshape(1, F), jnp.pad(qkv_bias, ((0, 0), (0, F - C))), jnp.zeros((EXTRA - 3, F), BF)], 0
    )
    qkv = jnp.concatenate([biases, jnp.transpose(qkv_weight, (1, 2, 0)).reshape(3 * C, D)], 0)
    qkv_x = cross(my_half(qkv))
    qkv_w = [(qkv,), (core(qkv),)]
    out_w = [(out_weight,), (core(out_weight),)]
    up_w = [(up_weight,), (core(up_weight),)]
    down_w = [(down_weight,), (core(down_weight),)]
    out_s, up_s, down_s = my_half(out_weight), my_half(up_weight), my_half(down_weight)

    g = cotangent[0]
    stream, normed, normed_t, g_v, cot_t, cot_sum, mask = first_norm(
        (attn_order, down_order), tokens[0], g, thought_slots, thoughts[0], vec(attn_gain), vec(attn_shift), segment_ids
    )
    saved = [None] * 4

    def forward(s, deps=()):
        saved[s] = attend(h, normed, mask, qkv_w[s], C, "attend%d" % s, deps)

    def wait(arrays, s):
        *arrays, stats = tie((*arrays, saved[s][2]))
        saved[s] = (*saved[s][:2], stats)
        return arrays

    forward(0, (out_s, up_s, down_s))
    forward(1)
    qkv_x, out_s, up_s, down_s = wait((qkv_x, out_s, up_s, down_s), 1)
    qkv_y, qkv_cx = beside(qkv_x), core(qkv_x)
    out_x, up_x, down_x = cross(out_s), cross(up_s), cross(down_s)
    qkv_w.append((qkv_x, qkv_y))
    forward(2, (qkv_cx,))
    qkv_y2, out_x = wait((qkv_y, out_x), 2)
    qkv_w.append((qkv_cx, core(qkv_y2)))
    out_y, out_cx = beside(out_x), core(out_x)
    forward(3)
    out_y, out_cx, up_x = wait((out_y, out_cx, up_x), 3)
    out_w += [(out_x, out_y), (out_cx, core(out_y))]
    up_y, up_cx = beside(up_x), core(up_x)
    middle, nm, nm_t = second_norm(
        h, up_order, stream, vec(out_bias), vec(mlp_gain), vec(mlp_shift), [c for _, c, _ in saved], out_w
    )
    accs, gb, acts, grads = (), [None] * 4, [None] * 4, [None] * 4
    first_bits = (up_bits[0].bit_length() - 1, down_bits[0].bit_length() - 1)

    def hidden(s, deps=()):
        o, m, hs, ps, gb[s] = mlp(h, nm, g_v, (qkv_w[s][:1] if s < 2 else qkv_w[s]), up_w[s], down_w[s], accs, "mlp%d" % s, deps)
        acts[s] = (hs, ps)
        return o, m

    def hidden_grads(s, adds=(), deps=()):
        grads[s] = mlp_grads(h, nm_t, cot_t, *acts[s], adds, first_bits, "mlp_grads%d" % s, deps)

    accs = hidden(1)
    hidden_grads(1)
    down_x, gb[1] = tie((down_x, gb[1]))
    down_y, down_cx = beside(down_x), core(down_x)
    near = [core(a) for a in grads[1]]
    accs = hidden(0)
    hidden_grads(0, near)
    up_y, up_cx, down_y, down_cx, gb[0] = tie((up_y, up_cx, down_y, down_cx, gb[0]))
    up_w += [(up_x, up_y), (up_cx, core(up_y))]
    down_w += [(down_x, down_y), (down_cx, core(down_y))]
    accs = hidden(2, grads[0])
    accs = hidden(3)
    hidden_grads(3)
    near = [core(a) for a in grads[3]]
    out, ag, ag_t, mg, sums2 = second_back(attn_order, middle, *accs, g_v, vec(mlp_gain), vec(down_bias))
    hidden_grads(2, near, (sums2,))

    wide = lambda a: a.astype(F32)

    def total(arrays):
        t = wide(arrays[0])
        for a in arrays[1:]:
            t = t + wide(a)
        return t

    def part(arrays, bit, mine):
        n = arrays[0].shape[0] // 2
        at = jnp.where((dp & bit != 0) == mine, n, 0)
        return [lax.dynamic_slice_in_dim(a, at, n, 0) for a in arrays]

    def along(sent, bit):
        return swap(sent, "dp", n_dp, bit)

    def outgoing(arrays, bit):
        return total(part(arrays, bit, False)).astype(BF)

    g_attn, g_qb = [None] * 4, [None] * 4
    attn_bit = attn_bits[0].bit_length() - 1

    def back(s, accs, adds=(), deps=()):
        acc, *g_attn[s], g_qb[s] = attend_back(
            h, ag, ag_t, normed_t, mask, saved[s], qkv_w[s], out_w[s], accs, adds, attn_bit, "attend_back%d" % s, deps
        )
        return (acc,)

    ways = (up_bits, down_bits)
    kept = lambda s: [grads[s][0], grads[s][2]]
    sent = lambda s: [grads[s][1], grads[s][3]]
    own = [[k, along(x, w[0])] for k, x, w in zip(kept(0), sent(0), ways)]
    far = [[k, along(x, w[0])] for k, x, w in zip(kept(2), sent(2), ways)]
    own_s = [outgoing(a, w[1]) for a, w in zip(own, ways)]
    accs = back(3, (), (), (*own_s, *sent(2)))
    own = [part(a, w[1], True) + [along(x, w[1])] for a, x, w in zip(own, own_s, ways)]
    accs = back(1, accs)
    far[0][1], far[1][1], g_qb[1] = tie((far[0][1], far[1][1], g_qb[1]))
    far_s = [outgoing(a, w[1]) for a, w in zip(far, ways)]
    accs = back(2, accs, (core(g_attn[3][0]),), far_s)
    far = [part(a, w[1], True) + [along(x, w[1])] for a, x, w in zip(far, far_s, ways)]
    attn_far = [g_attn[2][0], along(g_attn[2][1], attn_bits[0])]
    far[0][-1], far[1][-1], g_qb[2] = tie((far[0][-1], far[1][-1], g_qb[2]))
    far_s = [total(a).astype(BF) for a in far]
    accs = back(0, accs, (core(g_attn[1][0]),), far_s)
    own = [a + [cross(x)] for a, x in zip(own, far_s)]
    attn_own = [g_attn[0][0], along(g_attn[0][1], attn_bits[0])]
    attn_far[1], g_qb[0] = tie((attn_far[1], g_qb[0]))
    far_s = outgoing(attn_far, attn_bits[1])
    gtok, gth, sums1 = first_back(stream, mg, accs[0], vec(attn_gain), thought_slots)
    attn_far = part(attn_far, attn_bits[1], True) + [along(far_s, attn_bits[1])]
    own_s = outgoing(attn_own, attn_bits[1])
    attn_own = part(attn_own, attn_bits[1], True) + [along(own_s, attn_bits[1])]
    attn_own.append(cross(total(attn_far).astype(BF)))
    for i in range(2, len(bits)):
        sums = [(*own, attn_own), (*ways, attn_bits)]
        own_s = [outgoing(a, w[i]) for a, w in zip(*sums)]
        *own, attn_own = [part(a, w[i], True) + [along(x, w[i])] for a, x, w in zip(sums[0], own_s, sums[1])]
    r_up, r_dn, r_at = total(own[0]), total(own[1]), total(attn_own)

    me = lax.axis_index("tensor")
    rel = jnp.stack(
        [jnp.concatenate([b, jnp.pad(q, ((0, 0), (0, F - 3 * C)))], 0) for b, q in zip(gb, g_qb)]
    )
    ordered = jnp.concatenate([rel[me ^ t] for t in range(4)], 0)
    small = jnp.concatenate([ordered, sums1[:2], sums2[:3], cot_sum], 0)
    for axis, size in (("tensor", 4), ("dp", n_dp)):
        bit = 1
        while bit < size:
            small = small + swap(small, axis, size, bit)
            bit *= 2
    mine = lax.dynamic_slice(small, (2 * me, 0), (2, F))
    return (
        out[None],
        gtok[None],
        gth.astype(BF)[None],
        small[8],
        small[9],
        r_at[:, :3 * C].reshape(-1, 3, C),
        jnp.stack([mine[1, :C], mine[1, 2 * C:3 * C]]),
        r_at[:, 3 * C:].T,
        small[12],
        small[10],
        small[11],
        r_up,
        mine[0],
        r_dn.T,
        small[13],
    )


def solution(mesh):
    rows = P(("dp", "tensor"), None, None)
    placed = (
        rows,
        rows,
        P(("dp", "tensor"), None),
        P(("dp", "tensor"), None),
        P(),
        P(),
        P(None, None, "tensor"),
        P(None, "tensor"),
        P("tensor", None),
        P(),
        P(),
        P(),
        P(None, "tensor"),
        P("tensor"),
        P("tensor", None),
        P(),
        rows,
    )
    return jax.shard_map(
        functools.partial(local, mesh.shape["dp"]),
        mesh=mesh,
        in_specs=placed,
        out_specs=(
            rows,
            rows,
            rows,
            P(),
            P(),
            P("dp", None, "tensor"),
            P(None, "tensor"),
            P("tensor", "dp"),
            P(),
            P(),
            P(),
            P("dp", "tensor"),
            P("tensor"),
            P("tensor", "dp"),
            P(),
        ),
        check_vma=False,
    )
```

```python
import functools

import jax
import jax.numpy as jnp
from jax import lax
from jax.experimental import pallas as pl
from jax.experimental.pallas import tpu as pltpu
from jax.sharding import PartitionSpec as P

F32 = jnp.float32
BF = jnp.bfloat16
HD = 64
QB = 256
EPS = 1e-05
NEG = -1e30
NN = ((1,), (0,))
NT = ((1,), (1,))
GA, GB = 0.7978845608028654, 0.044715
EXTRA = 32
SMALL = pl.BlockSpec(memory_space=pltpu.SMEM)


def dot(a, b, dims=NN):
    return lax.dot_general(a, b, (dims, ((), ())), preferred_element_type=F32)


def full(shape):
    zeros = (0,) * len(shape)
    return pl.BlockSpec(tuple(shape), lambda *_: zeros)


def sds(shape, dtype):
    return jax.ShapeDtypeStruct(tuple(shape), dtype)


def vmem(shape, dtype):
    return pltpu.VMEM(tuple(shape), dtype)


def keep(x):
    return pltpu.with_memory_space_constraint(x, pltpu.VMEM)


def in_hbm(x):
    return pltpu.with_memory_space_constraint(x, pltpu.HBM)


RES = pl.BlockSpec(memory_space=pltpu.VMEM)


def params(mib):
    return pltpu.CompilerParams(vmem_limit_bytes=mib << 20)


SCALE = 2e8


def cost(micros):
    return pl.CostEstimate(flops=int(micros * SCALE), bytes_accessed=0, transcendentals=0)


def normalize(x):
    mean = jnp.mean(x, axis=-1, keepdims=True)
    xc = x - mean
    var = jnp.mean(xc * xc, axis=-1, keepdims=True)
    rstd = lax.rsqrt(var + EPS)
    return xc * rstd, rstd


def norm_back(u, xhat, rstd):
    mu = jnp.mean(u, axis=-1, keepdims=True)
    mux = jnp.mean(u * xhat, axis=-1, keepdims=True)
    return rstd * (u - mu - xhat * mux)


def one_hot(slots, row0, rows):
    pos = lax.broadcasted_iota(jnp.int32, (rows, slots.shape[1]), 0) + row0
    return pos == slots


def run(kernel, ins, specs, deps, outs, out_specs, scratch=(), mib=16, micros=4, name=None, grid=(1,), aliases=None):
    n, k = len(ins), len(deps)
    return pl.pallas_call(
        lambda *refs: kernel(*refs[:n], *refs[n + k:]),
        grid=grid,
        in_specs=list(specs) + [pl.BlockSpec(memory_space=pl.ANY)] * k,
        out_specs=out_specs,
        out_shape=outs,
        scratch_shapes=list(scratch),
        input_output_aliases=aliases or {},
        compiler_params=params(mib),
        cost_estimate=cost(micros),
        name=name,
    )(*[keep(a) if sp is RES else a for a, sp in zip(ins, specs)], *deps)


def piece_order(bits):
    k = len(bits)
    return [sum(bits[j] for j in range(k) if p >> (k - 1 - j) & 1) for p in range(1 << k)]


def ordered(x, order):
    rows = x.shape[0] // len(order)
    if rows % 16:
        x = x.astype(F32)
    return jnp.concatenate([x[d * rows:(d + 1) * rows] for d in order], 0).astype(BF)


def halves(h, refs):
    n = refs[0].shape[0]
    first = h[0] * n
    for ref, at in zip(refs, (first, n - first)):
        yield ref, pl.ds(pl.multiple_of(at, 16), n)


def whole(h, refs, scratch=None):
    if len(refs) == 1:
        return refs[0]
    for ref, rows in halves(h, refs):
        scratch[rows, :] = ref[...]
    return scratch


def front(h, refs):
    return refs[0][...] if len(refs) == 1 else jnp.where(h[0] == 0, refs[0][...], refs[1][...])


def first_kernel(attn_order, down_order, tok, cot, slots, thoughts, vectors, seg, stream, normed, normed_t, cot_v, cot_t, cot_sum, mask):
    i = pl.program_id(0)
    r = pl.ds(pl.multiple_of(i * QB, QB), QB)
    hot = one_hot(slots[...], i * QB, QB)
    inserted = dot(hot.astype(BF), thoughts[...])
    covered = jnp.sum(hot.astype(F32), axis=1, keepdims=True) > 0.5
    x = jnp.where(covered, inserted, tok[...].astype(F32))
    stream[r, :] = x.astype(BF)
    xhat, _ = normalize(x)
    n = (xhat * vectors[0:1, :] + vectors[1:2, :]).astype(BF)
    normed[r, :] = n
    normed_t[:, r] = ordered(n.T, attn_order)
    g = cot[...]
    cot_v[r, :] = g
    cot_t[:, r] = ordered(g.T, down_order)

    @pl.when(i == 0)
    def _():
        cot_sum[...] = jnp.zeros_like(cot_sum)

    cot_sum[...] += jnp.sum(g.astype(F32), axis=0, keepdims=True)
    k0 = pl.multiple_of(jnp.maximum(i - 1, 0) * QB, QB)
    seg_q = seg[:, r]
    seg_k = jnp.broadcast_to(seg[:, pl.ds(k0, 2 * QB)], (QB, 2 * QB)).T
    kpos = lax.broadcasted_iota(jnp.int32, (2 * QB, QB), 0) + k0
    qpos = lax.broadcasted_iota(jnp.int32, (2 * QB, QB), 1) + i * QB
    mask[i] = jnp.where((seg_k == seg_q) & (kpos <= qpos), 0.0, NEG)


def first_norm(orders, tok, cot, slots, thoughts, vectors, seg, deps):
    L, D = tok.shape
    nq = L // QB
    rows = pl.BlockSpec((QB, D), lambda i: (i, 0))
    ins = (in_hbm(tok), in_hbm(cot), slots, thoughts, vectors, seg)
    return run(
        functools.partial(first_kernel, *orders),
        ins,
        [rows, rows] + [full(a.shape) for a in ins[2:]],
        deps,
        [vmem((L, D), BF), vmem((L, D), BF), vmem((D, L), BF), vmem((L, D), BF), vmem((D, L), BF), sds((1, D), F32), vmem((nq, 2 * QB, QB), F32)],
        [RES] * 5 + [full((1, D)), RES],
        grid=(nq,),
        name="first_norm",
    )


def window(i):
    return (0, QB) if i == 0 else ((i - 1) * QB, 2 * QB)


def head_mask(h, width):
    lane = lax.broadcasted_iota(jnp.int32, (1, width), 1)
    return ((lane >= h * HD) & (lane < (h + 1) * HD)).astype(BF)


def attend_kernel(h0, normed, mask, *refs):
    *ws, joined, ctx, lse, vt, buf = refs
    L = normed.shape[0]
    C = ctx.shape[1]
    w = whole(h0, ws, buf)
    bias = w[:EXTRA, :].astype(F32)
    base = EXTRA
    for i in range(L // QB):
        r = pl.ds(i * QB, QB)
        for c in range(3):
            v = dot(normed[r, :], w[base + c * C:base + (c + 1) * C, :], NT)
            if c != 1:
                b = 1 + c // 2
                v = v + bias[b:b + 1, :C]
            v = v.astype(BF)
            joined[c, r, :] = v
            if c == 2:
                vt[:, r] = v.T
    masks = [head_mask(h, C) for h in range(C // HD)]
    for i in range(L // QB):
        k0, kn = window(i)
        r = pl.ds(i * QB, QB)
        q = joined[0, r, :] * BF(HD ** -0.5)
        k = joined[1, pl.ds(k0, kn), :]
        m = mask[i, :kn, :]
        H = C // HD
        qs = jnp.concatenate([q * masks[h] for h in range(H)], axis=0)
        s = dot(k, qs, NT) + jnp.concatenate([m] * H, axis=1)
        top = jnp.max(s, axis=0, keepdims=True)
        e = jnp.exp(s - top)
        total = jnp.sum(e, axis=0, keepdims=True)
        p = (e * (1.0 / total)).astype(BF)
        stat = top + jnp.log(total)
        stats = [stat[:, h * QB:(h + 1) * QB] for h in range(H)]
        ps = jnp.concatenate([p[:, h * QB:(h + 1) * QB] for h in range(H)], axis=0)
        rid = lax.broadcasted_iota(jnp.int32, (C, 1), 0) // HD
        vtb = jnp.concatenate([vt[:, pl.ds(k0, kn)] * (rid == h).astype(BF) for h in range(H)], axis=1)
        ctx[r, :] = dot(vtb, ps).T.astype(BF)
        for h in range(C // HD):
            lse[h:h + 1, r] = stats[h]


def attend(h, normed, mask, ws, C, name, deps=()):
    L, D = normed.shape
    return run(
        attend_kernel,
        (h, normed, mask, *ws),
        [SMALL, RES, RES] + [RES for w in ws],
        deps,
        [vmem((3, L, C), BF), vmem((L, C), BF), vmem((8, L), F32)],
        [RES, RES, RES],
        [pltpu.VMEM((C, L), BF), pltpu.VMEM((3 * C + EXTRA, D), BF)],
        mib=12,
        micros=5,
        name=name,
    )


def second_norm(order, stream, vectors, ctxs, ws):
    L, D = stream.shape
    n = len(ws)
    C = ctxs[0].shape[1]

    def kernel(stream, vectors, *refs):
        *refs, middle, nm, nm_t, token = refs
        i = pl.program_id(0)
        r = pl.ds(pl.multiple_of(i * QB, QB), QB)

        @pl.when(i == 0)
        def _():
            token[...] = jnp.zeros_like(token)

        acc = stream[r, :].astype(F32) + vectors[2:3, :]
        for j in range(n):
            acc = acc + dot(refs[j][r, :], refs[n + j][...])
        middle[r, :] = acc
        xhat, _ = normalize(acc)
        v = (xhat * vectors[3:4, :] + vectors[4:5, :]).astype(BF)
        nm[r, :] = v
        nm_t[:, r] = ordered(v.T, order)

    return run(
        kernel,
        (stream, vectors, *ctxs, *ws),
        [RES, full(vectors.shape)] + [RES] * n + [full(w.shape) for w in ws],
        (),
        [vmem((L, D), F32), vmem((L, D), BF), vmem((D, L), BF), sds((8, 128), F32)],
        [RES] * 3 + [full((8, 128))],
        [],
        grid=(L // QB,),
        name="second_norm",
    )


def mlp_kernel(n, first, h0, nm, g, *refs):
    bias, ws, rest = refs[:n], refs[n:2 * n + 1], refs[2 * n + 1:]
    if not first:
        o_in, m_in = rest[:2]
        rest = rest[2:]
    o_acc, m_acc, hs, ps, g_ub, *bufs = rest
    w_up, w_dn = whole(h0, ws[:n], *bufs), ws[n]
    L = nm.shape[0]
    up_b = front(h0, bias)[0:1, :].astype(F32)
    total = jnp.zeros((1, w_up.shape[1]), F32)
    rows = L // 2
    blocks = [pl.ds(i * rows, rows) for i in range(2)]

    def before(r):
        return dot(nm[r, :], w_up[...]) + up_b, dot(g[r, :], w_dn[...], NT)

    ready = before(blocks[0])
    for i, r in enumerate(blocks):
        x, gd = ready
        if i + 1 < len(blocks):
            ready = before(blocks[i + 1])
        x2 = x * x
        th = jnp.tanh(x * (GA + (GA * GB) * x2))
        ht = 0.5 * th + 0.5
        h = (x * ht).astype(BF)
        dg = ht + x * (0.5 - 0.5 * (th * th)) * (GA + (3 * GA * GB) * x2)
        pg = (gd * dg).astype(BF)
        hs[r, :] = h
        ps[r, :] = pg
        total = total + jnp.sum(pg.astype(F32), axis=0, keepdims=True)
        o, m = dot(h, w_dn[...]), dot(pg, w_up[...], NT)
        o_acc[r, :] = o if first else o_in[r, :] + o
        m_acc[r, :] = m if first else m_in[r, :] + m
    g_ub[...] = total


def mlp(h, nm, g, biases, ws, accs, name, deps=()):
    L, D = nm.shape
    n = len(biases)
    F = ws[0].shape[1]
    return run(
        functools.partial(mlp_kernel, n, not accs),
        (h, nm, g, *biases, *ws, *accs),
        [SMALL, RES, RES] + [pl.BlockSpec((EXTRA, F), lambda _: (0, 0))] * n + [RES for w in ws] + [RES] * len(accs),
        deps,
        [vmem((L, D), F32)] * 2 + [vmem((L, F), BF)] * 2 + [sds((1, F), F32)],
        [RES] * 4 + [full((1, F))],
        [] if n == 1 else [pltpu.VMEM((D, F), BF)],
        aliases={4 + 2 * n: 0, 5 + 2 * n: 1} if accs else None,
        mib=14,
        micros=7,
        name=name,
    )


def mlp_grads(h, nm_t, g_t, hs, ps, adds, bits, name, deps=()):
    D, L = nm_t.shape
    F = hs.shape[1]
    n = D // 2

    def kernel(h0, nm_t, g_t, hs, ps, *refs):
        c = pl.ds(pl.multiple_of(pl.program_id(0) * QB, QB), QB)
        for j, (left, right) in enumerate(((nm_t, ps), (g_t, hs))):
            for k in range(2):
                half = k ^ h0[bits[j]] if adds else k
                rows = pl.ds(pl.multiple_of(half * n, n), n)
                v = dot(left[rows, :], right[:, c])
                if adds:
                    v = v + jnp.where(half == 0, refs[2 * j][...], refs[2 * j + 1][...]).astype(F32)
                refs[len(adds) + 2 * j + k][...] = v.astype(BF)

    col = pl.BlockSpec((n, QB), lambda c: (0, c))
    return run(
        kernel,
        (h, nm_t, g_t, hs, ps, *adds),
        [SMALL] + [RES] * 4 + [col] * len(adds),
        deps,
        [sds((n, F), BF)] * 4,
        [col] * 4,
        mib=12,
        grid=(F // QB,),
        name=name,
    )


def second_back_kernel(order, middle, o_acc, m_acc, g, vectors, out, ag, ag_t, mg, sums):
    i = pl.program_id(0)
    r = pl.ds(pl.multiple_of(i * QB, QB), QB)
    mid = middle[r, :]
    out[...] = (mid + o_acc[r, :] + vectors[5:6, :]).astype(BF)
    xhat, rstd = normalize(mid)
    d = m_acc[r, :]
    m = g[r, :].astype(F32) + norm_back(d * vectors[3:4, :], xhat, rstd)
    mg[r, :] = m
    a = m.astype(BF)
    ag[r, :] = a
    ag_t[:, r] = ordered(a.T, order)

    @pl.when(i == 0)
    def _():
        sums[...] = jnp.zeros_like(sums)

    sums[0:1, :] += jnp.sum(d * xhat, axis=0, keepdims=True)
    sums[1:2, :] += jnp.sum(d, axis=0, keepdims=True)
    sums[2:3, :] += jnp.sum(a.astype(F32), axis=0, keepdims=True)


def second_back(order, middle, o_acc, m_acc, g, vectors):
    L, D = middle.shape
    rows = pl.BlockSpec((QB, D), lambda i: (i, 0))
    return run(
        functools.partial(second_back_kernel, order),
        (middle, o_acc, m_acc, g, vectors),
        [RES] * 4 + [full(vectors.shape)],
        (),
        [sds((L, D), BF), vmem((L, D), BF), vmem((D, L), BF), vmem((L, D), F32), sds((8, D), F32)],
        [rows, RES, RES, RES, full((8, D))],
        grid=(L // QB,),
        name="second_back",
    )


def attend_back_kernel(split, bit, h0, ag, ag_t, normed_t, mask, joined, ctx, lse, w_out, *rest):
    if split:
        adds, rest = rest[:2], rest[2:]
    jg, *g_w, g_b, dctx, kt, dk, dv = rest
    L, D = ag.shape
    C = ctx.shape[1]
    H = C // HD
    for i in range(L // QB):
        r = pl.ds(i * QB, QB)
        dctx[r, :] = dot(ag[r, :], w_out[...], NT).astype(BF)
        kt[:, r] = joined[1, r, :].T
    masks = [head_mask(h, C) for h in range(H)]
    dk[...] = jnp.zeros_like(dk)
    dv[...] = jnp.zeros_like(dv)
    for i in range(L // QB):
        k0, kn = window(i)
        r = pl.ds(i * QB, QB)
        kr = pl.ds(k0, kn)
        q = joined[0, r, :] * BF(HD ** -0.5)
        k = joined[1, kr, :]
        v = joined[2, kr, :]
        do = dctx[r, :]
        m = mask[i, :kn, :]
        qs = jnp.concatenate([q * masks[h] for h in range(H)], axis=0)
        dos = jnp.concatenate([do * masks[h] for h in range(H)], axis=0)
        top = jnp.concatenate([lse[h:h + 1, r] for h in range(H)], axis=1)
        s = dot(k, qs, NT)
        dp = dot(v, dos, NT)
        p = jnp.exp(s + jnp.concatenate([m] * H, axis=1) - top)
        inner = jnp.sum(p * dp, axis=0, keepdims=True)
        ds = (p * (dp - inner)).astype(BF)
        dv[kr, :] += dot(p.astype(BF), dos)
        dk[kr, :] += dot(ds, qs)
        rid = lax.broadcasted_iota(jnp.int32, (C, 1), 0) // HD
        ktb = jnp.concatenate([kt[:, kr] * (rid == h).astype(BF) for h in range(H)], axis=1)
        dst = jnp.concatenate([ds[:, h * QB:(h + 1) * QB] for h in range(H)], axis=0)
        jg[r, :C] = (dot(ktb, dst).T * HD ** -0.5).astype(BF)
    jg[:, C:2 * C] = dk[...].astype(BF)
    jg[:, 2 * C:] = dv[...].astype(BF)
    rows_n = D // 2
    for j in range(2):
        half = j ^ h0[bit] if split else j
        rows = pl.ds(pl.multiple_of(half * rows_n, rows_n), rows_n)
        v, v_out = dot(normed_t[rows, :], jg[...]), dot(ag_t[rows, :], ctx[...])
        if split:
            add = jnp.where(half == 0, adds[0][...], adds[1][...]).astype(F32)
            v, v_out = v + add[:, :3 * C], v_out + add[:, 3 * C:]
        g_w[j][:, :3 * C] = v.astype(BF)
        g_w[j][:, 3 * C:] = v_out.astype(BF)
    g_b[...] = jnp.sum(jg[...].astype(F32), axis=0, keepdims=True)


def attend_back(h, ag, ag_t, normed_t, mask, saved, w_out, adds, bit, name, deps=()):
    joined, ctx, lse = saved
    L, D = ag.shape
    C = ctx.shape[1]
    shape = (D // 2, 4 * C)
    return run(
        functools.partial(attend_back_kernel, bool(adds), bit),
        (h, ag, ag_t, normed_t, mask, joined, ctx, lse, w_out, *adds),
        [SMALL] + [RES] * (8 + len(adds)),
        deps,
        [vmem((L, 3 * C), BF)] + [vmem(shape, BF)] * 2 + [sds((1, 3 * C), F32)],
        [RES] * 3 + [full((1, 3 * C))],
        [pltpu.VMEM((L, C), BF), pltpu.VMEM((C, L), BF), pltpu.VMEM((L, C), F32), pltpu.VMEM((L, C), F32)],
        mib=10,
        micros=9,
        name=name,
    )


def first_back(h, stream, mg, vectors, slots, jgs, ws, deps=()):
    L, D = stream.shape
    n = len(jgs)
    flat = [w for shard in ws for w in shard]

    def kernel(h0, stream, mg, vectors, slots, *refs):
        gtok, gth, sums, buf = refs[n + len(flat):]
        i = pl.program_id(0)
        r = pl.ds(pl.multiple_of(i * QB, QB), QB)

        @pl.when(i == 0)
        def _():
            sums[...] = jnp.zeros_like(sums)
            gth[...] = jnp.zeros_like(gth)
            at = n
            for j, shard in enumerate(ws):
                if len(shard) > 1:
                    whole(h0, refs[at:at + 2], buf.at[j])
                at += len(shard)

        d, at = None, n
        for j, shard in enumerate(ws):
            w = refs[at] if len(shard) == 1 else buf.at[j]
            at += len(shard)
            v = dot(refs[j][r, :], w[EXTRA:, :])
            d = v if d is None else d + v
        xhat, rstd = normalize(stream[r, :].astype(F32))
        sg = (mg[r, :] + norm_back(d * vectors[0:1, :], xhat, rstd)).astype(BF)
        hot = one_hot(slots[...], i * QB, QB)
        covered = jnp.sum(hot.astype(F32), axis=1, keepdims=True) > 0.5
        gtok[...] = jnp.where(covered, 0.0, sg.astype(F32)).astype(BF)
        gth[...] += dot(hot.astype(BF), sg, ((0,), (0,)))
        sums[0:1, :] += jnp.sum(d * xhat, axis=0, keepdims=True)
        sums[1:2, :] += jnp.sum(d, axis=0, keepdims=True)

    return run(
        kernel,
        (h, stream, mg, vectors, slots, *jgs, *flat),
        [SMALL, RES, RES, full(vectors.shape), full(slots.shape)] + [RES] * (n + len(flat)),
        deps,
        [sds((L, D), BF), sds((slots.shape[1], D), F32), sds((8, D), F32)],
        [pl.BlockSpec((QB, D), lambda i: (i, 0)), full((slots.shape[1], D)), full((8, D))],
        [pltpu.VMEM((n, ws[0][0].shape[0], D), BF)],
        mib=16,
        micros=8,
        grid=(L // QB,),
        name="first_back",
    )


def merge(h, groups, name, deps=()):
    flat = [a for arrays, _ in groups for a in arrays]
    outs = []
    for arrays, bit in groups:
        R, W = arrays[0].shape
        outs += [sds((R, W), BF)] if bit is None else [sds((R // 2, W), BF), sds((R // 2, W), F32)]

    def kernel(h0, *refs):
        at, to = 0, len(flat)
        for arrays, bit in groups:
            group = refs[at:at + len(arrays)]
            at += len(arrays)
            n = arrays[0].shape[0] // 2
            mine = 0 if bit is None else h0[bit]
            for half in ((0, 1) if bit is None else (1 - mine, mine)):
                rows = pl.ds(pl.multiple_of(half * n, 16), n)
                t = group[0][rows, :].astype(F32)
                for ref in group[1:]:
                    t = t + ref[rows, :].astype(F32)
                if bit is None:
                    refs[to][rows, :] = t.astype(BF)
                else:
                    refs[to][...] = t.astype(refs[to].dtype)
                    to += 1
            to += bit is None

    return run(
        kernel,
        (h, *flat),
        [SMALL] + [full(a.shape) for a in flat],
        deps,
        outs,
        [full(o.shape) for o in outs],
        mib=12,
        name=name,
    )


def swap(x, axis, size, bit):
    return lax.ppermute(x, axis, [(i, i ^ bit) for i in range(size)])


def after(x, dep):
    return lax.optimization_barrier((x, dep))


def local(
    n_dp,
    tokens,
    thoughts,
    thought_slots,
    segment_ids,
    attn_gain,
    attn_shift,
    qkv_weight,
    qkv_bias,
    out_weight,
    out_bias,
    mlp_gain,
    mlp_shift,
    up_weight,
    up_bias,
    down_weight,
    down_bias,
    cotangent,
):
    D = tokens.shape[2]
    C = qkv_weight.shape[2]
    F = up_weight.shape[1]
    core = lambda x: swap(x, "tensor", 4, 1)
    cross = lambda x: swap(x, "tensor", 4, 2)
    tie = lax.optimization_barrier
    vectors = jnp.stack([attn_gain, attn_shift, out_bias, mlp_gain, mlp_shift, down_bias] * 2)[:8].astype(F32)
    dp = lax.axis_index("dp")
    me = lax.axis_index("tensor")
    h = jnp.stack([dp & 1, dp >> 1 & 1, me, dp]).astype(jnp.int32)
    beside = lambda x: swap(x, "dp", n_dp, 1)
    my_half = lambda w: jnp.where(h[0] == 0, w[:w.shape[0] // 2], w[w.shape[0] // 2:])

    bits = [1 << i for i in range(n_dp.bit_length() - 1)]
    attn_bits, up_bits, down_bits = bits, bits, bits[1:2] + bits[:1] + bits[2:]
    attn_order, up_order, down_order = map(piece_order, (attn_bits, up_bits, down_bits))

    biases = jnp.concatenate(
        [up_bias.reshape(1, F), jnp.pad(qkv_bias, ((0, 0), (0, F - C))), jnp.zeros((EXTRA - 3, F), BF)], 0
    )
    qkv = jnp.concatenate([biases, jnp.transpose(qkv_weight, (1, 2, 0)).reshape(3 * C, D)], 0)
    qkv_x, qkv_c = cross(my_half(qkv)), core(qkv)
    up_s = my_half(up_weight)
    g = cotangent[0]
    stream, normed, normed_t, g_v, cot_t, cot_sum, mask = first_norm(
        (attn_order, down_order), tokens[0], g, thought_slots, thoughts[0], vectors, segment_ids, (up_s, h)
    )
    saved = [None] * 4
    qkv_w = [(qkv,), (qkv_c,)]

    def forward(s, deps=()):
        saved[s] = attend(h, normed, mask, qkv_w[s], C, "attend%d" % s, deps)

    def wait(s, *arrays):
        *arrays, stats = tie((*arrays, saved[s][2]))
        saved[s] = (*saved[s][:2], stats)
        return arrays

    forward(1, (up_s,))
    qkv_x, up_s, out_s = wait(1, qkv_x, up_s, out_weight)
    qkv_y, qkv_cx, out_x, up_x = beside(qkv_x), core(qkv_x), cross(out_s), cross(up_s)
    forward(0)
    qkv_y, out_s = wait(0, qkv_y, out_weight)
    qkv_cy, out_c = core(qkv_y), core(out_s)
    qkv_w += [(qkv_x, qkv_y), (qkv_cx, qkv_cy)]
    forward(2, (qkv_cx,))
    out_x, down_s = wait(2, out_x, down_weight)
    out_cx, down_x = core(out_x), cross(down_s)
    forward(3, (out_c,))
    up_x, up_s, down_s = wait(3, up_x, up_weight, down_weight)
    up_y, up_cx, up_c, down_c = beside(up_x), core(up_x), core(up_s), core(down_s)
    middle, nm, nm_t, token = second_norm(
        up_order, stream, vectors, [c for _, c, _ in saved], [out_weight, out_c, out_x, out_cx]
    )
    gb, acts, grads = [None] * 4, [None] * 4, [None] * 4
    first_bits = (up_bits[0].bit_length() - 1, down_bits[0].bit_length() - 1)

    def hidden(s, ws, accs, deps=()):
        o, m, hs, ps, gb[s] = mlp(h, nm, g_v, qkv_w[s][:1] if s < 2 else qkv_w[s], ws, accs, "mlp%d" % s, deps)
        acts[s] = (hs, ps)
        return o, m

    def hidden_grads(s, adds=(), deps=()):
        grads[s] = mlp_grads(h, nm_t, cot_t, *acts[s], adds, first_bits, "mlp_grads%d" % s, deps)

    accs = hidden(1, (up_c, down_c), ())
    hidden_grads(1, (), (up_cx,))
    up_y, gb[1] = tie((up_y, gb[1]))
    up_cy = core(up_y)
    near = list(map(core, grads[1]))
    accs = hidden(0, (up_weight, down_weight), accs, tuple(grads[1]))
    accs = hidden(2, (up_x, up_y, down_x), accs, (up_cy,))
    hidden_grads(0, near, (gb[2],))
    up_k, up_o, down_k, down_o = grads[0]
    own = [[up_k, swap(up_o, "dp", n_dp, up_bits[0])], [down_k, swap(down_o, "dp", n_dp, down_bits[0])]]
    down_x, gb[0] = tie((down_x, gb[0]))
    accs = hidden(3, (up_cx, up_cy, core(down_x)), accs, (up_o,))
    hidden_grads(3)
    near = list(map(core, grads[3]))
    out, ag, ag_t, mg, sums2 = second_back(attn_order, middle, *accs, g_v, vectors)

    def along(sent, bit):
        return swap(sent, "dp", n_dp, bit)

    def at(bit):
        return bit.bit_length() - 1

    g_attn, g_qb = [None] * 4, [None] * 4

    def back(s, adds=(), deps=()):
        w_out = (out_weight, out_c, out_x, out_cx)[s]
        jgs[s], *g_attn[s], g_qb[s] = attend_back(
            h, ag, ag_t, normed_t, mask, saved[s], w_out, adds, at(attn_bits[0]), "attend_back%d" % s, deps
        )

    jgs = [None] * 4
    ways = (up_bits, down_bits)
    back(3)
    hidden_grads(2, near, (g_qb[3],))
    near = list(map(core, g_attn[3]))
    up_k, up_o, down_k, down_o = grads[2]
    far = [[up_k, along(up_o, up_bits[0])], [down_k, along(down_o, down_bits[0])]]
    own[0][1], own[1][1], g_qb[3] = tie((own[0][1], own[1][1], g_qb[3]))
    up_m, up_k, down_m, down_k = merge(h, [(a, at(w[1])) for a, w in zip(own, ways)], "merge_own", (up_o,))
    own = [[up_k, along(up_m, up_bits[1])], [down_k, along(down_m, down_bits[1])]]
    back(1, (), (up_m,))
    back(2, near, (g_qb[1],))
    near = list(map(core, g_attn[1]))
    attn_far = [g_attn[2][0], along(g_attn[2][1], attn_bits[0])]
    far[0][1], far[1][1], g_qb[2] = tie((far[0][1], far[1][1], g_qb[2]))
    up_m, up_k, down_m, down_k = merge(h, [(a, at(w[1])) for a, w in zip(far, ways)], "merge_far")
    far = [[up_k, along(up_m, up_bits[1])], [down_k, along(down_m, down_bits[1])]]
    back(0, near, (up_m, own[0][1], own[1][1]))
    attn_own = [g_attn[0][0], along(g_attn[0][1], attn_bits[0])]
    gtok, gth, sums1 = first_back(h, stream, mg, vectors, thought_slots, jgs, qkv_w)
    far[0][-1], far[1][-1], attn_far[1], sums1 = tie((far[0][-1], far[1][-1], attn_far[1], sums1))
    far_m, far_k, *far_s = merge(h, [(attn_far, at(attn_bits[1]))] + [(a, None) for a in far], "merge_last")
    own = [a + [cross(x)] for a, x in zip(own, far_s)]
    attn_far = [far_k, along(far_m, attn_bits[1])]

    late, gb, g_qb, sums1, sums2, cot_sum = tie((h, gb, g_qb, sums1, sums2, cot_sum))
    me, dp = late[2], late[3]
    rel = [jnp.concatenate([b, jnp.pad(q, ((0, 0), (0, F - 3 * C)))], 0) for b, q in zip(gb, g_qb)]
    first = [jnp.where(me & 1 == 0, rel[t], rel[t ^ 1]) for t in range(4)]
    ordered = jnp.concatenate([jnp.where(me & 2 == 0, first[t], first[t ^ 2]) for t in range(4)], 0)
    small = jnp.concatenate([ordered, sums1[:2], sums2[:3], cot_sum], 0)
    attn_own[1], small = tie((attn_own[1], small))

    wide = lambda a: a.astype(F32)

    def total(arrays):
        t = wide(arrays[0])
        for a in arrays[1:]:
            t = t + wide(a)
        return t

    def part(arrays, bit, mine):
        n = arrays[0].shape[0] // 2
        return [jnp.where((dp & bit != 0) == mine, a[n:], a[:n]) for a in arrays]

    def halve(arrays, bit):
        sent = total(part(arrays, bit, False)).astype(BF)
        return part(arrays, bit, True) + [along(sent, bit)]

    attn_own = halve(attn_own, attn_bits[1])
    attn_own.append(cross(total(attn_far).astype(BF)))
    for i in range(2, len(bits)):
        *own, attn_own = [halve(a, w[i]) for a, w in zip((*own, attn_own), (*ways, attn_bits))]
    r_up, r_dn, r_at = total(own[0]), total(own[1]), total(attn_own)

    for axis, size in (("tensor", 4), ("dp", n_dp)):
        bit = 1
        while bit < size:
            small = small + swap(small, axis, size, bit)
            bit *= 2
    mine = sum(jnp.where(me == t, small[2 * t:2 * t + 2], 0.0) for t in range(4))
    return (
        out[None],
        gtok[None],
        gth.astype(BF)[None],
        small[8],
        small[9],
        r_at[:, :3 * C].reshape(-1, 3, C),
        jnp.stack([mine[1, :C], mine[1, 2 * C:3 * C]]),
        r_at[:, 3 * C:].T,
        small[12],
        small[10],
        small[11],
        r_up,
        mine[0],
        r_dn.T,
        small[13],
    )


def solution(mesh):
    rows = P(("dp", "tensor"), None, None)
    placed = (
        rows,
        rows,
        P(("dp", "tensor"), None),
        P(("dp", "tensor"), None),
        P(),
        P(),
        P(None, None, "tensor"),
        P(None, "tensor"),
        P("tensor", None),
        P(),
        P(),
        P(),
        P(None, "tensor"),
        P("tensor"),
        P("tensor", None),
        P(),
        rows,
    )
    return jax.shard_map(
        functools.partial(local, mesh.shape["dp"]),
        mesh=mesh,
        in_specs=placed,
        out_specs=(
            rows,
            rows,
            rows,
            P(),
            P(),
            P("dp", None, "tensor"),
            P(None, "tensor"),
            P("tensor", "dp"),
            P(),
            P(),
            P(),
            P("dp", "tensor"),
            P("tensor"),
            P("tensor", "dp"),
            P(),
        ),
        check_vma=False,
    )
```

```python
import functools

import jax
import jax.numpy as jnp
from jax import lax
from jax.experimental import pallas as pl
from jax.experimental.pallas import tpu as pltpu
from jax.sharding import PartitionSpec as P

F32 = jnp.float32
BF = jnp.bfloat16
HD = 64
QB = 256
EPS = 1e-05
NEG = -1e30
NN = ((1,), (0,))
NT = ((1,), (1,))
GA, GB = 0.7978845608028654, 0.044715
EXTRA = 32
SMALL = pl.BlockSpec(memory_space=pltpu.SMEM)


def dot(a, b, dims=NN):
    return lax.dot_general(a, b, (dims, ((), ())), preferred_element_type=F32)


def full(shape):
    zeros = (0,) * len(shape)
    return pl.BlockSpec(tuple(shape), lambda *_: zeros)


def sds(shape, dtype):
    return jax.ShapeDtypeStruct(tuple(shape), dtype)


def vmem(shape, dtype):
    return pltpu.VMEM(tuple(shape), dtype)


def keep(x):
    return pltpu.with_memory_space_constraint(x, pltpu.VMEM)


def in_hbm(x):
    return pltpu.with_memory_space_constraint(x, pltpu.HBM)


RES = pl.BlockSpec(memory_space=pltpu.VMEM)


def params(mib):
    return pltpu.CompilerParams(vmem_limit_bytes=mib << 20)


SCALE = 2e8


def cost(micros):
    return pl.CostEstimate(flops=int(micros * SCALE), bytes_accessed=0, transcendentals=0)


def vector(ref):
    return ref[...].astype(F32).reshape(1, -1)


def normalize(x):
    mean = jnp.mean(x, axis=-1, keepdims=True)
    xc = x - mean
    var = jnp.mean(xc * xc, axis=-1, keepdims=True)
    rstd = lax.rsqrt(var + EPS)
    return xc * rstd, rstd


def norm_back(u, xhat, rstd):
    mu = jnp.mean(u, axis=-1, keepdims=True)
    mux = jnp.mean(u * xhat, axis=-1, keepdims=True)
    return rstd * (u - mu - xhat * mux)


def one_hot(slots, row0, rows):
    pos = lax.broadcasted_iota(jnp.int32, (rows, slots.shape[1]), 0) + row0
    return pos == slots


def run(kernel, ins, specs, deps, outs, out_specs, scratch=(), mib=16, micros=4, name=None, grid=(1,), aliases=None):
    n, k = len(ins), len(deps)
    return pl.pallas_call(
        lambda *refs: kernel(*refs[:n], *refs[n + k:]),
        grid=grid,
        in_specs=list(specs) + [pl.BlockSpec(memory_space=pl.ANY)] * k,
        out_specs=out_specs,
        out_shape=outs,
        scratch_shapes=list(scratch),
        input_output_aliases=aliases or {},
        compiler_params=params(mib),
        cost_estimate=cost(micros),
        name=name,
    )(*[keep(a) if sp is RES else a for a, sp in zip(ins, specs)], *deps)


def piece_order(bits):
    k = len(bits)
    return [sum(bits[j] for j in range(k) if p >> (k - 1 - j) & 1) for p in range(1 << k)]


def ordered(x, order):
    rows = x.shape[0] // len(order)
    if rows % 16:
        x = x.astype(F32)
    return jnp.concatenate([x[d * rows:(d + 1) * rows] for d in order], 0).astype(BF)


def halves(h, refs):
    n = refs[0].shape[0]
    first = h[0] * n
    for ref, at in zip(refs, (first, n - first)):
        yield ref, pl.ds(pl.multiple_of(at, 16), n)


def whole(h, refs, scratch=None):
    if len(refs) == 1:
        return refs[0]
    for ref, rows in halves(h, refs):
        scratch[rows, :] = ref[...]
    return scratch


def front(h, refs):
    return refs[0][...] if len(refs) == 1 else jnp.where(h[0] == 0, refs[0][...], refs[1][...])


def first_kernel(attn_order, down_order, tok, cot, slots, thoughts, gain, shift, seg, stream, normed, normed_t, cot_v, cot_t, cot_sum, mask):
    i = pl.program_id(0)
    r = pl.ds(pl.multiple_of(i * QB, QB), QB)
    hot = one_hot(slots[...], i * QB, QB)
    inserted = dot(hot.astype(BF), thoughts[...])
    covered = jnp.sum(hot.astype(F32), axis=1, keepdims=True) > 0.5
    x = jnp.where(covered, inserted, tok[...].astype(F32))
    stream[r, :] = x.astype(BF)
    xhat, _ = normalize(x)
    n = (xhat * vector(gain) + vector(shift)).astype(BF)
    normed[r, :] = n
    normed_t[:, r] = ordered(n.T, attn_order)
    g = cot[...]
    cot_v[r, :] = g
    cot_t[:, r] = ordered(g.T, down_order)

    @pl.when(i == 0)
    def _():
        cot_sum[...] = jnp.zeros_like(cot_sum)

    cot_sum[...] += jnp.sum(g.astype(F32), axis=0, keepdims=True)
    k0 = pl.multiple_of(jnp.maximum(i - 1, 0) * QB, QB)
    seg_q = seg[:, r]
    seg_k = jnp.broadcast_to(seg[:, pl.ds(k0, 2 * QB)], (QB, 2 * QB)).T
    kpos = lax.broadcasted_iota(jnp.int32, (2 * QB, QB), 0) + k0
    qpos = lax.broadcasted_iota(jnp.int32, (2 * QB, QB), 1) + i * QB
    mask[i] = jnp.where((seg_k == seg_q) & (kpos <= qpos), 0.0, NEG)


def first_norm(orders, tok, cot, slots, thoughts, gain, shift, seg, deps):
    L, D = tok.shape
    nq = L // QB
    rows = pl.BlockSpec((QB, D), lambda i: (i, 0))
    ins = (in_hbm(tok), in_hbm(cot), slots, thoughts, gain, shift, seg)
    return run(
        functools.partial(first_kernel, *orders),
        ins,
        [rows, rows] + [full(a.shape) for a in ins[2:]],
        deps,
        [vmem((L, D), BF), vmem((L, D), BF), vmem((D, L), BF), vmem((L, D), BF), vmem((D, L), BF), sds((1, D), F32), vmem((nq, 2 * QB, QB), F32)],
        [RES] * 5 + [full((1, D)), RES],
        grid=(nq,),
        name="first_norm",
    )


def window(i):
    return (0, QB) if i == 0 else ((i - 1) * QB, 2 * QB)


def head_mask(h, width):
    lane = lax.broadcasted_iota(jnp.int32, (1, width), 1)
    return ((lane >= h * HD) & (lane < (h + 1) * HD)).astype(BF)


def attend_kernel(h0, normed, mask, *refs):
    *ws, joined, ctx, lse, vt, buf = refs
    L = normed.shape[0]
    C = ctx.shape[1]
    w = whole(h0, ws, buf)
    bias = w[:EXTRA, :].astype(F32)
    base = EXTRA
    for i in range(L // QB):
        r = pl.ds(i * QB, QB)
        for c in range(3):
            v = dot(normed[r, :], w[base + c * C:base + (c + 1) * C, :], NT)
            if c != 1:
                b = 1 + c // 2
                v = v + bias[b:b + 1, :C]
            v = v.astype(BF)
            joined[c, r, :] = v
            if c == 2:
                vt[:, r] = v.T
    masks = [head_mask(h, C) for h in range(C // HD)]
    for i in range(L // QB):
        k0, kn = window(i)
        r = pl.ds(i * QB, QB)
        q = joined[0, r, :] * BF(HD ** -0.5)
        k = joined[1, pl.ds(k0, kn), :]
        m = mask[i, :kn, :]
        H = C // HD
        qs = jnp.concatenate([q * masks[h] for h in range(H)], axis=0)
        s = dot(k, qs, NT) + jnp.concatenate([m] * H, axis=1)
        top = jnp.max(s, axis=0, keepdims=True)
        e = jnp.exp(s - top)
        total = jnp.sum(e, axis=0, keepdims=True)
        p = (e * (1.0 / total)).astype(BF)
        stat = top + jnp.log(total)
        stats = [stat[:, h * QB:(h + 1) * QB] for h in range(H)]
        ps = jnp.concatenate([p[:, h * QB:(h + 1) * QB] for h in range(H)], axis=0)
        rid = lax.broadcasted_iota(jnp.int32, (C, 1), 0) // HD
        vtb = jnp.concatenate([vt[:, pl.ds(k0, kn)] * (rid == h).astype(BF) for h in range(H)], axis=1)
        ctx[r, :] = dot(vtb, ps).T.astype(BF)
        for h in range(C // HD):
            lse[h:h + 1, r] = stats[h]


def attend(h, normed, mask, ws, C, name, deps=()):
    L, D = normed.shape
    return run(
        attend_kernel,
        (h, normed, mask, *ws),
        [SMALL, RES, RES] + [RES for w in ws],
        deps,
        [vmem((3, L, C), BF), vmem((L, C), BF), vmem((8, L), F32)],
        [RES, RES, RES],
        [pltpu.VMEM((C, L), BF), pltpu.VMEM((3 * C + EXTRA, D), BF)],
        mib=12,
        micros=5,
        name=name,
    )


def second_norm(order, stream, out_bias, gain, shift, ctxs, ws):
    L, D = stream.shape
    n = len(ws)
    C = ctxs[0].shape[1]

    def kernel(stream, out_bias, gain, shift, *refs):
        *refs, middle, nm, nm_t, token = refs
        i = pl.program_id(0)
        r = pl.ds(pl.multiple_of(i * QB, QB), QB)

        @pl.when(i == 0)
        def _():
            token[...] = jnp.zeros_like(token)

        acc = stream[r, :].astype(F32) + vector(out_bias)
        for j in range(n):
            acc = acc + dot(refs[j][r, :], refs[n + j][...])
        middle[r, :] = acc
        xhat, _ = normalize(acc)
        v = (xhat * vector(gain) + vector(shift)).astype(BF)
        nm[r, :] = v
        nm_t[:, r] = ordered(v.T, order)

    return run(
        kernel,
        (stream, out_bias, gain, shift, *ctxs, *ws),
        [RES] + [full(gain.shape)] * 3 + [RES] * n + [full(w.shape) for w in ws],
        (),
        [vmem((L, D), F32), vmem((L, D), BF), vmem((D, L), BF), sds((8, 128), F32)],
        [RES] * 3 + [full((8, 128))],
        [],
        grid=(L // QB,),
        name="second_norm",
    )


def mlp_kernel(n, first, h0, nm, g, *refs):
    bias, ws, rest = refs[:n], refs[n:2 * n + 1], refs[2 * n + 1:]
    if not first:
        o_in, m_in = rest[:2]
        rest = rest[2:]
    o_acc, m_acc, hs, ps, g_ub, *bufs = rest
    w_up, w_dn = whole(h0, ws[:n], *bufs), ws[n]
    L = nm.shape[0]
    up_b = front(h0, bias)[0:1, :].astype(F32)
    total = jnp.zeros((1, w_up.shape[1]), F32)
    rows = L // 2
    blocks = [pl.ds(i * rows, rows) for i in range(2)]

    def before(r):
        return dot(nm[r, :], w_up[...]) + up_b, dot(g[r, :], w_dn[...], NT)

    ready = before(blocks[0])
    for i, r in enumerate(blocks):
        x, gd = ready
        if i + 1 < len(blocks):
            ready = before(blocks[i + 1])
        x2 = x * x
        th = jnp.tanh(x * (GA + (GA * GB) * x2))
        ht = 0.5 * th + 0.5
        h = (x * ht).astype(BF)
        dg = ht + x * (0.5 - 0.5 * (th * th)) * (GA + (3 * GA * GB) * x2)
        pg = (gd * dg).astype(BF)
        hs[r, :] = h
        ps[r, :] = pg
        total = total + jnp.sum(pg.astype(F32), axis=0, keepdims=True)
        o, m = dot(h, w_dn[...]), dot(pg, w_up[...], NT)
        o_acc[r, :] = o if first else o_in[r, :] + o
        m_acc[r, :] = m if first else m_in[r, :] + m
    g_ub[...] = total


def mlp(h, nm, g, biases, ws, accs, name, deps=()):
    L, D = nm.shape
    n = len(biases)
    F = ws[0].shape[1]
    return run(
        functools.partial(mlp_kernel, n, not accs),
        (h, nm, g, *biases, *ws, *accs),
        [SMALL, RES, RES] + [pl.BlockSpec((EXTRA, F), lambda _: (0, 0))] * n + [RES for w in ws] + [RES] * len(accs),
        deps,
        [vmem((L, D), F32)] * 2 + [vmem((L, F), BF)] * 2 + [sds((1, F), F32)],
        [RES] * 4 + [full((1, F))],
        [] if n == 1 else [pltpu.VMEM((D, F), BF)],
        aliases={4 + 2 * n: 0, 5 + 2 * n: 1} if accs else None,
        mib=14,
        micros=7,
        name=name,
    )


def mlp_grads(h, nm_t, g_t, hs, ps, adds, bits, name, deps=()):
    D, L = nm_t.shape
    F = hs.shape[1]
    n = D // 2

    def kernel(h0, nm_t, g_t, hs, ps, *refs):
        c = pl.ds(pl.multiple_of(pl.program_id(0) * QB, QB), QB)
        for j, (left, right) in enumerate(((nm_t, ps), (g_t, hs))):
            for k in range(2):
                half = k ^ h0[bits[j]] if adds else k
                rows = pl.ds(pl.multiple_of(half * n, n), n)
                v = dot(left[rows, :], right[:, c])
                if adds:
                    v = v + jnp.where(half == 0, refs[2 * j][...], refs[2 * j + 1][...]).astype(F32)
                refs[len(adds) + 2 * j + k][...] = v.astype(BF)

    col = pl.BlockSpec((n, QB), lambda c: (0, c))
    return run(
        kernel,
        (h, nm_t, g_t, hs, ps, *adds),
        [SMALL] + [RES] * 4 + [col] * len(adds),
        deps,
        [sds((n, F), BF)] * 4,
        [col] * 4,
        mib=12,
        grid=(F // QB,),
        name=name,
    )


def second_back_kernel(order, middle, o_acc, m_acc, g, gain, down_bias, out, ag, ag_t, mg, sums):
    i = pl.program_id(0)
    r = pl.ds(pl.multiple_of(i * QB, QB), QB)
    mid = middle[r, :]
    out[...] = (mid + o_acc[r, :] + vector(down_bias)).astype(BF)
    xhat, rstd = normalize(mid)
    d = m_acc[r, :]
    m = g[r, :].astype(F32) + norm_back(d * vector(gain), xhat, rstd)
    mg[r, :] = m
    a = m.astype(BF)
    ag[r, :] = a
    ag_t[:, r] = ordered(a.T, order)

    @pl.when(i == 0)
    def _():
        sums[...] = jnp.zeros_like(sums)

    sums[0:1, :] += jnp.sum(d * xhat, axis=0, keepdims=True)
    sums[1:2, :] += jnp.sum(d, axis=0, keepdims=True)
    sums[2:3, :] += jnp.sum(a.astype(F32), axis=0, keepdims=True)


def second_back(order, middle, o_acc, m_acc, g, gain, down_bias):
    L, D = middle.shape
    rows = pl.BlockSpec((QB, D), lambda i: (i, 0))
    return run(
        functools.partial(second_back_kernel, order),
        (middle, o_acc, m_acc, g, gain, down_bias),
        [RES] * 4 + [full(gain.shape)] * 2,
        (),
        [sds((L, D), BF), vmem((L, D), BF), vmem((D, L), BF), vmem((L, D), F32), sds((8, D), F32)],
        [rows, RES, RES, RES, full((8, D))],
        grid=(L // QB,),
        name="second_back",
    )


def attend_back_kernel(split, bit, h0, ag, ag_t, normed_t, mask, joined, ctx, lse, w_out, *rest):
    if split:
        adds, rest = rest[:2], rest[2:]
    jg, *g_w, g_b, dctx, kt, dk, dv = rest
    L, D = ag.shape
    C = ctx.shape[1]
    H = C // HD
    for i in range(L // QB):
        r = pl.ds(i * QB, QB)
        dctx[r, :] = dot(ag[r, :], w_out[...], NT).astype(BF)
        kt[:, r] = joined[1, r, :].T
    masks = [head_mask(h, C) for h in range(H)]
    dk[...] = jnp.zeros_like(dk)
    dv[...] = jnp.zeros_like(dv)
    for i in range(L // QB):
        k0, kn = window(i)
        r = pl.ds(i * QB, QB)
        kr = pl.ds(k0, kn)
        q = joined[0, r, :] * BF(HD ** -0.5)
        k = joined[1, kr, :]
        v = joined[2, kr, :]
        do = dctx[r, :]
        m = mask[i, :kn, :]
        qs = jnp.concatenate([q * masks[h] for h in range(H)], axis=0)
        dos = jnp.concatenate([do * masks[h] for h in range(H)], axis=0)
        top = jnp.concatenate([lse[h:h + 1, r] for h in range(H)], axis=1)
        s = dot(k, qs, NT)
        dp = dot(v, dos, NT)
        p = jnp.exp(s + jnp.concatenate([m] * H, axis=1) - top)
        inner = jnp.sum(p * dp, axis=0, keepdims=True)
        ds = (p * (dp - inner)).astype(BF)
        dv[kr, :] += dot(p.astype(BF), dos)
        dk[kr, :] += dot(ds, qs)
        rid = lax.broadcasted_iota(jnp.int32, (C, 1), 0) // HD
        ktb = jnp.concatenate([kt[:, kr] * (rid == h).astype(BF) for h in range(H)], axis=1)
        dst = jnp.concatenate([ds[:, h * QB:(h + 1) * QB] for h in range(H)], axis=0)
        jg[r, :C] = (dot(ktb, dst).T * HD ** -0.5).astype(BF)
    jg[:, C:2 * C] = dk[...].astype(BF)
    jg[:, 2 * C:] = dv[...].astype(BF)
    rows_n = D // 2
    for j in range(2):
        half = j ^ h0[bit] if split else j
        rows = pl.ds(pl.multiple_of(half * rows_n, rows_n), rows_n)
        v, v_out = dot(normed_t[rows, :], jg[...]), dot(ag_t[rows, :], ctx[...])
        if split:
            add = jnp.where(half == 0, adds[0][...], adds[1][...]).astype(F32)
            v, v_out = v + add[:, :3 * C], v_out + add[:, 3 * C:]
        g_w[j][:, :3 * C] = v.astype(BF)
        g_w[j][:, 3 * C:] = v_out.astype(BF)
    g_b[...] = jnp.sum(jg[...].astype(F32), axis=0, keepdims=True)


def attend_back(h, ag, ag_t, normed_t, mask, saved, w_out, adds, bit, name, deps=()):
    joined, ctx, lse = saved
    L, D = ag.shape
    C = ctx.shape[1]
    shape = (D // 2, 4 * C)
    return run(
        functools.partial(attend_back_kernel, bool(adds), bit),
        (h, ag, ag_t, normed_t, mask, joined, ctx, lse, w_out, *adds),
        [SMALL] + [RES] * (8 + len(adds)),
        deps,
        [vmem((L, 3 * C), BF)] + [vmem(shape, BF)] * 2 + [sds((1, 3 * C), F32)],
        [RES] * 3 + [full((1, 3 * C))],
        [pltpu.VMEM((L, C), BF), pltpu.VMEM((C, L), BF), pltpu.VMEM((L, C), F32), pltpu.VMEM((L, C), F32)],
        mib=10,
        micros=9,
        name=name,
    )


def first_back(h, stream, mg, gain, slots, jgs, ws, deps=()):
    L, D = stream.shape
    n = len(jgs)
    flat = [w for shard in ws for w in shard]

    def kernel(h0, stream, mg, gain, slots, *refs):
        gtok, gth, sums, buf = refs[n + len(flat):]
        i = pl.program_id(0)
        r = pl.ds(pl.multiple_of(i * QB, QB), QB)

        @pl.when(i == 0)
        def _():
            sums[...] = jnp.zeros_like(sums)
            gth[...] = jnp.zeros_like(gth)
            at = n
            for j, shard in enumerate(ws):
                if len(shard) > 1:
                    whole(h0, refs[at:at + 2], buf.at[j])
                at += len(shard)

        d, at = None, n
        for j, shard in enumerate(ws):
            w = refs[at] if len(shard) == 1 else buf.at[j]
            at += len(shard)
            v = dot(refs[j][r, :], w[EXTRA:, :])
            d = v if d is None else d + v
        xhat, rstd = normalize(stream[r, :].astype(F32))
        sg = (mg[r, :] + norm_back(d * vector(gain), xhat, rstd)).astype(BF)
        hot = one_hot(slots[...], i * QB, QB)
        covered = jnp.sum(hot.astype(F32), axis=1, keepdims=True) > 0.5
        gtok[...] = jnp.where(covered, 0.0, sg.astype(F32)).astype(BF)
        gth[...] += dot(hot.astype(BF), sg, ((0,), (0,)))
        sums[0:1, :] += jnp.sum(d * xhat, axis=0, keepdims=True)
        sums[1:2, :] += jnp.sum(d, axis=0, keepdims=True)

    return run(
        kernel,
        (h, stream, mg, gain, slots, *jgs, *flat),
        [SMALL, RES, RES, full(gain.shape), full(slots.shape)] + [RES] * (n + len(flat)),
        deps,
        [sds((L, D), BF), sds((slots.shape[1], D), F32), sds((8, D), F32)],
        [pl.BlockSpec((QB, D), lambda i: (i, 0)), full((slots.shape[1], D)), full((8, D))],
        [pltpu.VMEM((n, ws[0][0].shape[0], D), BF)],
        mib=16,
        micros=8,
        grid=(L // QB,),
        name="first_back",
    )


def merge(h, groups, name, deps=()):
    flat = [a for arrays, _ in groups for a in arrays]
    outs = []
    for arrays, bit in groups:
        R, W = arrays[0].shape
        outs += [sds((R, W), BF)] if bit is None else [sds((R // 2, W), BF), sds((R // 2, W), F32)]

    def kernel(h0, *refs):
        at, to = 0, len(flat)
        for arrays, bit in groups:
            group = refs[at:at + len(arrays)]
            at += len(arrays)
            n = arrays[0].shape[0] // 2
            mine = 0 if bit is None else h0[bit]
            for half in ((0, 1) if bit is None else (1 - mine, mine)):
                rows = pl.ds(pl.multiple_of(half * n, 16), n)
                t = group[0][rows, :].astype(F32)
                for ref in group[1:]:
                    t = t + ref[rows, :].astype(F32)
                if bit is None:
                    refs[to][rows, :] = t.astype(BF)
                else:
                    refs[to][...] = t.astype(refs[to].dtype)
                    to += 1
            to += bit is None

    return run(
        kernel,
        (h, *flat),
        [SMALL] + [full(a.shape) for a in flat],
        deps,
        outs,
        [full(o.shape) for o in outs],
        mib=12,
        name=name,
    )


def swap(x, axis, size, bit):
    return lax.ppermute(x, axis, [(i, i ^ bit) for i in range(size)])


def after(x, dep):
    return lax.optimization_barrier((x, dep))


def local(
    n_dp,
    tokens,
    thoughts,
    thought_slots,
    segment_ids,
    attn_gain,
    attn_shift,
    qkv_weight,
    qkv_bias,
    out_weight,
    out_bias,
    mlp_gain,
    mlp_shift,
    up_weight,
    up_bias,
    down_weight,
    down_bias,
    cotangent,
):
    D = tokens.shape[2]
    C = qkv_weight.shape[2]
    F = up_weight.shape[1]
    core = lambda x: swap(x, "tensor", 4, 1)
    cross = lambda x: swap(x, "tensor", 4, 2)
    tie = lax.optimization_barrier
    dp = lax.axis_index("dp")
    me = lax.axis_index("tensor")
    h = jnp.stack([dp & 1, dp >> 1 & 1, me, dp]).astype(jnp.int32)
    beside = lambda x: swap(x, "dp", n_dp, 1)
    my_half = lambda w: lax.dynamic_slice_in_dim(w, (dp & 1) * (w.shape[0] // 2), w.shape[0] // 2, 0)

    bits = [1 << i for i in range(n_dp.bit_length() - 1)]
    attn_bits, up_bits, down_bits = bits, bits, bits[1:2] + bits[:1] + bits[2:]
    attn_order, up_order, down_order = map(piece_order, (attn_bits, up_bits, down_bits))

    biases = jnp.concatenate(
        [up_bias.reshape(1, F), jnp.pad(qkv_bias, ((0, 0), (0, F - C))), jnp.zeros((EXTRA - 3, F), BF)], 0
    )
    qkv = jnp.concatenate([biases, jnp.transpose(qkv_weight, (1, 2, 0)).reshape(3 * C, D)], 0)
    qkv_x, qkv_c = cross(my_half(qkv)), core(qkv)
    up_s = my_half(up_weight)
    g = cotangent[0]
    stream, normed, normed_t, g_v, cot_t, cot_sum, mask = first_norm(
        (attn_order, down_order), tokens[0], g, thought_slots, thoughts[0], attn_gain, attn_shift, segment_ids, (up_s, h)
    )
    saved = [None] * 4
    qkv_w = [(qkv,), (qkv_c,)]

    def forward(s, deps=()):
        saved[s] = attend(h, normed, mask, qkv_w[s], C, "attend%d" % s, deps)

    def wait(s, *arrays):
        *arrays, stats = tie((*arrays, saved[s][2]))
        saved[s] = (*saved[s][:2], stats)
        return arrays

    forward(1, (up_s,))
    qkv_x, up_s, out_s = wait(1, qkv_x, up_s, out_weight)
    qkv_y, qkv_cx, out_x, up_x = beside(qkv_x), core(qkv_x), cross(out_s), cross(up_s)
    forward(0)
    qkv_y, out_s = wait(0, qkv_y, out_weight)
    qkv_cy, out_c = core(qkv_y), core(out_s)
    qkv_w += [(qkv_x, qkv_y), (qkv_cx, qkv_cy)]
    forward(2, (qkv_cx,))
    out_x, down_s = wait(2, out_x, down_weight)
    out_cx, down_x = core(out_x), cross(down_s)
    forward(3, (out_c,))
    up_x, up_s, down_s = wait(3, up_x, up_weight, down_weight)
    up_y, up_cx, up_c, down_c = beside(up_x), core(up_x), core(up_s), core(down_s)
    middle, nm, nm_t, token = second_norm(
        up_order, stream, out_bias, mlp_gain, mlp_shift, [c for _, c, _ in saved], [out_weight, out_c, out_x, out_cx]
    )
    gb, acts, grads = [None] * 4, [None] * 4, [None] * 4
    first_bits = (up_bits[0].bit_length() - 1, down_bits[0].bit_length() - 1)

    def hidden(s, ws, accs, deps=()):
        o, m, hs, ps, gb[s] = mlp(h, nm, g_v, qkv_w[s][:1] if s < 2 else qkv_w[s], ws, accs, "mlp%d" % s, deps)
        acts[s] = (hs, ps)
        return o, m

    def hidden_grads(s, adds=(), deps=()):
        grads[s] = mlp_grads(h, nm_t, cot_t, *acts[s], adds, first_bits, "mlp_grads%d" % s, deps)

    accs = hidden(1, (up_c, down_c), ())
    hidden_grads(1, (), (up_cx,))
    near = list(map(core, grads[1]))
    accs = hidden(0, (up_weight, down_weight), accs, tuple(grads[1]))
    up_y, gb[0] = tie((up_y, gb[0]))
    up_cy = core(up_y)
    accs = hidden(2, (up_x, up_y, down_x), accs)
    hidden_grads(0, near, (gb[2],))
    up_k, up_o, down_k, down_o = grads[0]
    own = [[up_k, swap(up_o, "dp", n_dp, up_bits[0])], [down_k, swap(down_o, "dp", n_dp, down_bits[0])]]
    down_x, gb[0] = tie((down_x, gb[0]))
    accs = hidden(3, (up_cx, up_cy, core(down_x)), accs, (up_o,))
    hidden_grads(3)
    near = list(map(core, grads[3]))
    out, ag, ag_t, mg, sums2 = second_back(attn_order, middle, *accs, g_v, mlp_gain, down_bias)

    def along(sent, bit):
        return swap(sent, "dp", n_dp, bit)

    def at(bit):
        return bit.bit_length() - 1

    g_attn, g_qb = [None] * 4, [None] * 4

    def back(s, adds=(), deps=()):
        w_out = (out_weight, out_c, out_x, out_cx)[s]
        jgs[s], *g_attn[s], g_qb[s] = attend_back(
            h, ag, ag_t, normed_t, mask, saved[s], w_out, adds, at(attn_bits[0]), "attend_back%d" % s, deps
        )

    jgs = [None] * 4
    ways = (up_bits, down_bits)
    back(3)
    hidden_grads(2, near, (g_qb[3],))
    near = list(map(core, g_attn[3]))
    up_k, up_o, down_k, down_o = grads[2]
    far = [[up_k, along(up_o, up_bits[0])], [down_k, along(down_o, down_bits[0])]]
    own[0][1], own[1][1], g_qb[3] = tie((own[0][1], own[1][1], g_qb[3]))
    up_m, up_k, down_m, down_k = merge(h, [(a, at(w[1])) for a, w in zip(own, ways)], "merge_own", (up_o,))
    own = [[up_k, along(up_m, up_bits[1])], [down_k, along(down_m, down_bits[1])]]
    back(1, (), (up_m,))
    back(2, near, (g_qb[1],))
    near = list(map(core, g_attn[1]))
    attn_far = [g_attn[2][0], along(g_attn[2][1], attn_bits[0])]
    far[0][1], far[1][1], g_qb[2] = tie((far[0][1], far[1][1], g_qb[2]))
    up_m, up_k, down_m, down_k = merge(h, [(a, at(w[1])) for a, w in zip(far, ways)], "merge_far")
    far = [[up_k, along(up_m, up_bits[1])], [down_k, along(down_m, down_bits[1])]]
    back(0, near, (up_m, own[0][1], own[1][1]))
    attn_own = [g_attn[0][0], along(g_attn[0][1], attn_bits[0])]
    gtok, gth, sums1 = first_back(h, stream, mg, attn_gain, thought_slots, jgs, qkv_w)
    far[0][-1], far[1][-1], attn_far[1], sums1 = tie((far[0][-1], far[1][-1], attn_far[1], sums1))
    far_m, far_k, *far_s = merge(h, [(attn_far, at(attn_bits[1]))] + [(a, None) for a in far], "merge_last")
    own = [a + [cross(x)] for a, x in zip(own, far_s)]
    attn_far = [far_k, along(far_m, attn_bits[1])]

    late, gb, g_qb, sums1, sums2, cot_sum = tie((h, gb, g_qb, sums1, sums2, cot_sum))
    me, dp = late[2], late[3]
    rel = [jnp.concatenate([b, jnp.pad(q, ((0, 0), (0, F - 3 * C)))], 0) for b, q in zip(gb, g_qb)]
    first = [jnp.where(me & 1 == 0, rel[t], rel[t ^ 1]) for t in range(4)]
    ordered = jnp.concatenate([jnp.where(me & 2 == 0, first[t], first[t ^ 2]) for t in range(4)], 0)
    small = jnp.concatenate([ordered, sums1[:2], sums2[:3], cot_sum], 0)
    attn_own[1], small = tie((attn_own[1], small))

    wide = lambda a: a.astype(F32)

    def total(arrays):
        t = wide(arrays[0])
        for a in arrays[1:]:
            t = t + wide(a)
        return t

    def part(arrays, bit, mine):
        n = arrays[0].shape[0] // 2
        return [jnp.where((dp & bit != 0) == mine, a[n:], a[:n]) for a in arrays]

    def halve(arrays, bit):
        sent = total(part(arrays, bit, False)).astype(BF)
        return part(arrays, bit, True) + [along(sent, bit)]

    attn_own = halve(attn_own, attn_bits[1])
    attn_own.append(cross(total(attn_far).astype(BF)))
    for i in range(2, len(bits)):
        *own, attn_own = [halve(a, w[i]) for a, w in zip((*own, attn_own), (*ways, attn_bits))]
    r_up, r_dn, r_at = total(own[0]), total(own[1]), total(attn_own)

    for axis, size in (("tensor", 4), ("dp", n_dp)):
        bit = 1
        while bit < size:
            small = small + swap(small, axis, size, bit)
            bit *= 2
    mine = sum(jnp.where(me == t, small[2 * t:2 * t + 2], 0.0) for t in range(4))
    return (
        out[None],
        gtok[None],
        gth.astype(BF)[None],
        small[8],
        small[9],
        r_at[:, :3 * C].reshape(-1, 3, C),
        jnp.stack([mine[1, :C], mine[1, 2 * C:3 * C]]),
        r_at[:, 3 * C:].T,
        small[12],
        small[10],
        small[11],
        r_up,
        mine[0],
        r_dn.T,
        small[13],
    )


def solution(mesh):
    rows = P(("dp", "tensor"), None, None)
    placed = (
        rows,
        rows,
        P(("dp", "tensor"), None),
        P(("dp", "tensor"), None),
        P(),
        P(),
        P(None, None, "tensor"),
        P(None, "tensor"),
        P("tensor", None),
        P(),
        P(),
        P(),
        P(None, "tensor"),
        P("tensor"),
        P("tensor", None),
        P(),
        rows,
    )
    return jax.shard_map(
        functools.partial(local, mesh.shape["dp"]),
        mesh=mesh,
        in_specs=placed,
        out_specs=(
            rows,
            rows,
            rows,
            P(),
            P(),
            P("dp", None, "tensor"),
            P(None, "tensor"),
            P("tensor", "dp"),
            P(),
            P(),
            P(),
            P("dp", "tensor"),
            P("tensor"),
            P("tensor", "dp"),
            P(),
        ),
        check_vma=False,
    )
```

```python
import functools

import jax
import jax.numpy as jnp
from jax import lax
from jax.experimental import pallas as pl
from jax.experimental.pallas import tpu as pltpu
from jax.sharding import PartitionSpec as P

F32 = jnp.float32
BF = jnp.bfloat16
HD = 64
QB = 256
EPS = 1e-05
NEG = -1e30
NN = ((1,), (0,))
NT = ((1,), (1,))
GA, GB = 0.7978845608028654, 0.044715
EXTRA = 32
SMALL = pl.BlockSpec(memory_space=pltpu.SMEM)


def dot(a, b, dims=NN):
    return lax.dot_general(a, b, (dims, ((), ())), preferred_element_type=F32)


def full(shape):
    zeros = (0,) * len(shape)
    return pl.BlockSpec(tuple(shape), lambda *_: zeros)


def sds(shape, dtype):
    return jax.ShapeDtypeStruct(tuple(shape), dtype)


def vmem(shape, dtype):
    return pltpu.VMEM(tuple(shape), dtype)


def keep(x):
    return pltpu.with_memory_space_constraint(x, pltpu.VMEM)


def in_hbm(x):
    return pltpu.with_memory_space_constraint(x, pltpu.HBM)


RES = pl.BlockSpec(memory_space=pltpu.VMEM)


def params(mib):
    return pltpu.CompilerParams(vmem_limit_bytes=mib << 20)


SCALE = 1.2e8


def cost(micros):
    return pl.CostEstimate(flops=int(micros * SCALE), bytes_accessed=0, transcendentals=0)


def vector(ref):
    return ref[...].astype(F32).reshape(1, -1)


def normalize(x):
    mean = jnp.mean(x, axis=-1, keepdims=True)
    xc = x - mean
    var = jnp.mean(xc * xc, axis=-1, keepdims=True)
    rstd = lax.rsqrt(var + EPS)
    return xc * rstd, rstd


def norm_back(u, xhat, rstd):
    mu = jnp.mean(u, axis=-1, keepdims=True)
    mux = jnp.mean(u * xhat, axis=-1, keepdims=True)
    return rstd * (u - mu - xhat * mux)


def one_hot(slots, row0, rows):
    pos = lax.broadcasted_iota(jnp.int32, (rows, slots.shape[1]), 0) + row0
    return pos == slots


def run(kernel, ins, specs, deps, outs, out_specs, scratch=(), mib=16, micros=4, name=None, grid=(1,), aliases=None):
    n, k = len(ins), len(deps)
    return pl.pallas_call(
        lambda *refs: kernel(*refs[:n], *refs[n + k:]),
        grid=grid,
        in_specs=list(specs) + [pl.BlockSpec(memory_space=pl.ANY)] * k,
        out_specs=out_specs,
        out_shape=outs,
        scratch_shapes=list(scratch),
        input_output_aliases=aliases or {},
        compiler_params=params(mib),
        cost_estimate=cost(micros),
        name=name,
    )(*[keep(a) if sp is RES else a for a, sp in zip(ins, specs)], *deps)


def piece_order(bits):
    k = len(bits)
    return [sum(bits[j] for j in range(k) if p >> (k - 1 - j) & 1) for p in range(1 << k)]


def ordered(x, order):
    rows = x.shape[0] // len(order)
    if rows % 16:
        x = x.astype(F32)
    return jnp.concatenate([x[d * rows:(d + 1) * rows] for d in order], 0).astype(BF)


def halves(h, refs):
    n = refs[0].shape[0]
    first = h[0] * n
    for ref, at in zip(refs, (first, n - first)):
        yield ref, pl.ds(pl.multiple_of(at, 16), n)


def whole(h, refs, scratch=None):
    if len(refs) == 1:
        return refs[0]
    for ref, rows in halves(h, refs):
        scratch[rows, :] = ref[...]
    return scratch


def front(h, refs):
    return refs[0][...] if len(refs) == 1 else jnp.where(h[0] == 0, refs[0][...], refs[1][...])


def first_kernel(attn_order, down_order, tok, cot, slots, thoughts, gain, shift, seg, stream, normed, normed_t, cot_v, cot_t, cot_sum, mask):
    i = pl.program_id(0)
    r = pl.ds(pl.multiple_of(i * QB, QB), QB)
    hot = one_hot(slots[...], i * QB, QB)
    inserted = dot(hot.astype(BF), thoughts[...])
    covered = jnp.sum(hot.astype(F32), axis=1, keepdims=True) > 0.5
    x = jnp.where(covered, inserted, tok[...].astype(F32))
    stream[r, :] = x.astype(BF)
    xhat, _ = normalize(x)
    n = (xhat * vector(gain) + vector(shift)).astype(BF)
    normed[r, :] = n
    normed_t[:, r] = ordered(n.T, attn_order)
    g = cot[...]
    cot_v[r, :] = g
    cot_t[:, r] = ordered(g.T, down_order)

    @pl.when(i == 0)
    def _():
        cot_sum[...] = jnp.zeros_like(cot_sum)

    cot_sum[...] += jnp.sum(g.astype(F32), axis=0, keepdims=True)
    k0 = pl.multiple_of(jnp.maximum(i - 1, 0) * QB, QB)
    seg_q = seg[:, r]
    seg_k = jnp.broadcast_to(seg[:, pl.ds(k0, 2 * QB)], (QB, 2 * QB)).T
    kpos = lax.broadcasted_iota(jnp.int32, (2 * QB, QB), 0) + k0
    qpos = lax.broadcasted_iota(jnp.int32, (2 * QB, QB), 1) + i * QB
    mask[i] = jnp.where((seg_k == seg_q) & (kpos <= qpos), 0.0, NEG)


def first_norm(orders, tok, cot, slots, thoughts, gain, shift, seg, deps):
    L, D = tok.shape
    nq = L // QB
    rows = pl.BlockSpec((QB, D), lambda i: (i, 0))
    ins = (in_hbm(tok), in_hbm(cot), slots, thoughts, gain, shift, seg)
    return run(
        functools.partial(first_kernel, *orders),
        ins,
        [rows, rows] + [full(a.shape) for a in ins[2:]],
        deps,
        [vmem((L, D), BF), vmem((L, D), BF), vmem((D, L), BF), vmem((L, D), BF), vmem((D, L), BF), sds((1, D), F32), vmem((nq, 2 * QB, QB), F32)],
        [RES] * 5 + [full((1, D)), RES],
        grid=(nq,),
        name="first_norm",
    )


def window(i):
    return (0, QB) if i == 0 else ((i - 1) * QB, 2 * QB)


def head_mask(h, width):
    lane = lax.broadcasted_iota(jnp.int32, (1, width), 1)
    return ((lane >= h * HD) & (lane < (h + 1) * HD)).astype(BF)


def attend_kernel(h0, normed, mask, *refs):
    *ws, joined, ctx, lse, vt, buf = refs
    L = normed.shape[0]
    C = ctx.shape[1]
    w = whole(h0, ws, buf)
    bias = w[:EXTRA, :].astype(F32)
    base = EXTRA
    for i in range(L // QB):
        r = pl.ds(i * QB, QB)
        for c in range(3):
            v = dot(normed[r, :], w[base + c * C:base + (c + 1) * C, :], NT)
            if c != 1:
                b = 1 + c // 2
                v = v + bias[b:b + 1, :C]
            v = v.astype(BF)
            joined[c, r, :] = v
            if c == 2:
                vt[:, r] = v.T
    masks = [head_mask(h, C) for h in range(C // HD)]
    for i in range(L // QB):
        k0, kn = window(i)
        r = pl.ds(i * QB, QB)
        q = joined[0, r, :] * BF(HD ** -0.5)
        k = joined[1, pl.ds(k0, kn), :]
        m = mask[i, :kn, :]
        H = C // HD
        qs = jnp.concatenate([q * masks[h] for h in range(H)], axis=0)
        s = dot(k, qs, NT) + jnp.concatenate([m] * H, axis=1)
        top = jnp.max(s, axis=0, keepdims=True)
        e = jnp.exp(s - top)
        total = jnp.sum(e, axis=0, keepdims=True)
        p = (e * (1.0 / total)).astype(BF)
        stat = top + jnp.log(total)
        stats = [stat[:, h * QB:(h + 1) * QB] for h in range(H)]
        ps = jnp.concatenate([p[:, h * QB:(h + 1) * QB] for h in range(H)], axis=0)
        rid = lax.broadcasted_iota(jnp.int32, (C, 1), 0) // HD
        vtb = jnp.concatenate([vt[:, pl.ds(k0, kn)] * (rid == h).astype(BF) for h in range(H)], axis=1)
        ctx[r, :] = dot(vtb, ps).T.astype(BF)
        for h in range(C // HD):
            lse[h:h + 1, r] = stats[h]


def attend(h, normed, mask, ws, C, name, deps=()):
    L, D = normed.shape
    return run(
        attend_kernel,
        (h, normed, mask, *ws),
        [SMALL, RES, RES] + [RES for w in ws],
        deps,
        [vmem((3, L, C), BF), vmem((L, C), BF), vmem((8, L), F32)],
        [RES, RES, RES],
        [pltpu.VMEM((C, L), BF), pltpu.VMEM((3 * C + EXTRA, D), BF)],
        mib=12,
        micros=5,
        name=name,
    )


def second_norm(order, stream, out_bias, gain, shift, ctxs, ws):
    L, D = stream.shape
    n = len(ws)
    C = ctxs[0].shape[1]

    def kernel(stream, out_bias, gain, shift, *refs):
        *refs, middle, nm, nm_t, token = refs
        i = pl.program_id(0)
        r = pl.ds(pl.multiple_of(i * QB, QB), QB)

        @pl.when(i == 0)
        def _():
            token[...] = jnp.zeros_like(token)

        acc = stream[r, :].astype(F32) + vector(out_bias)
        for j in range(n):
            acc = acc + dot(refs[j][r, :], refs[n + j][...])
        middle[r, :] = acc
        xhat, _ = normalize(acc)
        v = (xhat * vector(gain) + vector(shift)).astype(BF)
        nm[r, :] = v
        nm_t[:, r] = ordered(v.T, order)

    return run(
        kernel,
        (stream, out_bias, gain, shift, *ctxs, *ws),
        [RES] + [full(gain.shape)] * 3 + [RES] * n + [full(w.shape) for w in ws],
        (),
        [vmem((L, D), F32), vmem((L, D), BF), vmem((D, L), BF), sds((8, 128), F32)],
        [RES] * 3 + [full((8, 128))],
        [],
        grid=(L // QB,),
        name="second_norm",
    )


def mlp_kernel(n, first, h0, nm, g, *refs):
    bias, ws, rest = refs[:n], refs[n:2 * n + 1], refs[2 * n + 1:]
    if not first:
        o_in, m_in = rest[:2]
        rest = rest[2:]
    o_acc, m_acc, hs, ps, g_ub, *bufs = rest
    w_up, w_dn = whole(h0, ws[:n], *bufs), ws[n]
    L = nm.shape[0]
    up_b = front(h0, bias)[0:1, :].astype(F32)
    total = jnp.zeros((1, w_up.shape[1]), F32)
    rows = L // 2
    blocks = [pl.ds(i * rows, rows) for i in range(2)]

    def before(r):
        return dot(nm[r, :], w_up[...]) + up_b, dot(g[r, :], w_dn[...], NT)

    ready = before(blocks[0])
    for i, r in enumerate(blocks):
        x, gd = ready
        if i + 1 < len(blocks):
            ready = before(blocks[i + 1])
        x2 = x * x
        th = jnp.tanh(x * (GA + (GA * GB) * x2))
        ht = 0.5 * th + 0.5
        h = (x * ht).astype(BF)
        dg = ht + x * (0.5 - 0.5 * (th * th)) * (GA + (3 * GA * GB) * x2)
        pg = (gd * dg).astype(BF)
        hs[r, :] = h
        ps[r, :] = pg
        total = total + jnp.sum(pg.astype(F32), axis=0, keepdims=True)
        o, m = dot(h, w_dn[...]), dot(pg, w_up[...], NT)
        o_acc[r, :] = o if first else o_in[r, :] + o
        m_acc[r, :] = m if first else m_in[r, :] + m
    g_ub[...] = total


def mlp(h, nm, g, biases, ws, accs, name, deps=()):
    L, D = nm.shape
    n = len(biases)
    F = ws[0].shape[1]
    return run(
        functools.partial(mlp_kernel, n, not accs),
        (h, nm, g, *biases, *ws, *accs),
        [SMALL, RES, RES] + [pl.BlockSpec((EXTRA, F), lambda _: (0, 0))] * n + [RES for w in ws] + [RES] * len(accs),
        deps,
        [vmem((L, D), F32)] * 2 + [vmem((L, F), BF)] * 2 + [sds((1, F), F32)],
        [RES] * 4 + [full((1, F))],
        [] if n == 1 else [pltpu.VMEM((D, F), BF)],
        aliases={4 + 2 * n: 0, 5 + 2 * n: 1} if accs else None,
        mib=14,
        micros=7,
        name=name,
    )


def mlp_grads(h, nm_t, g_t, hs, ps, adds, bits, name, deps=()):
    D, L = nm_t.shape
    F = hs.shape[1]
    n = D // 2

    def kernel(h0, nm_t, g_t, hs, ps, *refs):
        c = pl.ds(pl.multiple_of(pl.program_id(0) * QB, QB), QB)
        for j, (left, right) in enumerate(((nm_t, ps), (g_t, hs))):
            for k in range(2):
                half = k ^ h0[bits[j]] if adds else k
                rows = pl.ds(pl.multiple_of(half * n, n), n)
                v = dot(left[rows, :], right[:, c])
                if adds:
                    v = v + jnp.where(half == 0, refs[2 * j][...], refs[2 * j + 1][...]).astype(F32)
                refs[len(adds) + 2 * j + k][...] = v.astype(BF)

    col = pl.BlockSpec((n, QB), lambda c: (0, c))
    return run(
        kernel,
        (h, nm_t, g_t, hs, ps, *adds),
        [SMALL] + [RES] * 4 + [col] * len(adds),
        deps,
        [sds((n, F), BF)] * 4,
        [col] * 4,
        mib=12,
        grid=(F // QB,),
        name=name,
    )


def second_back_kernel(order, middle, o_acc, m_acc, g, gain, down_bias, out, ag, ag_t, mg, sums):
    i = pl.program_id(0)
    r = pl.ds(pl.multiple_of(i * QB, QB), QB)
    mid = middle[r, :]
    out[...] = (mid + o_acc[r, :] + vector(down_bias)).astype(BF)
    xhat, rstd = normalize(mid)
    d = m_acc[r, :]
    m = g[r, :].astype(F32) + norm_back(d * vector(gain), xhat, rstd)
    mg[r, :] = m
    a = m.astype(BF)
    ag[r, :] = a
    ag_t[:, r] = ordered(a.T, order)

    @pl.when(i == 0)
    def _():
        sums[...] = jnp.zeros_like(sums)

    sums[0:1, :] += jnp.sum(d * xhat, axis=0, keepdims=True)
    sums[1:2, :] += jnp.sum(d, axis=0, keepdims=True)
    sums[2:3, :] += jnp.sum(a.astype(F32), axis=0, keepdims=True)


def second_back(order, middle, o_acc, m_acc, g, gain, down_bias):
    L, D = middle.shape
    rows = pl.BlockSpec((QB, D), lambda i: (i, 0))
    return run(
        functools.partial(second_back_kernel, order),
        (middle, o_acc, m_acc, g, gain, down_bias),
        [RES] * 4 + [full(gain.shape)] * 2,
        (),
        [sds((L, D), BF), vmem((L, D), BF), vmem((D, L), BF), vmem((L, D), F32), sds((8, D), F32)],
        [rows, RES, RES, RES, full((8, D))],
        grid=(L // QB,),
        name="second_back",
    )


def attend_back_kernel(split, bit, h0, ag, ag_t, normed_t, mask, joined, ctx, lse, w_out, *rest):
    if split:
        adds, rest = rest[:2], rest[2:]
    jg, *g_w, g_b, dctx, kt, dk, dv = rest
    L, D = ag.shape
    C = ctx.shape[1]
    H = C // HD
    for i in range(L // QB):
        r = pl.ds(i * QB, QB)
        dctx[r, :] = dot(ag[r, :], w_out[...], NT).astype(BF)
        kt[:, r] = joined[1, r, :].T
    masks = [head_mask(h, C) for h in range(H)]
    dk[...] = jnp.zeros_like(dk)
    dv[...] = jnp.zeros_like(dv)
    for i in range(L // QB):
        k0, kn = window(i)
        r = pl.ds(i * QB, QB)
        kr = pl.ds(k0, kn)
        q = joined[0, r, :] * BF(HD ** -0.5)
        k = joined[1, kr, :]
        v = joined[2, kr, :]
        do = dctx[r, :]
        m = mask[i, :kn, :]
        qs = jnp.concatenate([q * masks[h] for h in range(H)], axis=0)
        dos = jnp.concatenate([do * masks[h] for h in range(H)], axis=0)
        top = jnp.concatenate([lse[h:h + 1, r] for h in range(H)], axis=1)
        s = dot(k, qs, NT)
        dp = dot(v, dos, NT)
        p = jnp.exp(s + jnp.concatenate([m] * H, axis=1) - top)
        inner = jnp.sum(p * dp, axis=0, keepdims=True)
        ds = (p * (dp - inner)).astype(BF)
        dv[kr, :] += dot(p.astype(BF), dos)
        dk[kr, :] += dot(ds, qs)
        rid = lax.broadcasted_iota(jnp.int32, (C, 1), 0) // HD
        ktb = jnp.concatenate([kt[:, kr] * (rid == h).astype(BF) for h in range(H)], axis=1)
        dst = jnp.concatenate([ds[:, h * QB:(h + 1) * QB] for h in range(H)], axis=0)
        jg[r, :C] = (dot(ktb, dst).T * HD ** -0.5).astype(BF)
    jg[:, C:2 * C] = dk[...].astype(BF)
    jg[:, 2 * C:] = dv[...].astype(BF)
    rows_n = D // 2
    for j in range(2):
        half = j ^ h0[bit] if split else j
        rows = pl.ds(pl.multiple_of(half * rows_n, rows_n), rows_n)
        v, v_out = dot(normed_t[rows, :], jg[...]), dot(ag_t[rows, :], ctx[...])
        if split:
            add = jnp.where(half == 0, adds[0][...], adds[1][...]).astype(F32)
            v, v_out = v + add[:, :3 * C], v_out + add[:, 3 * C:]
        g_w[j][:, :3 * C] = v.astype(BF)
        g_w[j][:, 3 * C:] = v_out.astype(BF)
    g_b[...] = jnp.sum(jg[...].astype(F32), axis=0, keepdims=True)


def attend_back(h, ag, ag_t, normed_t, mask, saved, w_out, adds, bit, name, deps=()):
    joined, ctx, lse = saved
    L, D = ag.shape
    C = ctx.shape[1]
    shape = (D // 2, 4 * C)
    return run(
        functools.partial(attend_back_kernel, bool(adds), bit),
        (h, ag, ag_t, normed_t, mask, joined, ctx, lse, w_out, *adds),
        [SMALL] + [RES] * (8 + len(adds)),
        deps,
        [vmem((L, 3 * C), BF)] + [vmem(shape, BF)] * 2 + [sds((1, 3 * C), F32)],
        [RES] * 3 + [full((1, 3 * C))],
        [pltpu.VMEM((L, C), BF), pltpu.VMEM((C, L), BF), pltpu.VMEM((L, C), F32), pltpu.VMEM((L, C), F32)],
        mib=10,
        micros=9,
        name=name,
    )


def first_back(h, stream, mg, gain, slots, jgs, ws, deps=()):
    L, D = stream.shape
    n = len(jgs)
    flat = [w for shard in ws for w in shard]

    def kernel(h0, stream, mg, gain, slots, *refs):
        gtok, gth, sums, buf = refs[n + len(flat):]
        i = pl.program_id(0)
        r = pl.ds(pl.multiple_of(i * QB, QB), QB)

        @pl.when(i == 0)
        def _():
            sums[...] = jnp.zeros_like(sums)
            gth[...] = jnp.zeros_like(gth)
            at = n
            for j, shard in enumerate(ws):
                if len(shard) > 1:
                    whole(h0, refs[at:at + 2], buf.at[j])
                at += len(shard)

        d, at = None, n
        for j, shard in enumerate(ws):
            w = refs[at] if len(shard) == 1 else buf.at[j]
            at += len(shard)
            v = dot(refs[j][r, :], w[EXTRA:, :])
            d = v if d is None else d + v
        xhat, rstd = normalize(stream[r, :].astype(F32))
        sg = (mg[r, :] + norm_back(d * vector(gain), xhat, rstd)).astype(BF)
        hot = one_hot(slots[...], i * QB, QB)
        covered = jnp.sum(hot.astype(F32), axis=1, keepdims=True) > 0.5
        gtok[...] = jnp.where(covered, 0.0, sg.astype(F32)).astype(BF)
        gth[...] += dot(hot.astype(BF), sg, ((0,), (0,)))
        sums[0:1, :] += jnp.sum(d * xhat, axis=0, keepdims=True)
        sums[1:2, :] += jnp.sum(d, axis=0, keepdims=True)

    return run(
        kernel,
        (h, stream, mg, gain, slots, *jgs, *flat),
        [SMALL, RES, RES, full(gain.shape), full(slots.shape)] + [RES] * (n + len(flat)),
        deps,
        [sds((L, D), BF), sds((slots.shape[1], D), F32), sds((8, D), F32)],
        [pl.BlockSpec((QB, D), lambda i: (i, 0)), full((slots.shape[1], D)), full((8, D))],
        [pltpu.VMEM((n, ws[0][0].shape[0], D), BF)],
        mib=16,
        micros=8,
        grid=(L // QB,),
        name="first_back",
    )


def merge(h, groups, name, deps=()):
    flat = [a for arrays, _ in groups for a in arrays]
    outs = []
    for arrays, bit in groups:
        R, W = arrays[0].shape
        outs += [sds((R, W), BF)] if bit is None else [sds((R // 2, W), BF), sds((R // 2, W), F32)]

    def kernel(h0, *refs):
        at, to = 0, len(flat)
        for arrays, bit in groups:
            group = refs[at:at + len(arrays)]
            at += len(arrays)
            n = arrays[0].shape[0] // 2
            mine = 0 if bit is None else h0[bit]
            for half in ((0, 1) if bit is None else (1 - mine, mine)):
                rows = pl.ds(pl.multiple_of(half * n, 16), n)
                t = group[0][rows, :].astype(F32)
                for ref in group[1:]:
                    t = t + ref[rows, :].astype(F32)
                if bit is None:
                    refs[to][rows, :] = t.astype(BF)
                else:
                    refs[to][...] = t.astype(refs[to].dtype)
                    to += 1
            to += bit is None

    return run(
        kernel,
        (h, *flat),
        [SMALL] + [full(a.shape) for a in flat],
        deps,
        outs,
        [full(o.shape) for o in outs],
        mib=12,
        name=name,
    )


def swap(x, axis, size, bit):
    return lax.ppermute(x, axis, [(i, i ^ bit) for i in range(size)])


def after(x, dep):
    return lax.optimization_barrier((x, dep))


def local(
    n_dp,
    tokens,
    thoughts,
    thought_slots,
    segment_ids,
    attn_gain,
    attn_shift,
    qkv_weight,
    qkv_bias,
    out_weight,
    out_bias,
    mlp_gain,
    mlp_shift,
    up_weight,
    up_bias,
    down_weight,
    down_bias,
    cotangent,
):
    D = tokens.shape[2]
    C = qkv_weight.shape[2]
    F = up_weight.shape[1]
    core = lambda x: swap(x, "tensor", 4, 1)
    cross = lambda x: swap(x, "tensor", 4, 2)
    tie = lax.optimization_barrier
    dp = lax.axis_index("dp")
    me = lax.axis_index("tensor")
    h = jnp.stack([dp & 1, dp >> 1 & 1, me, dp]).astype(jnp.int32)
    beside = lambda x: swap(x, "dp", n_dp, 1)
    my_half = lambda w: lax.dynamic_slice_in_dim(w, (dp & 1) * (w.shape[0] // 2), w.shape[0] // 2, 0)

    bits = [1 << i for i in range(n_dp.bit_length() - 1)]
    attn_bits, up_bits, down_bits = bits, bits, bits[1:2] + bits[:1] + bits[2:]
    attn_order, up_order, down_order = map(piece_order, (attn_bits, up_bits, down_bits))

    biases = jnp.concatenate(
        [up_bias.reshape(1, F), jnp.pad(qkv_bias, ((0, 0), (0, F - C))), jnp.zeros((EXTRA - 3, F), BF)], 0
    )
    qkv = jnp.concatenate([biases, jnp.transpose(qkv_weight, (1, 2, 0)).reshape(3 * C, D)], 0)
    qkv_x, qkv_c = cross(my_half(qkv)), core(qkv)
    up_s = my_half(up_weight)
    g = cotangent[0]
    stream, normed, normed_t, g_v, cot_t, cot_sum, mask = first_norm(
        (attn_order, down_order), tokens[0], g, thought_slots, thoughts[0], attn_gain, attn_shift, segment_ids, (up_s, h)
    )
    saved = [None] * 4
    qkv_w = [(qkv,), (qkv_c,)]

    def forward(s, deps=()):
        saved[s] = attend(h, normed, mask, qkv_w[s], C, "attend%d" % s, deps)

    def wait(s, *arrays):
        *arrays, stats = tie((*arrays, saved[s][2]))
        saved[s] = (*saved[s][:2], stats)
        return arrays

    forward(1, (up_s,))
    qkv_x, up_s, out_s = wait(1, qkv_x, up_s, out_weight)
    qkv_y, qkv_cx, out_x, up_x = beside(qkv_x), core(qkv_x), cross(out_s), cross(up_s)
    forward(0)
    qkv_y, out_s = wait(0, qkv_y, out_weight)
    qkv_cy, out_c = core(qkv_y), core(out_s)
    qkv_w += [(qkv_x, qkv_y), (qkv_cx, qkv_cy)]
    forward(2, (qkv_cx,))
    out_x, down_s = wait(2, out_x, down_weight)
    out_cx, down_x = core(out_x), cross(down_s)
    forward(3, (out_c,))
    up_x, up_s, down_s = wait(3, up_x, up_weight, down_weight)
    up_y, up_cx, up_c, down_c = beside(up_x), core(up_x), core(up_s), core(down_s)
    middle, nm, nm_t, token = second_norm(
        up_order, stream, out_bias, mlp_gain, mlp_shift, [c for _, c, _ in saved], [out_weight, out_c, out_x, out_cx]
    )
    gb, acts, grads = [None] * 4, [None] * 4, [None] * 4
    first_bits = (up_bits[0].bit_length() - 1, down_bits[0].bit_length() - 1)

    def hidden(s, ws, accs, deps=()):
        o, m, hs, ps, gb[s] = mlp(h, nm, g_v, qkv_w[s][:1] if s < 2 else qkv_w[s], ws, accs, "mlp%d" % s, deps)
        acts[s] = (hs, ps)
        return o, m

    def hidden_grads(s, adds=(), deps=()):
        grads[s] = mlp_grads(h, nm_t, cot_t, *acts[s], adds, first_bits, "mlp_grads%d" % s, deps)

    accs = hidden(1, (up_c, down_c), ())
    hidden_grads(1, (), (up_cx,))
    near = list(map(core, grads[1]))
    accs = hidden(0, (up_weight, down_weight), accs, tuple(grads[1]))
    up_y, gb[0] = tie((up_y, gb[0]))
    up_cy = core(up_y)
    accs = hidden(2, (up_x, up_y, down_x), accs)
    hidden_grads(0, near, (gb[2],))
    up_k, up_o, down_k, down_o = grads[0]
    own = [[up_k, swap(up_o, "dp", n_dp, up_bits[0])], [down_k, swap(down_o, "dp", n_dp, down_bits[0])]]
    down_x, gb[0] = tie((down_x, gb[0]))
    accs = hidden(3, (up_cx, up_cy, core(down_x)), accs, (up_o,))
    hidden_grads(3)
    near = list(map(core, grads[3]))
    out, ag, ag_t, mg, sums2 = second_back(attn_order, middle, *accs, g_v, mlp_gain, down_bias)

    def along(sent, bit):
        return swap(sent, "dp", n_dp, bit)

    def at(bit):
        return bit.bit_length() - 1

    g_attn, g_qb = [None] * 4, [None] * 4

    def back(s, adds=(), deps=()):
        w_out = (out_weight, out_c, out_x, out_cx)[s]
        jgs[s], *g_attn[s], g_qb[s] = attend_back(
            h, ag, ag_t, normed_t, mask, saved[s], w_out, adds, at(attn_bits[0]), "attend_back%d" % s, deps
        )

    jgs = [None] * 4
    ways = (up_bits, down_bits)
    back(3)
    hidden_grads(2, near, (g_qb[3],))
    near = list(map(core, g_attn[3]))
    up_k, up_o, down_k, down_o = grads[2]
    far = [[up_k, along(up_o, up_bits[0])], [down_k, along(down_o, down_bits[0])]]
    own[0][1], own[1][1], g_qb[3] = tie((own[0][1], own[1][1], g_qb[3]))
    up_m, up_k, down_m, down_k = merge(h, [(a, at(w[1])) for a, w in zip(own, ways)], "merge_own", (up_o,))
    own = [[up_k, along(up_m, up_bits[1])], [down_k, along(down_m, down_bits[1])]]
    back(1, (), (up_m,))
    back(2, near, (g_qb[1],))
    near = list(map(core, g_attn[1]))
    attn_far = [g_attn[2][0], along(g_attn[2][1], attn_bits[0])]
    far[0][1], far[1][1], g_qb[2] = tie((far[0][1], far[1][1], g_qb[2]))
    up_m, up_k, down_m, down_k = merge(h, [(a, at(w[1])) for a, w in zip(far, ways)], "merge_far")
    far = [[up_k, along(up_m, up_bits[1])], [down_k, along(down_m, down_bits[1])]]
    back(0, near, (up_m, own[0][1], own[1][1]))
    attn_own = [g_attn[0][0], along(g_attn[0][1], attn_bits[0])]
    gtok, gth, sums1 = first_back(h, stream, mg, attn_gain, thought_slots, jgs, qkv_w)
    far[0][-1], far[1][-1], attn_far[1], sums1 = tie((far[0][-1], far[1][-1], attn_far[1], sums1))
    far_m, far_k, *far_s = merge(h, [(attn_far, at(attn_bits[1]))] + [(a, None) for a in far], "merge_last")
    own = [a + [cross(x)] for a, x in zip(own, far_s)]
    attn_far = [far_k, along(far_m, attn_bits[1])]

    late, gb, g_qb, sums1, sums2, cot_sum = tie((h, gb, g_qb, sums1, sums2, cot_sum))
    me, dp = late[2], late[3]
    rel = [jnp.concatenate([b, jnp.pad(q, ((0, 0), (0, F - 3 * C)))], 0) for b, q in zip(gb, g_qb)]
    first = [jnp.where(me & 1 == 0, rel[t], rel[t ^ 1]) for t in range(4)]
    ordered = jnp.concatenate([jnp.where(me & 2 == 0, first[t], first[t ^ 2]) for t in range(4)], 0)
    small = jnp.concatenate([ordered, sums1[:2], sums2[:3], cot_sum], 0)
    attn_own[1], small = tie((attn_own[1], small))

    wide = lambda a: a.astype(F32)

    def total(arrays):
        t = wide(arrays[0])
        for a in arrays[1:]:
            t = t + wide(a)
        return t

    def part(arrays, bit, mine):
        n = arrays[0].shape[0] // 2
        return [jnp.where((dp & bit != 0) == mine, a[n:], a[:n]) for a in arrays]

    def halve(arrays, bit):
        sent = total(part(arrays, bit, False)).astype(BF)
        return part(arrays, bit, True) + [along(sent, bit)]

    attn_own = halve(attn_own, attn_bits[1])
    attn_own.append(cross(total(attn_far).astype(BF)))
    for i in range(2, len(bits)):
        *own, attn_own = [halve(a, w[i]) for a, w in zip((*own, attn_own), (*ways, attn_bits))]
    r_up, r_dn, r_at = total(own[0]), total(own[1]), total(attn_own)

    for axis, size in (("tensor", 4), ("dp", n_dp)):
        bit = 1
        while bit < size:
            small = small + swap(small, axis, size, bit)
            bit *= 2
    mine = sum(jnp.where(me == t, small[2 * t:2 * t + 2], 0.0) for t in range(4))
    return (
        out[None],
        gtok[None],
        gth.astype(BF)[None],
        small[8],
        small[9],
        r_at[:, :3 * C].reshape(-1, 3, C),
        jnp.stack([mine[1, :C], mine[1, 2 * C:3 * C]]),
        r_at[:, 3 * C:].T,
        small[12],
        small[10],
        small[11],
        r_up,
        mine[0],
        r_dn.T,
        small[13],
    )


def solution(mesh):
    rows = P(("dp", "tensor"), None, None)
    placed = (
        rows,
        rows,
        P(("dp", "tensor"), None),
        P(("dp", "tensor"), None),
        P(),
        P(),
        P(None, None, "tensor"),
        P(None, "tensor"),
        P("tensor", None),
        P(),
        P(),
        P(),
        P(None, "tensor"),
        P("tensor"),
        P("tensor", None),
        P(),
        rows,
    )
    return jax.shard_map(
        functools.partial(local, mesh.shape["dp"]),
        mesh=mesh,
        in_specs=placed,
        out_specs=(
            rows,
            rows,
            rows,
            P(),
            P(),
            P("dp", None, "tensor"),
            P(None, "tensor"),
            P("tensor", "dp"),
            P(),
            P(),
            P(),
            P("dp", "tensor"),
            P("tensor"),
            P("tensor", "dp"),
            P(),
        ),
        check_vma=False,
    )
```

```python
import functools

import jax
import jax.numpy as jnp
from jax import lax
from jax.experimental import pallas as pl
from jax.experimental.pallas import tpu as pltpu
from jax.sharding import PartitionSpec as P

F32 = jnp.float32
BF = jnp.bfloat16
HD = 64
QB = 256
EPS = 1e-05
NEG = -1e30
NN = ((1,), (0,))
NT = ((1,), (1,))
GA, GB = 0.7978845608028654, 0.044715
EXTRA = 32
SMALL = pl.BlockSpec(memory_space=pltpu.SMEM)


def dot(a, b, dims=NN):
    return lax.dot_general(a, b, (dims, ((), ())), preferred_element_type=F32)


def full(shape):
    zeros = (0,) * len(shape)
    return pl.BlockSpec(tuple(shape), lambda *_: zeros)


def sds(shape, dtype):
    return jax.ShapeDtypeStruct(tuple(shape), dtype)


def vmem(shape, dtype):
    return pltpu.VMEM(tuple(shape), dtype)


def keep(x):
    return pltpu.with_memory_space_constraint(x, pltpu.VMEM)


def in_hbm(x):
    return pltpu.with_memory_space_constraint(x, pltpu.HBM)


RES = pl.BlockSpec(memory_space=pltpu.VMEM)


def params(mib):
    return pltpu.CompilerParams(vmem_limit_bytes=mib << 20)


SCALE = 1.2e8


def cost(micros):
    return pl.CostEstimate(flops=int(micros * SCALE), bytes_accessed=0, transcendentals=0)


def vector(ref):
    return ref[...].astype(F32).reshape(1, -1)


def normalize(x):
    mean = jnp.mean(x, axis=-1, keepdims=True)
    xc = x - mean
    var = jnp.mean(xc * xc, axis=-1, keepdims=True)
    rstd = lax.rsqrt(var + EPS)
    return xc * rstd, rstd


def norm_back(u, xhat, rstd):
    mu = jnp.mean(u, axis=-1, keepdims=True)
    mux = jnp.mean(u * xhat, axis=-1, keepdims=True)
    return rstd * (u - mu - xhat * mux)


def one_hot(slots, row0, rows):
    pos = lax.broadcasted_iota(jnp.int32, (rows, slots.shape[1]), 0) + row0
    return pos == slots


def run(kernel, ins, specs, deps, outs, out_specs, scratch=(), mib=16, micros=4, name=None, grid=(1,), aliases=None):
    n, k = len(ins), len(deps)
    return pl.pallas_call(
        lambda *refs: kernel(*refs[:n], *refs[n + k:]),
        grid=grid,
        in_specs=list(specs) + [pl.BlockSpec(memory_space=pl.ANY)] * k,
        out_specs=out_specs,
        out_shape=outs,
        scratch_shapes=list(scratch),
        input_output_aliases=aliases or {},
        compiler_params=params(mib),
        cost_estimate=cost(micros),
        name=name,
    )(*[keep(a) if sp is RES else a for a, sp in zip(ins, specs)], *deps)


def piece_order(bits):
    k = len(bits)
    return [sum(bits[j] for j in range(k) if p >> (k - 1 - j) & 1) for p in range(1 << k)]


def ordered(x, order):
    rows = x.shape[0] // len(order)
    if rows % 16:
        x = x.astype(F32)
    return jnp.concatenate([x[d * rows:(d + 1) * rows] for d in order], 0).astype(BF)


def halves(h, refs):
    n = refs[0].shape[0]
    first = h[0] * n
    for ref, at in zip(refs, (first, n - first)):
        yield ref, pl.ds(pl.multiple_of(at, 16), n)


def whole(h, refs, scratch=None):
    if len(refs) == 1:
        return refs[0]
    for ref, rows in halves(h, refs):
        scratch[rows, :] = ref[...]
    return scratch


def front(h, refs):
    return refs[0][...] if len(refs) == 1 else jnp.where(h[0] == 0, refs[0][...], refs[1][...])


def first_kernel(attn_order, down_order, tok, cot, slots, thoughts, gain, shift, seg, stream, normed, normed_t, cot_v, cot_t, cot_sum, mask):
    i = pl.program_id(0)
    r = pl.ds(pl.multiple_of(i * QB, QB), QB)
    hot = one_hot(slots[...], i * QB, QB)
    inserted = dot(hot.astype(BF), thoughts[...])
    covered = jnp.sum(hot.astype(F32), axis=1, keepdims=True) > 0.5
    x = jnp.where(covered, inserted, tok[...].astype(F32))
    stream[r, :] = x.astype(BF)
    xhat, _ = normalize(x)
    n = (xhat * vector(gain) + vector(shift)).astype(BF)
    normed[r, :] = n
    normed_t[:, r] = ordered(n.T, attn_order)
    g = cot[...]
    cot_v[r, :] = g
    cot_t[:, r] = ordered(g.T, down_order)

    @pl.when(i == 0)
    def _():
        cot_sum[...] = jnp.zeros_like(cot_sum)

    cot_sum[...] += jnp.sum(g.astype(F32), axis=0, keepdims=True)
    k0 = pl.multiple_of(jnp.maximum(i - 1, 0) * QB, QB)
    seg_q = seg[:, r]
    seg_k = jnp.broadcast_to(seg[:, pl.ds(k0, 2 * QB)], (QB, 2 * QB)).T
    kpos = lax.broadcasted_iota(jnp.int32, (2 * QB, QB), 0) + k0
    qpos = lax.broadcasted_iota(jnp.int32, (2 * QB, QB), 1) + i * QB
    mask[i] = jnp.where((seg_k == seg_q) & (kpos <= qpos), 0.0, NEG)


def first_norm(orders, tok, cot, slots, thoughts, gain, shift, seg, deps):
    L, D = tok.shape
    nq = L // QB
    rows = pl.BlockSpec((QB, D), lambda i: (i, 0))
    ins = (in_hbm(tok), in_hbm(cot), slots, thoughts, gain, shift, seg)
    return run(
        functools.partial(first_kernel, *orders),
        ins,
        [rows, rows] + [full(a.shape) for a in ins[2:]],
        deps,
        [vmem((L, D), BF), vmem((L, D), BF), vmem((D, L), BF), vmem((L, D), BF), vmem((D, L), BF), sds((1, D), F32), vmem((nq, 2 * QB, QB), F32)],
        [RES] * 5 + [full((1, D)), RES],
        grid=(nq,),
        name="first_norm",
    )


def window(i):
    return (0, QB) if i == 0 else ((i - 1) * QB, 2 * QB)


def head_mask(h, width):
    lane = lax.broadcasted_iota(jnp.int32, (1, width), 1)
    return ((lane >= h * HD) & (lane < (h + 1) * HD)).astype(BF)


def attend_kernel(h0, normed, mask, *refs):
    *ws, joined, ctx, lse, vt, buf = refs
    L = normed.shape[0]
    C = ctx.shape[1]
    w = whole(h0, ws, buf)
    bias = w[:EXTRA, :].astype(F32)
    base = EXTRA
    for i in range(L // QB):
        r = pl.ds(i * QB, QB)
        for c in range(3):
            v = dot(normed[r, :], w[base + c * C:base + (c + 1) * C, :], NT)
            if c != 1:
                b = 1 + c // 2
                v = v + bias[b:b + 1, :C]
            v = v.astype(BF)
            joined[c, r, :] = v
            if c == 2:
                vt[:, r] = v.T
    masks = [head_mask(h, C) for h in range(C // HD)]
    for i in range(L // QB):
        k0, kn = window(i)
        r = pl.ds(i * QB, QB)
        q = joined[0, r, :] * BF(HD ** -0.5)
        k = joined[1, pl.ds(k0, kn), :]
        m = mask[i, :kn, :]
        H = C // HD
        qs = jnp.concatenate([q * masks[h] for h in range(H)], axis=0)
        s = dot(k, qs, NT) + jnp.concatenate([m] * H, axis=1)
        top = jnp.max(s, axis=0, keepdims=True)
        e = jnp.exp(s - top)
        total = jnp.sum(e, axis=0, keepdims=True)
        p = (e * (1.0 / total)).astype(BF)
        stat = top + jnp.log(total)
        stats = [stat[:, h * QB:(h + 1) * QB] for h in range(H)]
        ps = jnp.concatenate([p[:, h * QB:(h + 1) * QB] for h in range(H)], axis=0)
        rid = lax.broadcasted_iota(jnp.int32, (C, 1), 0) // HD
        vtb = jnp.concatenate([vt[:, pl.ds(k0, kn)] * (rid == h).astype(BF) for h in range(H)], axis=1)
        ctx[r, :] = dot(vtb, ps).T.astype(BF)
        for h in range(C // HD):
            lse[h:h + 1, r] = stats[h]


def attend(h, normed, mask, ws, C, name, deps=()):
    L, D = normed.shape
    return run(
        attend_kernel,
        (h, normed, mask, *ws),
        [SMALL, RES, RES] + [RES for w in ws],
        deps,
        [vmem((3, L, C), BF), vmem((L, C), BF), vmem((8, L), F32)],
        [RES, RES, RES],
        [pltpu.VMEM((C, L), BF), pltpu.VMEM((3 * C + EXTRA, D), BF)],
        mib=12,
        micros=5,
        name=name,
    )


def second_norm(order, stream, out_bias, gain, shift, ctxs, ws):
    L, D = stream.shape
    n = len(ws)
    C = ctxs[0].shape[1]

    def kernel(stream, out_bias, gain, shift, *refs):
        *refs, middle, nm, nm_t, token = refs
        i = pl.program_id(0)
        r = pl.ds(pl.multiple_of(i * QB, QB), QB)

        @pl.when(i == 0)
        def _():
            token[...] = jnp.zeros_like(token)

        acc = stream[r, :].astype(F32) + vector(out_bias)
        for j in range(n):
            acc = acc + dot(refs[j][r, :], refs[n + j][...])
        middle[r, :] = acc
        xhat, _ = normalize(acc)
        v = (xhat * vector(gain) + vector(shift)).astype(BF)
        nm[r, :] = v
        nm_t[:, r] = ordered(v.T, order)

    return run(
        kernel,
        (stream, out_bias, gain, shift, *ctxs, *ws),
        [RES] + [full(gain.shape)] * 3 + [RES] * n + [full(w.shape) for w in ws],
        (),
        [vmem((L, D), F32), vmem((L, D), BF), vmem((D, L), BF), sds((8, 128), F32)],
        [RES] * 3 + [full((8, 128))],
        [],
        grid=(L // QB,),
        name="second_norm",
    )


def mlp_kernel(n, first, h0, nm, g, *refs):
    bias, ws, rest = refs[:n], refs[n:2 * n + 1], refs[2 * n + 1:]
    if not first:
        o_in, m_in = rest[:2]
        rest = rest[2:]
    o_acc, m_acc, hs, ps, g_ub, *bufs = rest
    w_up, w_dn = whole(h0, ws[:n], *bufs), ws[n]
    L = nm.shape[0]
    up_b = front(h0, bias)[0:1, :].astype(F32)
    total = jnp.zeros((1, w_up.shape[1]), F32)
    rows = L // 2
    blocks = [pl.ds(i * rows, rows) for i in range(2)]

    def before(r):
        return dot(nm[r, :], w_up[...]) + up_b, dot(g[r, :], w_dn[...], NT)

    ready = before(blocks[0])
    for i, r in enumerate(blocks):
        x, gd = ready
        if i + 1 < len(blocks):
            ready = before(blocks[i + 1])
        x2 = x * x
        th = jnp.tanh(x * (GA + (GA * GB) * x2))
        ht = 0.5 * th + 0.5
        h = (x * ht).astype(BF)
        dg = ht + x * (0.5 - 0.5 * (th * th)) * (GA + (3 * GA * GB) * x2)
        pg = (gd * dg).astype(BF)
        hs[r, :] = h
        ps[r, :] = pg
        total = total + jnp.sum(pg.astype(F32), axis=0, keepdims=True)
        o, m = dot(h, w_dn[...]), dot(pg, w_up[...], NT)
        o_acc[r, :] = o if first else o_in[r, :] + o
        m_acc[r, :] = m if first else m_in[r, :] + m
    g_ub[...] = total


def mlp(h, nm, g, biases, ws, accs, name, deps=()):
    L, D = nm.shape
    n = len(biases)
    F = ws[0].shape[1]
    return run(
        functools.partial(mlp_kernel, n, not accs),
        (h, nm, g, *biases, *ws, *accs),
        [SMALL, RES, RES] + [pl.BlockSpec((EXTRA, F), lambda _: (0, 0))] * n + [RES for w in ws] + [RES] * len(accs),
        deps,
        [vmem((L, D), F32)] * 2 + [vmem((L, F), BF)] * 2 + [sds((1, F), F32)],
        [RES] * 4 + [full((1, F))],
        [] if n == 1 else [pltpu.VMEM((D, F), BF)],
        aliases={4 + 2 * n: 0, 5 + 2 * n: 1} if accs else None,
        mib=14,
        micros=7,
        name=name,
    )


def mlp_grads(h, nm_t, g_t, hs, ps, adds, bits, name, deps=()):
    D, L = nm_t.shape
    F = hs.shape[1]
    n = D // 2

    def kernel(h0, nm_t, g_t, hs, ps, *refs):
        c = pl.ds(pl.multiple_of(pl.program_id(0) * QB, QB), QB)
        for j, (left, right) in enumerate(((nm_t, ps), (g_t, hs))):
            for k in range(2):
                half = k ^ h0[bits[j]] if adds else k
                rows = pl.ds(pl.multiple_of(half * n, n), n)
                v = dot(left[rows, :], right[:, c])
                if adds:
                    v = v + jnp.where(half == 0, refs[2 * j][...], refs[2 * j + 1][...]).astype(F32)
                refs[len(adds) + 2 * j + k][...] = v.astype(BF)

    col = pl.BlockSpec((n, QB), lambda c: (0, c))
    return run(
        kernel,
        (h, nm_t, g_t, hs, ps, *adds),
        [SMALL] + [RES] * 4 + [col] * len(adds),
        deps,
        [sds((n, F), BF)] * 4,
        [col] * 4,
        mib=12,
        grid=(F // QB,),
        name=name,
    )


def second_back_kernel(order, middle, o_acc, m_acc, g, gain, down_bias, out, ag, ag_t, mg, sums):
    i = pl.program_id(0)
    r = pl.ds(pl.multiple_of(i * QB, QB), QB)
    mid = middle[r, :]
    out[...] = (mid + o_acc[r, :] + vector(down_bias)).astype(BF)
    xhat, rstd = normalize(mid)
    d = m_acc[r, :]
    m = g[r, :].astype(F32) + norm_back(d * vector(gain), xhat, rstd)
    mg[r, :] = m
    a = m.astype(BF)
    ag[r, :] = a
    ag_t[:, r] = ordered(a.T, order)

    @pl.when(i == 0)
    def _():
        sums[...] = jnp.zeros_like(sums)

    sums[0:1, :] += jnp.sum(d * xhat, axis=0, keepdims=True)
    sums[1:2, :] += jnp.sum(d, axis=0, keepdims=True)
    sums[2:3, :] += jnp.sum(a.astype(F32), axis=0, keepdims=True)


def second_back(order, middle, o_acc, m_acc, g, gain, down_bias):
    L, D = middle.shape
    rows = pl.BlockSpec((QB, D), lambda i: (i, 0))
    return run(
        functools.partial(second_back_kernel, order),
        (middle, o_acc, m_acc, g, gain, down_bias),
        [RES] * 4 + [full(gain.shape)] * 2,
        (),
        [sds((L, D), BF), vmem((L, D), BF), vmem((D, L), BF), vmem((L, D), F32), sds((8, D), F32)],
        [rows, RES, RES, RES, full((8, D))],
        grid=(L // QB,),
        name="second_back",
    )


def attend_back_kernel(split, bit, h0, ag, ag_t, normed_t, mask, joined, ctx, lse, w_out, *rest):
    if split:
        adds, rest = rest[:2], rest[2:]
    jg, *g_w, g_b, dctx, kt, dk, dv = rest
    L, D = ag.shape
    C = ctx.shape[1]
    H = C // HD
    for i in range(L // QB):
        r = pl.ds(i * QB, QB)
        dctx[r, :] = dot(ag[r, :], w_out[...], NT).astype(BF)
        kt[:, r] = joined[1, r, :].T
    masks = [head_mask(h, C) for h in range(H)]
    dk[...] = jnp.zeros_like(dk)
    dv[...] = jnp.zeros_like(dv)
    for i in range(L // QB):
        k0, kn = window(i)
        r = pl.ds(i * QB, QB)
        kr = pl.ds(k0, kn)
        q = joined[0, r, :] * BF(HD ** -0.5)
        k = joined[1, kr, :]
        v = joined[2, kr, :]
        do = dctx[r, :]
        m = mask[i, :kn, :]
        qs = jnp.concatenate([q * masks[h] for h in range(H)], axis=0)
        dos = jnp.concatenate([do * masks[h] for h in range(H)], axis=0)
        top = jnp.concatenate([lse[h:h + 1, r] for h in range(H)], axis=1)
        s = dot(k, qs, NT)
        dp = dot(v, dos, NT)
        p = jnp.exp(s + jnp.concatenate([m] * H, axis=1) - top)
        inner = jnp.sum(p * dp, axis=0, keepdims=True)
        ds = (p * (dp - inner)).astype(BF)
        dv[kr, :] += dot(p.astype(BF), dos)
        dk[kr, :] += dot(ds, qs)
        rid = lax.broadcasted_iota(jnp.int32, (C, 1), 0) // HD
        ktb = jnp.concatenate([kt[:, kr] * (rid == h).astype(BF) for h in range(H)], axis=1)
        dst = jnp.concatenate([ds[:, h * QB:(h + 1) * QB] for h in range(H)], axis=0)
        jg[r, :C] = (dot(ktb, dst).T * HD ** -0.5).astype(BF)
    jg[:, C:2 * C] = dk[...].astype(BF)
    jg[:, 2 * C:] = dv[...].astype(BF)
    rows_n = D // 2
    for j in range(2):
        half = j ^ h0[bit] if split else j
        rows = pl.ds(pl.multiple_of(half * rows_n, rows_n), rows_n)
        v, v_out = dot(normed_t[rows, :], jg[...]), dot(ag_t[rows, :], ctx[...])
        if split:
            add = jnp.where(half == 0, adds[0][...], adds[1][...]).astype(F32)
            v, v_out = v + add[:, :3 * C], v_out + add[:, 3 * C:]
        g_w[j][:, :3 * C] = v.astype(BF)
        g_w[j][:, 3 * C:] = v_out.astype(BF)
    g_b[...] = jnp.sum(jg[...].astype(F32), axis=0, keepdims=True)


def attend_back(h, ag, ag_t, normed_t, mask, saved, w_out, adds, bit, name, deps=()):
    joined, ctx, lse = saved
    L, D = ag.shape
    C = ctx.shape[1]
    shape = (D // 2, 4 * C)
    return run(
        functools.partial(attend_back_kernel, bool(adds), bit),
        (h, ag, ag_t, normed_t, mask, joined, ctx, lse, w_out, *adds),
        [SMALL] + [RES] * (8 + len(adds)),
        deps,
        [vmem((L, 3 * C), BF)] + [vmem(shape, BF)] * 2 + [sds((1, 3 * C), F32)],
        [RES] * 3 + [full((1, 3 * C))],
        [pltpu.VMEM((L, C), BF), pltpu.VMEM((C, L), BF), pltpu.VMEM((L, C), F32), pltpu.VMEM((L, C), F32)],
        mib=10,
        micros=9,
        name=name,
    )


def first_back(h, stream, mg, gain, slots, jgs, ws, deps=()):
    L, D = stream.shape
    n = len(jgs)
    flat = [w for shard in ws for w in shard]

    def kernel(h0, stream, mg, gain, slots, *refs):
        gtok, gth, sums, buf = refs[n + len(flat):]
        i = pl.program_id(0)
        r = pl.ds(pl.multiple_of(i * QB, QB), QB)

        @pl.when(i == 0)
        def _():
            sums[...] = jnp.zeros_like(sums)
            gth[...] = jnp.zeros_like(gth)
            at = n
            for j, shard in enumerate(ws):
                if len(shard) > 1:
                    whole(h0, refs[at:at + 2], buf.at[j])
                at += len(shard)

        d, at = None, n
        for j, shard in enumerate(ws):
            w = refs[at] if len(shard) == 1 else buf.at[j]
            at += len(shard)
            v = dot(refs[j][r, :], w[EXTRA:, :])
            d = v if d is None else d + v
        xhat, rstd = normalize(stream[r, :].astype(F32))
        sg = (mg[r, :] + norm_back(d * vector(gain), xhat, rstd)).astype(BF)
        hot = one_hot(slots[...], i * QB, QB)
        covered = jnp.sum(hot.astype(F32), axis=1, keepdims=True) > 0.5
        gtok[...] = jnp.where(covered, 0.0, sg.astype(F32)).astype(BF)
        gth[...] += dot(hot.astype(BF), sg, ((0,), (0,)))
        sums[0:1, :] += jnp.sum(d * xhat, axis=0, keepdims=True)
        sums[1:2, :] += jnp.sum(d, axis=0, keepdims=True)

    return run(
        kernel,
        (h, stream, mg, gain, slots, *jgs, *flat),
        [SMALL, RES, RES, full(gain.shape), full(slots.shape)] + [RES] * (n + len(flat)),
        deps,
        [sds((L, D), BF), sds((slots.shape[1], D), F32), sds((8, D), F32)],
        [pl.BlockSpec((QB, D), lambda i: (i, 0)), full((slots.shape[1], D)), full((8, D))],
        [pltpu.VMEM((n, ws[0][0].shape[0], D), BF)],
        mib=16,
        micros=8,
        grid=(L // QB,),
        name="first_back",
    )


def merge(h, groups, name, deps=()):
    flat = [a for arrays, _ in groups for a in arrays]
    outs = []
    for arrays, bit in groups:
        R, W = arrays[0].shape
        outs += [sds((R, W), BF)] if bit is None else [sds((R // 2, W), BF), sds((R // 2, W), F32)]

    def kernel(h0, *refs):
        at, to = 0, len(flat)
        for arrays, bit in groups:
            group = refs[at:at + len(arrays)]
            at += len(arrays)
            n = arrays[0].shape[0] // 2
            mine = 0 if bit is None else h0[bit]
            for half in ((0, 1) if bit is None else (1 - mine, mine)):
                rows = pl.ds(pl.multiple_of(half * n, 16), n)
                t = group[0][rows, :].astype(F32)
                for ref in group[1:]:
                    t = t + ref[rows, :].astype(F32)
                if bit is None:
                    refs[to][rows, :] = t.astype(BF)
                else:
                    refs[to][...] = t.astype(refs[to].dtype)
                    to += 1
            to += bit is None

    return run(
        kernel,
        (h, *flat),
        [SMALL] + [full(a.shape) for a in flat],
        deps,
        outs,
        [full(o.shape) for o in outs],
        mib=12,
        name=name,
    )


def swap(x, axis, size, bit):
    return lax.ppermute(x, axis, [(i, i ^ bit) for i in range(size)])


def after(x, dep):
    return lax.optimization_barrier((x, dep))


def local(
    n_dp,
    tokens,
    thoughts,
    thought_slots,
    segment_ids,
    attn_gain,
    attn_shift,
    qkv_weight,
    qkv_bias,
    out_weight,
    out_bias,
    mlp_gain,
    mlp_shift,
    up_weight,
    up_bias,
    down_weight,
    down_bias,
    cotangent,
):
    D = tokens.shape[2]
    C = qkv_weight.shape[2]
    F = up_weight.shape[1]
    core = lambda x: swap(x, "tensor", 4, 1)
    cross = lambda x: swap(x, "tensor", 4, 2)
    tie = lax.optimization_barrier
    dp = lax.axis_index("dp")
    me = lax.axis_index("tensor")
    h = jnp.stack([dp & 1, dp >> 1 & 1, me, dp]).astype(jnp.int32)
    beside = lambda x: swap(x, "dp", n_dp, 1)
    my_half = lambda w: lax.dynamic_slice_in_dim(w, (dp & 1) * (w.shape[0] // 2), w.shape[0] // 2, 0)

    bits = [1 << i for i in range(n_dp.bit_length() - 1)]
    attn_bits, up_bits, down_bits = bits, bits, bits[1:2] + bits[:1] + bits[2:]
    attn_order, up_order, down_order = map(piece_order, (attn_bits, up_bits, down_bits))

    biases = jnp.concatenate(
        [up_bias.reshape(1, F), jnp.pad(qkv_bias, ((0, 0), (0, F - C))), jnp.zeros((EXTRA - 3, F), BF)], 0
    )
    qkv = jnp.concatenate([biases, jnp.transpose(qkv_weight, (1, 2, 0)).reshape(3 * C, D)], 0)
    qkv_x, qkv_c = cross(my_half(qkv)), core(qkv)
    up_s = my_half(up_weight)
    g = cotangent[0]
    stream, normed, normed_t, g_v, cot_t, cot_sum, mask = first_norm(
        (attn_order, down_order), tokens[0], g, thought_slots, thoughts[0], attn_gain, attn_shift, segment_ids, (up_s, h)
    )
    saved = [None] * 4
    qkv_w = [(qkv,), (qkv_c,)]

    def forward(s, deps=()):
        saved[s] = attend(h, normed, mask, qkv_w[s], C, "attend%d" % s, deps)

    def wait(s, *arrays):
        *arrays, stats = tie((*arrays, saved[s][2]))
        saved[s] = (*saved[s][:2], stats)
        return arrays

    forward(1, (up_s,))
    qkv_x, up_s, out_s = wait(1, qkv_x, up_s, out_weight)
    qkv_y, qkv_cx, out_x, up_x = beside(qkv_x), core(qkv_x), cross(out_s), cross(up_s)
    forward(0)
    qkv_y, out_s = wait(0, qkv_y, out_weight)
    qkv_cy, out_c = core(qkv_y), core(out_s)
    qkv_w += [(qkv_x, qkv_y), (qkv_cx, qkv_cy)]
    forward(2, (qkv_cx,))
    out_x, down_s = wait(2, out_x, down_weight)
    out_cx, down_x = core(out_x), cross(down_s)
    forward(3, (out_c,))
    up_x, up_s, down_s = wait(3, up_x, up_weight, down_weight)
    up_y, up_cx, up_c, down_c = beside(up_x), core(up_x), core(up_s), core(down_s)
    middle, nm, nm_t, token = second_norm(
        up_order, stream, out_bias, mlp_gain, mlp_shift, [c for _, c, _ in saved], [out_weight, out_c, out_x, out_cx]
    )
    gb, acts, grads = [None] * 4, [None] * 4, [None] * 4
    first_bits = (up_bits[0].bit_length() - 1, down_bits[0].bit_length() - 1)

    def hidden(s, ws, accs, deps=()):
        o, m, hs, ps, gb[s] = mlp(h, nm, g_v, qkv_w[s][:1] if s < 2 else qkv_w[s], ws, accs, "mlp%d" % s, deps)
        acts[s] = (hs, ps)
        return o, m

    def hidden_grads(s, adds=(), deps=()):
        grads[s] = mlp_grads(h, nm_t, cot_t, *acts[s], adds, first_bits, "mlp_grads%d" % s, deps)

    accs = hidden(1, (up_c, down_c), ())
    hidden_grads(1, (), (up_cx,))
    near = list(map(core, grads[1]))
    accs = hidden(0, (up_weight, down_weight), accs, tuple(grads[1]))
    up_y, gb[0] = tie((up_y, gb[0]))
    up_cy = core(up_y)
    accs = hidden(2, (up_x, up_y, down_x), accs)
    hidden_grads(0, near, (gb[2],))
    up_k, up_o, down_k, down_o = grads[0]
    own = [[up_k, swap(up_o, "dp", n_dp, up_bits[0])], [down_k, swap(down_o, "dp", n_dp, down_bits[0])]]
    down_x, gb[0] = tie((down_x, gb[0]))
    accs = hidden(3, (up_cx, up_cy, core(down_x)), accs, (up_o,))
    hidden_grads(3)
    near = list(map(core, grads[3]))
    out, ag, ag_t, mg, sums2 = second_back(attn_order, middle, *accs, g_v, mlp_gain, down_bias)

    def along(sent, bit):
        return swap(sent, "dp", n_dp, bit)

    def at(bit):
        return bit.bit_length() - 1

    g_attn, g_qb = [None] * 4, [None] * 4

    def back(s, adds=(), deps=()):
        w_out = (out_weight, out_c, out_x, out_cx)[s]
        jgs[s], *g_attn[s], g_qb[s] = attend_back(
            h, ag, ag_t, normed_t, mask, saved[s], w_out, adds, at(attn_bits[0]), "attend_back%d" % s, deps
        )

    jgs = [None] * 4
    ways = (up_bits, down_bits)
    back(3)
    hidden_grads(2, near, (g_qb[3],))
    near = list(map(core, g_attn[3]))
    up_k, up_o, down_k, down_o = grads[2]
    far = [[up_k, along(up_o, up_bits[0])], [down_k, along(down_o, down_bits[0])]]
    own[0][1], own[1][1], g_qb[3] = tie((own[0][1], own[1][1], g_qb[3]))
    up_m, up_k, down_m, down_k = merge(h, [(a, at(w[1])) for a, w in zip(own, ways)], "merge_own", (up_o,))
    own = [[up_k, along(up_m, up_bits[1])], [down_k, along(down_m, down_bits[1])]]
    back(1, (), (up_m,))
    back(2, near, (g_qb[1],))
    near = list(map(core, g_attn[1]))
    attn_far = [g_attn[2][0], along(g_attn[2][1], attn_bits[0])]
    far[0][1], far[1][1], g_qb[2] = tie((far[0][1], far[1][1], g_qb[2]))
    up_m, up_k, down_m, down_k = merge(h, [(a, at(w[1])) for a, w in zip(far, ways)], "merge_far")
    far = [[up_k, along(up_m, up_bits[1])], [down_k, along(down_m, down_bits[1])]]
    back(0, near, (up_m, own[0][1], own[1][1]))
    attn_own = [g_attn[0][0], along(g_attn[0][1], attn_bits[0])]
    gtok, gth, sums1 = first_back(h, stream, mg, attn_gain, thought_slots, jgs, qkv_w)
    far[0][-1], far[1][-1], attn_far[1], sums1 = tie((far[0][-1], far[1][-1], attn_far[1], sums1))
    far_m, far_k, *far_s = merge(h, [(attn_far, at(attn_bits[1]))] + [(a, None) for a in far], "merge_last")

    late, gb, g_qb, sums1, sums2, cot_sum, far_m, far_s = tie((h, gb, g_qb, sums1, sums2, cot_sum, far_m, far_s))
    attn_far = [far_k, along(far_m, attn_bits[1])]
    own = [a + [cross(x)] for a, x in zip(own, far_s)]
    me, dp = late[2], late[3]
    rel = [jnp.concatenate([b, jnp.pad(q, ((0, 0), (0, F - 3 * C)))], 0) for b, q in zip(gb, g_qb)]
    first = [jnp.where(me & 1 == 0, rel[t], rel[t ^ 1]) for t in range(4)]
    ordered = jnp.concatenate([jnp.where(me & 2 == 0, first[t], first[t ^ 2]) for t in range(4)], 0)
    small = jnp.concatenate([ordered, sums1[:2], sums2[:3], cot_sum], 0)
    attn_own[1], small = tie((attn_own[1], small))

    wide = lambda a: a.astype(F32)

    def total(arrays):
        t = wide(arrays[0])
        for a in arrays[1:]:
            t = t + wide(a)
        return t

    def part(arrays, bit, mine):
        n = arrays[0].shape[0] // 2
        return [jnp.where((dp & bit != 0) == mine, a[n:], a[:n]) for a in arrays]

    def halve(arrays, bit):
        sent = total(part(arrays, bit, False)).astype(BF)
        return part(arrays, bit, True) + [along(sent, bit)]

    attn_own = halve(attn_own, attn_bits[1])
    attn_own.append(cross(total(attn_far).astype(BF)))
    for i in range(2, len(bits)):
        *own, attn_own = [halve(a, w[i]) for a, w in zip((*own, attn_own), (*ways, attn_bits))]
    r_up, r_dn, r_at = total(own[0]), total(own[1]), total(attn_own)

    for axis, size in (("tensor", 4), ("dp", n_dp)):
        bit = 1
        while bit < size:
            small = small + swap(small, axis, size, bit)
            bit *= 2
    mine = sum(jnp.where(me == t, small[2 * t:2 * t + 2], 0.0) for t in range(4))
    return (
        out[None],
        gtok[None],
        gth.astype(BF)[None],
        small[8],
        small[9],
        r_at[:, :3 * C].reshape(-1, 3, C),
        jnp.stack([mine[1, :C], mine[1, 2 * C:3 * C]]),
        r_at[:, 3 * C:].T,
        small[12],
        small[10],
        small[11],
        r_up,
        mine[0],
        r_dn.T,
        small[13],
    )


def solution(mesh):
    rows = P(("dp", "tensor"), None, None)
    placed = (
        rows,
        rows,
        P(("dp", "tensor"), None),
        P(("dp", "tensor"), None),
        P(),
        P(),
        P(None, None, "tensor"),
        P(None, "tensor"),
        P("tensor", None),
        P(),
        P(),
        P(),
        P(None, "tensor"),
        P("tensor"),
        P("tensor", None),
        P(),
        rows,
    )
    return jax.shard_map(
        functools.partial(local, mesh.shape["dp"]),
        mesh=mesh,
        in_specs=placed,
        out_specs=(
            rows,
            rows,
            rows,
            P(),
            P(),
            P("dp", None, "tensor"),
            P(None, "tensor"),
            P("tensor", "dp"),
            P(),
            P(),
            P(),
            P("dp", "tensor"),
            P("tensor"),
            P("tensor", "dp"),
            P(),
        ),
        check_vma=False,
    )
```
